32 devices in a mesh: mem: 4 (over z), dp: 8 (over y, x, core).
Axes of the slice: x: 2, y: 2, z: 4, core: 2. Of those that a mesh axis runs over, the one named last changes fastest.
Arguments:
- block_input: bfloat16 [8, 4, 256, 1024], P('dp', 'mem'), may hold values from -6 to 6
- memory: bfloat16 [8, 4, 512, 1024], P('dp', None, 'mem'), may hold values from -6 to 6
- out_grad: bfloat16 [8, 4, 256, 1024], P('dp', 'mem'), may hold values from -6 to 6
- decoder_segments: int32 [8, 4, 256], P('dp', 'mem'), may hold values from 0 to 7, as said below
- encoder_segments: int32 [8, 4, 512], P('dp', 'mem'), may hold values from 0 to 7, as said below
- distance_buckets: int32 [256], replicated, may hold values from 0 to 31, as said below
- self_gain: float32 [1024], replicated, may hold values from 0.1 to 1.9
- cross_gain: float32 [1024], replicated, may hold values from 0.1 to 1.9
- ffn_gain: float32 [1024], replicated, may hold values from 0.1 to 1.9
- position_bias: float32 [32, 16], replicated, may hold values from -4 to 4
- self_query: bfloat16 [1024, 1024], P(('mem', 'dp')), may hold values from -0.1875 to 0.1875
- self_key: bfloat16 [1024, 512], P(('mem', 'dp')), may hold values from -0.1875 to 0.1875
- self_value: bfloat16 [1024, 512], P(('mem', 'dp')), may hold values from -0.1875 to 0.1875
- self_out: bfloat16 [1024, 1024], P(('mem', 'dp')), may hold values from -0.75 to 0.75
- cross_query: bfloat16 [1024, 1024], P(('mem', 'dp')), may hold values from -0.1875 to 0.1875
- cross_key: bfloat16 [1024, 512], P(('mem', 'dp')), may hold values from -0.1875 to 0.1875
- cross_value: bfloat16 [1024, 512], P(('mem', 'dp')), may hold values from -0.1875 to 0.1875
- cross_out: bfloat16 [1024, 1024], P(('mem', 'dp')), may hold values from -1 to 1
- ffn_gate: bfloat16 [1024, 2816], P(('mem', 'dp')), may hold values from -0.1875 to 0.1875
- ffn_up: bfloat16 [1024, 2816], P(('mem', 'dp')), may hold values from -0.1875 to 0.1875
- ffn_down: bfloat16 [1024, 2816], P(('mem', 'dp')), may hold values from -0.15625 to 0.15625
Outputs:
- result: bfloat16 [8, 4, 256, 1024], P('dp', 'mem')
- input_grad: float32 [8, 4, 256, 1024], P('dp', 'mem')
- memory_grad: float32 [8, 4, 512, 1024], P('dp', None, 'mem')
- self_gain_grad: float32 [1024], replicated
- cross_gain_grad: float32 [1024], replicated
- ffn_gain_grad: float32 [1024], replicated
- position_bias_grad: float32 [32, 16], replicated
- self_query_grad: float32 [1024, 1024], P(('mem', 'dp'))
- self_key_grad: float32 [1024, 512], P(('mem', 'dp'))
- self_value_grad: float32 [1024, 512], P(('mem', 'dp'))
- self_out_grad: float32 [1024, 1024], P(('mem', 'dp'))
- cross_query_grad: float32 [1024, 1024], P(('mem', 'dp'))
- cross_key_grad: float32 [1024, 512], P(('mem', 'dp'))
- cross_value_grad: float32 [1024, 512], P(('mem', 'dp'))
- cross_out_grad: float32 [1024, 1024], P(('mem', 'dp'))
- ffn_gate_grad: float32 [1024, 2816], P(('mem', 'dp'))
- ffn_up_grad: float32 [1024, 2816], P(('mem', 'dp'))
- ffn_down_grad: float32 [1024, 2816], P(('mem', 'dp'))
The draws below stay inside these ranges and needn't reach their ends.
Inputs may be any that keep to these rules, and one draw needn't show every extreme that they name: `decoder_segments`: within each row the ids never fall, and every document 0 to 7 has one or more tokens. `encoder_segments`: every aligned run of 8 positions of a row holds each document once. `distance_buckets`: never falls as the distance grows; distance 0 has bucket 0 and every bucket occurs.
All inputs are finite; a program needn't handle non-finite values.
Results may differ from the reference program's by a relative error of at most 0.018.
Values may be sent and summed in bfloat16 or wider, within the bound.
No kernel may reach another device: no remote copies, remote signals or barrier semaphores. Data moves between devices by JAX's collectives and lax.ppermute only.
A program may use at most 256 MiB of HBM per device.

```python
import math
import jax
import jax.numpy as jnp
from jax import lax

D = 1024
HQ = 16
KVH = 8
DH = 64
FF = 2816
BUCKETS = 32
LEN = 256
MEMLEN = 512
DOCS = 8
GROUPS = 8
ROWS_IN = 4


def draw_decoder_segments(key, part):
    key = jax.random.fold_in(key, 11)
    row_keys = jax.random.split(key, GROUPS * ROWS_IN)

    def one_row(row_key):
        cuts = jax.random.permutation(row_key, LEN - 1)[:DOCS - 1].astype(jnp.int32) + 1
        places = lax.iota(jnp.int32, LEN)
        return jnp.sum((places[:, None] >= cuts[None, :]).astype(jnp.int32), axis=1)
    return jax.vmap(one_row)(row_keys).reshape(GROUPS, ROWS_IN, LEN).astype(jnp.int32)


def draw_encoder_segments(key, part):
    key = jax.random.fold_in(key, 23)
    block_keys = jax.random.split(key, GROUPS * ROWS_IN * (MEMLEN // DOCS))

    def one_block(block_key):
        return jax.random.permutation(block_key, DOCS).astype(jnp.int32)
    orders = jax.vmap(one_block)(block_keys)
    return orders.reshape(GROUPS, ROWS_IN, MEMLEN).astype(jnp.int32)


def draw_distance_buckets(key, part):
    key = jax.random.fold_in(key, 37)
    cuts = jax.random.permutation(key, LEN - 1)[:BUCKETS - 1].astype(jnp.int32) + 1
    places = lax.iota(jnp.int32, LEN)
    return jnp.sum((places[:, None] >= cuts[None, :]).astype(jnp.int32), axis=1).astype(jnp.int32)


def level_of(key, shape, shards, smallest, high):
    level, own = 1.0, jax.random.fold_in(key, 6)
    for position, blocks in shards:
        heights = jnp.exp(jax.random.uniform(jax.random.fold_in(own, position), (blocks,), jnp.float32, smallest / len(shards), high / len(shards)))
        level = level * jnp.repeat(heights, shape[position] // blocks).reshape([-1 if axis == position else 1 for axis in range(len(shape))])
    return level


def noise(rng, dims, spread, bound, shards=(), kind=jnp.bfloat16):
    loudness = level_of(rng, dims, shards, -0.22, 0.18) if shards else 1.0
    entries = jax.random.normal(rng, dims, jnp.float32) * spread * loudness
    return jnp.minimum(jnp.maximum(entries, -bound), bound).astype(kind)


def setup_inputs(seed: int = 0) -> dict:
    arg_keys = jax.random.split(jax.random.key(seed), 22)
    return {
        "block_input": noise(arg_keys[0], (GROUPS, ROWS_IN, LEN, D), 1.0, 6.0, ((0, 8), (1, 4))),
        "memory": noise(arg_keys[1], (GROUPS, ROWS_IN, MEMLEN, D), 1.0, 6.0, ((0, 8), (2, 4))),
        "out_grad": noise(arg_keys[2], (GROUPS, ROWS_IN, LEN, D), 1.0, 6.0, ((0, 8), (1, 4))),
        "decoder_segments": draw_decoder_segments(jax.random.fold_in(arg_keys[21], 71), 0),
        "encoder_segments": draw_encoder_segments(jax.random.fold_in(arg_keys[21], 71), 0),
        "distance_buckets": draw_distance_buckets(jax.random.fold_in(arg_keys[21], 71), 0),
        "self_gain": jnp.clip(1.0 + 0.18 * jax.random.normal(arg_keys[6], (D,), jnp.float32), 0.1, 1.9),
        "cross_gain": jnp.clip(1.0 + 0.18 * jax.random.normal(arg_keys[7], (D,), jnp.float32), 0.1, 1.9),
        "ffn_gain": jnp.clip(1.0 + 0.18 * jax.random.normal(arg_keys[8], (D,), jnp.float32), 0.1, 1.9),
        "position_bias": noise(arg_keys[9], (BUCKETS, HQ), 1.0, 4.0, (), jnp.float32),
        "self_query": noise(arg_keys[10], (D, HQ * DH), D ** -0.5, 0.1875, ((0, 32),)),
        "self_key": noise(arg_keys[11], (D, KVH * DH), D ** -0.5, 0.1875, ((0, 32),)),
        "self_value": noise(arg_keys[12], (D, KVH * DH), D ** -0.5, 0.1875, ((0, 32),)),
        "self_out": noise(arg_keys[13], (D, HQ * DH), (HQ * DH // 16) ** -0.5, 0.75, ((0, 32),)),
        "cross_query": noise(arg_keys[14], (D, HQ * DH), D ** -0.5, 0.1875, ((0, 32),)),
        "cross_key": noise(arg_keys[15], (D, KVH * DH), D ** -0.5, 0.1875, ((0, 32),)),
        "cross_value": noise(arg_keys[16], (D, KVH * DH), D ** -0.5, 0.1875, ((0, 32),)),
        "cross_out": noise(arg_keys[17], (D, HQ * DH), (HQ * DH // 32) ** -0.5, 1.0, ((0, 32),)),
        "ffn_gate": noise(arg_keys[18], (D, FF), D ** -0.5, 0.1875, ((0, 32),)),
        "ffn_up": noise(arg_keys[19], (D, FF), D ** -0.5, 0.1875, ((0, 32),)),
        "ffn_down": noise(arg_keys[20], (D, FF), (FF // 2) ** -0.5, 0.15625, ((0, 32),)),
    }


@jax.custom_vjp
def low(v):
    return lax.optimization_barrier(v.astype(jnp.bfloat16)).astype(jnp.float32)

@jax.custom_vjp
def low_back(v):
    return v

def low_keep(v):
    return (low(v), None)

def low_pass(kept, grad):
    return (grad,)

def back_keep(v):
    return (v, None)

def back_low(kept, grad):
    return (low(grad),)
low.defvjp(low_keep, low_pass)
low_back.defvjp(back_keep, back_low)
HIGHEST = lax.Precision.HIGHEST
EPSILON = 1e-06
NEGATIVE = -1e+30

def rounded_both(value):
    return low(low_back(value))

def matrix(left, right):
    return jnp.dot(left, right, precision=HIGHEST)

def norm_rows(stream, gain):
    return stream * lax.rsqrt(lax.optimization_barrier(jnp.mean(stream * stream, axis=-1, keepdims=True)) + EPSILON) * gain

def block_rows(length):
    return 512 if length % 512 == 0 else length

def attention(queries, keys, values, allowed, extra):
    scores = jnp.einsum('qkgd,skd->kgqs', queries, keys, precision=HIGHEST) * (1.0 / math.sqrt(DH)) + extra
    scores = jnp.where(allowed, low_back(scores), NEGATIVE)
    top = lax.optimization_barrier(jnp.max(scores, axis=-1, keepdims=True))
    expo = jnp.exp(scores - top)
    probs = low(expo / lax.optimization_barrier(jnp.sum(expo, axis=-1, keepdims=True)))
    return jnp.einsum('kgqs,skd->qkgd', probs, values, precision=HIGHEST)

def reference(block_input, memory, out_grad, decoder_segments, encoder_segments, distance_buckets, self_gain, cross_gain, ffn_gain, position_bias, self_query, self_key, self_value, self_out, cross_query, cross_key, cross_value, cross_out, ffn_gate, ffn_up, ffn_down):
    groups = HQ // KVH
    size = block_rows(LEN)
    count = LEN // size
    decoder_rows = decoder_segments.reshape(-1, LEN)
    encoder_rows = encoder_segments.reshape(-1, MEMLEN)
    starts = lax.iota(jnp.int32, count) * size

    def forward(block_in, memory_in, gain_self, gain_cross, gain_ffn, bias_table, w_query, w_key, w_value, w_out, c_query, c_key, c_value, c_out, f_gate, f_up, f_down):
        distance_bias = jnp.take(bias_table, distance_buckets, axis=0).T

        def one_row(pieces):
            row_input, row_memory, query_seg, key_seg = pieces
            normed = low(norm_rows(row_input, gain_self))
            queries = rounded_both(matrix(normed, w_query)).reshape(count, size, KVH, groups, DH)
            keys = rounded_both(matrix(normed, w_key)).reshape(LEN, KVH, DH)
            values = rounded_both(matrix(normed, w_value)).reshape(LEN, KVH, DH)

            def self_block(parts):
                block, start = parts
                places = start + lax.iota(jnp.int32, size)
                offset = places[:, None] - lax.iota(jnp.int32, LEN)[None, :]
                seg_block = lax.dynamic_slice_in_dim(query_seg, start, size)
                allowed = (offset >= 0) & (seg_block[:, None] == query_seg[None, :])
                extra = jnp.take(distance_bias, jnp.clip(offset, 0, LEN - 1), axis=1).reshape(KVH, groups, size, LEN)
                return attention(block, keys, values, allowed, extra)
            mixed = lax.map(jax.checkpoint(self_block), (queries, starts)).reshape(LEN, HQ * DH)
            middle = row_input + low_back(matrix(rounded_both(mixed), w_out.T))
            normed = low(norm_rows(middle, gain_cross))
            queries = rounded_both(matrix(normed, c_query)).reshape(count, size, KVH, groups, DH)
            keys = rounded_both(matrix(row_memory, c_key)).reshape(MEMLEN, KVH, DH)
            values = rounded_both(matrix(row_memory, c_value)).reshape(MEMLEN, KVH, DH)

            def cross_block(parts):
                block, start = parts
                seg_block = lax.dynamic_slice_in_dim(query_seg, start, size)
                allowed = seg_block[:, None] == key_seg[None, :]
                return attention(block, keys, values, allowed, jnp.float32(0.0))
            mixed = lax.map(jax.checkpoint(cross_block), (queries, starts)).reshape(LEN, HQ * DH)
            second = middle + low_back(matrix(rounded_both(mixed), c_out.T))
            normed = low(norm_rows(second, gain_ffn))
            gate = low_back(matrix(normed, f_gate))
            lifted = low_back(matrix(normed, f_up))
            hidden = low(jax.nn.gelu(gate, approximate=True) * lifted)
            return second + low_back(matrix(hidden, f_down.T))
        outputs = lax.map(jax.checkpoint(one_row), (block_in.reshape(-1, LEN, D), memory_in.reshape(-1, MEMLEN, D), decoder_rows, encoder_rows))
        return outputs.reshape(block_in.shape)
    floats = (block_input.astype(jnp.float32), memory.astype(jnp.float32), self_gain, cross_gain, ffn_gain, position_bias, self_query.astype(jnp.float32), self_key.astype(jnp.float32), self_value.astype(jnp.float32), self_out.astype(jnp.float32), cross_query.astype(jnp.float32), cross_key.astype(jnp.float32), cross_value.astype(jnp.float32), cross_out.astype(jnp.float32), ffn_gate.astype(jnp.float32), ffn_up.astype(jnp.float32), ffn_down.astype(jnp.float32))
    result, backward = jax.vjp(forward, *floats)
    grads = backward(out_grad.astype(jnp.float32))
    return (result.astype(jnp.bfloat16), grads[0], grads[1], grads[2], grads[3], grads[4], grads[5], grads[6], grads[7], grads[8], grads[9], grads[10], grads[11], grads[12], grads[13], grads[14], grads[15], grads[16])
```

```python
import functools

import jax
import jax.numpy as jnp
import numpy as np
from jax import lax
from jax.experimental import pallas as pl
from jax.experimental.pallas import tpu as pltpu
from jax.sharding import PartitionSpec as P

DH = 64
TILE = 256
EPSILON = 1e-06
NEGATIVE = -1e30
AXES = ("mem", "dp")
F32 = jnp.float32
BF16 = jnp.bfloat16
HIGHEST = lax.Precision.HIGHEST
VMEM = 58 * 1024 * 1024


def steps(n):
    high = list(range(n.bit_length() - 2, 2, -1))
    return (high + [2, 1], high + [1, 2])


def exchange(n, k):
    order = steps(n)
    return [(d, d ^ (1 << order[d & 1][k])) for d in range(n)]


def sibling(n):
    return [(d, d ^ 1) for d in range(n)]


def source(n, me):
    order = steps(n)
    half = n // 2
    table = np.zeros((2, half), np.int32)
    for core in range(2):
        for slot in range(half):
            for k in range(len(order[core])):
                if slot >> k & 1:
                    table[core, slot] ^= 1 << order[core][k]
    odd = (me & 1) == 1
    own = jnp.where(odd, table[1], table[0])
    other = jnp.where(odd, table[0], table[1])
    return jnp.concatenate([me ^ own, me ^ 1 ^ other])


def gather(shard, n):
    held = shard
    last = n.bit_length() - 3
    for k in range(last):
        held = jnp.concatenate([held, lax.ppermute(held, AXES, exchange(n, k))], axis=0)
    pieces = [held, lax.ppermute(held, AXES, exchange(n, last))]
    return pieces + [lax.ppermute(piece, AXES, sibling(n)) for piece in pieces]


def scatter(pieces, n):
    last = n.bit_length() - 3
    there = [lax.ppermute(piece, AXES, sibling(n)) for piece in pieces[2:]]
    send = (pieces[1].astype(F32) + there[1].astype(F32)).astype(BF16)
    held = pieces[0].astype(F32) + there[0].astype(F32)
    held = held + lax.ppermute(send, AXES, exchange(n, last)).astype(F32)
    for k in range(last - 1, -1, -1):
        half = held.shape[0] // 2
        came = lax.ppermute(held[half:].astype(BF16), AXES, exchange(n, k))
        held = held[:half] + came.astype(F32)
    return held


def sum_all(value, n):
    for bit in range(n.bit_length() - 1):
        value = value + lax.ppermute(value, AXES, [(d, d ^ (1 << bit)) for d in range(n)])
    return value


def swap_rows(blocks, nm, nd):
    n = nm * nd
    return [blocks[0]] + [
        lax.ppermute(blocks[t], AXES, [(d, d ^ (t * nd)) for d in range(n)]) for t in range(1, nm)
    ]


def dot(left, right, a=1, b=0):
    return lax.dot_general(left, right, (((a,), (b,)), ((), ())), preferred_element_type=F32)


def rows_of(left, p):
    size = left.shape[1] // 4
    return left[:, p * size : (p + 1) * size]


def project(left, weights):
    total = dot(rows_of(left, 0), weights[0])
    for p in range(1, 4):
        total = total + dot(rows_of(left, p), weights[p])
    return total


def project_back(left, weights):
    return jnp.concatenate([dot(left, w, 1, 1) for w in weights], axis=1)


def scale_of(stream):
    return lax.rsqrt(jnp.mean(stream * stream, axis=1, keepdims=True) + EPSILON)


def norm_back(stream, gain, grad):
    scale = scale_of(stream)
    weighted = grad * gain
    inner = jnp.mean(weighted * stream, axis=1, keepdims=True)
    out = scale * weighted - stream * (scale * scale * scale) * inner
    return out, jnp.sum(grad * stream * scale, axis=0, keepdims=True)


def transposed(value):
    return value.astype(F32).T.astype(BF16)


def spread(part):
    zero = jnp.zeros_like(part)
    top = jnp.concatenate([part, zero], axis=1)
    low = jnp.concatenate([zero, part], axis=1)
    return jnp.concatenate([top, low], axis=0)


def softmax(scores):
    expo = jnp.exp(scores - jnp.max(scores, axis=1, keepdims=True))
    return (expo / jnp.sum(expo, axis=1, keepdims=True)).astype(BF16)


def toeplitz(start):
    block = start
    size = block.shape[0]
    while size < start.shape[1]:
        block = jnp.concatenate([block, pltpu.roll(block, size, 1)], axis=0)
        size *= 2
    return block


def diagonals(block):
    size = block.shape[0]
    while size > 8:
        size //= 2
        block = block[:size] + pltpu.roll(block[size:], block.shape[1] - size, 1)
    return block


def self_forward(x, normed, start, seg_col, seg_row, gain, w0, w1, w2, w3,
                 q_out, kt_out, vt_out, p_out, mixed_out, middle_out, n_out):
    weights = (w0, w1, w2, w3)
    width = x.shape[1]
    keys = w0.shape[1] - 2 * width
    kv = keys // 2
    length = x.shape[0]
    n = normed[...]
    q_out[...] = (project(n, [w[:, :width] for w in weights]).astype(BF16).astype(F32) * 0.125).astype(BF16)
    pair = project(n, [w[:, width : width + keys] for w in weights])
    pair_t = pair.T.astype(BF16)
    kt_out[...] = pair_t[:kv]
    vt_out[...] = pair_t[kv:]
    row = lax.broadcasted_iota(jnp.int32, (length, length), 0)
    column = lax.broadcasted_iota(jnp.int32, (length, length), 1)
    allowed = (column <= row) & (seg_col[...] == seg_row[...])
    for g in range(kv // DH):
        kk = spread(kt_out[g * DH : (g + 1) * DH])
        vv = spread(vt_out[g * DH : (g + 1) * DH])
        scores = dot(q_out[:, g * 2 * DH : (g + 1) * 2 * DH], kk)
        for h in range(2):
            part = scores[:, h * length : (h + 1) * length] + toeplitz(start[2 * g + h])
            p_out[g, :, h * length : (h + 1) * length] = softmax(jnp.where(allowed, part, NEGATIVE))
        mixed_out[:, g * 2 * DH : (g + 1) * 2 * DH] = dot(p_out[g], vv, 1, 1).astype(BF16)
    middle = x[...].astype(F32) + project_back(mixed_out[...], [w[:, width + keys :] for w in weights])
    middle_out[...] = middle
    n_out[...] = (middle * scale_of(middle) * gain[...]).astype(BF16)


def memory_forward(memory, w0, w1, w2, w3, pair_out):
    pair = project(memory[...], [w[...] for w in (w0, w1, w2, w3)])
    pair_out[...] = pair.T.astype(BF16)


def cross_forward(middle, normed, pair, seg_col, seg_row, gain, w0, w1, w2, w3,
                  q_out, p_out, mixed_out, second_out, n_out, nt_out):
    weights = (w0, w1, w2, w3)
    width = middle.shape[1]
    kv = pair.shape[0] // 2
    span = pair.shape[1]
    q = project(normed[...], [w[:, :width] for w in weights])
    q_out[...] = (q.astype(BF16).astype(F32) * 0.125).astype(BF16)
    allowed = seg_col[...] == seg_row[...]
    for g in range(kv // DH):
        kk = spread(pair[g * DH : (g + 1) * DH])
        vv = spread(pair[kv + g * DH : kv + (g + 1) * DH])
        scores = dot(q_out[:, g * 2 * DH : (g + 1) * 2 * DH], kk)
        for h in range(2):
            part = scores[:, h * span : (h + 1) * span]
            p_out[g, :, h * span : (h + 1) * span] = softmax(jnp.where(allowed, part, NEGATIVE))
        mixed_out[:, g * 2 * DH : (g + 1) * 2 * DH] = dot(p_out[g], vv, 1, 1).astype(BF16)
    second = middle[...] + project_back(mixed_out[...], [w[:, width:] for w in weights])
    second_out[...] = second
    n = second * scale_of(second) * gain[...]
    n_out[...] = n.astype(BF16)
    nt_out[...] = n.T.astype(BF16)


def ffn_tile(n, nt, dy, dyt, res_in, dn_in, w0, w1, w2, w3, res_out, dn_out, g0, g1, g2, g3):
    weights = (w0, w1, w2, w3)

    @pl.when(pl.program_id(0) == 0)
    def _():
        res_out[...] = res_in[...]
        dn_out[...] = dn_in[...]

    pair = project(n[...], [w[:, : 2 * TILE] for w in weights])
    gate = pair[:, :TILE]
    lifted = pair[:, TILE:]
    hidden_grad = project(dy[...], [w[:, 2 * TILE :] for w in weights])
    root = 0.7978845608028654
    square = gate * gate
    tanh = jnp.tanh(root * gate * (1.0 + 0.044715 * square))
    half = 0.5 * (1.0 + tanh)
    gelu = gate * half
    slope = half + 0.5 * gate * (1.0 - tanh * tanh) * (root * (1.0 + 3.0 * 0.044715 * square))
    hidden = (gelu * lifted).astype(BF16)
    pair_grad = jnp.concatenate(
        [(hidden_grad * lifted * slope).astype(BF16), (hidden_grad * gelu).astype(BF16)], axis=1
    )
    res_out[...] += project_back(hidden, [w[:, 2 * TILE :] for w in weights])
    dn_out[...] += project_back(pair_grad, [w[:, : 2 * TILE] for w in weights])
    size = n.shape[1] // 4
    for p, g in enumerate((g0, g1, g2, g3)):
        g[:, : 2 * TILE] = dot(nt[p * size : (p + 1) * size], pair_grad).astype(BF16)
        g[:, 2 * TILE :] = dot(dyt[p * size : (p + 1) * size], hidden).astype(BF16)


def ffn_end(second, res, dn, dy, gain, w0, w1, w2, w3, result_out, grad_out, gain_out, branch_out, mixed_out):
    result_out[...] = (second[...] + res[...]).astype(BF16)
    back, gain_grad = norm_back(second[...], gain[...], dn[...])
    grad = dy[...].astype(F32) + back
    grad_out[...] = grad
    gain_out[...] = gain_grad
    branch = grad.astype(BF16)
    branch_out[...] = branch
    mixed_out[...] = project(branch, [w[...] for w in (w0, w1, w2, w3)]).astype(BF16)


def attention_back(q, kt, vt, p, mixed_grad, span, g, head):
    lanes = slice(g * 2 * DH, (g + 1) * 2 * DH)
    kk = spread(kt)
    vv = spread(vt)
    queries = q[:, lanes]
    grad = mixed_grad[:, lanes]
    prob_grad = dot(grad, vv)
    probs = p[g]
    parts = []
    for h in range(2):
        one = probs[:, h * span : (h + 1) * span].astype(F32)
        change = prob_grad[:, h * span : (h + 1) * span]
        score = one * (change - jnp.sum(one * change, axis=1, keepdims=True))
        if head is not None:
            head(2 * g + h, score)
        parts.append(score.astype(BF16))
    score = jnp.concatenate(parts, axis=1)
    query_grad = (dot(score, kk, 1, 1) * 0.125).astype(BF16)
    key_grad = dot(queries, score, 0, 0)
    value_grad = dot(grad, probs, 0, 0)
    key_grad = key_grad[:DH, :span] + key_grad[DH:, span:]
    value_grad = value_grad[:DH, :span] + value_grad[DH:, span:]
    return query_grad, key_grad, value_grad


def cross_back(q, pair, p, mixed_grad, q_out, pair_out):
    kv = pair.shape[0] // 2
    span = pair.shape[1]
    for g in range(kv // DH):
        mine = slice(g * DH, (g + 1) * DH)
        far = slice(kv + g * DH, kv + (g + 1) * DH)
        query_grad, key_grad, value_grad = attention_back(
            q, pair[mine], pair[far], p, mixed_grad, span, g, None
        )
        q_out[:, g * 2 * DH : (g + 1) * 2 * DH] = query_grad
        pair_out[mine] = key_grad.astype(BF16)
        pair_out[far] = value_grad.astype(BF16)


def cross_grads(branch, mixed, normed, q_grad, middle, grad, gain, w0, w1, w2, w3, s0, s1, s2, s3,
                grad_out, gain_out, branch_out, mixed_out, g0, g1, g2, g3):
    width = middle.shape[1]
    size = width // 4
    dq = q_grad[...]
    for p, g in enumerate((g0, g1, g2, g3)):
        g[:, :width] = dot(rows_of(normed, p), dq, 0, 0).astype(BF16)
        g[:, width:] = dot(rows_of(branch, p), mixed[...], 0, 0).astype(BF16)
    dn = project_back(dq, [w[...] for w in (w0, w1, w2, w3)])
    back, gain_grad = norm_back(middle[...], gain[...], dn)
    total = grad[...] + back
    grad_out[...] = total
    gain_out[...] = gain_grad
    low = total.astype(BF16)
    branch_out[...] = low
    mixed_out[...] = project(low, [s[...] for s in (s0, s1, s2, s3)]).astype(BF16)


def self_back(q, kt, vt, p, mixed_grad, out, diagonal_out):
    length = q.shape[0]
    width = q.shape[1]
    kv = kt.shape[0]

    def head(h, score):
        diagonal_out[h] = diagonals(score)

    keys = []
    values = []
    for g in range(kv // DH):
        mine = slice(g * DH, (g + 1) * DH)
        query_grad, key_grad, value_grad = attention_back(
            q, kt[mine], vt[mine], p, mixed_grad, length, g, head
        )
        out[:, g * 2 * DH : (g + 1) * 2 * DH] = query_grad
        keys.append(key_grad)
        values.append(value_grad)
    out[:, width:] = jnp.concatenate(keys + values, axis=0).T.astype(BF16)


def self_grads(normed_t, grads, g0, g1, g2, g3):
    size = normed_t.shape[0] // 4
    for p, g in enumerate((g0, g1, g2, g3)):
        g[...] = dot(normed_t[p * size : (p + 1) * size], grads[...]).astype(BF16)


def restore(value, order):
    high = value.astype(BF16)
    low = (value - high.astype(F32)).astype(BF16)
    return dot(high, order, 1, 1) + dot(low, order, 1, 1)


def self_end(x, grad, grads, gain, order, w0, w1, w2, w3, input_out, gain_out):
    dn = project_back(grads[...], [w[...] for w in (w0, w1, w2, w3)])
    back, gain_grad = norm_back(x[...].astype(F32), gain[...], dn)
    input_out[...] = restore(grad[...] + back, order[...])
    gain_out[...] = gain_grad


def memory_grads(memory_t, pair_t, branch, mixed, g0, g1, g2, g3):
    size = memory_t.shape[0] // 4
    width = pair_t.shape[0]
    pair = transposed(pair_t[...])
    for p, g in enumerate((g0, g1, g2, g3)):
        g[:, :width] = dot(memory_t[p * size : (p + 1) * size], pair).astype(BF16)
        g[:, width:] = dot(rows_of(branch, p), mixed[...], 0, 0).astype(BF16)


def memory_end(pair_t, order, w0, w1, w2, w3, out):
    pair = transposed(pair_t[...])
    out[...] = restore(project_back(pair, [w[...] for w in (w0, w1, w2, w3)]), order[...])


def shape(dims, kind):
    return jax.ShapeDtypeStruct(dims, kind)


def full(value):
    return pl.BlockSpec(value.shape, lambda i, rank=len(value.shape): (0,) * rank)


def columns(value, size, place):
    return pl.BlockSpec((value.shape[0], size), lambda i, place=place: (0, place))


def call(body, outs, args, specs=None, flops=0):
    specs = [full(a) if s is None else s for a, s in zip(args, specs or [None] * len(args))]
    moved = sum(int(np.prod(o.shape)) * o.dtype.itemsize for o in outs)
    moved += sum(int(np.prod(s.block_shape)) * a.dtype.itemsize for a, s in zip(args, specs))
    return pl.pallas_call(
        body,
        grid=(1,),
        in_specs=specs,
        out_specs=[full(o) for o in outs],
        out_shape=outs,
        compiler_params=pltpu.CompilerParams(vmem_limit_bytes=VMEM),
        cost_estimate=pl.CostEstimate(flops=flops, bytes_accessed=moved, transcendentals=0),
    )(*args)


def ffn(n, nt, dy, dyt, res, dn, pieces):
    tiles = pieces[0].shape[1] // (3 * TILE)
    piece = pl.BlockSpec((pieces[0].shape[0], 3 * TILE), lambda j: (0, j))
    keep = lambda v: pl.BlockSpec(v.shape, lambda j: (0, 0))
    outs = [shape(res.shape, F32), shape(dn.shape, F32)] + [shape(w.shape, BF16) for w in pieces]
    work = n.shape[0] * n.shape[1] * TILE * 3 * 3 * 2 * tiles
    return pl.pallas_call(
        ffn_tile,
        grid=(tiles,),
        in_specs=[keep(n), keep(nt), keep(dy), keep(dyt), keep(res), keep(dn)] + [piece] * 4,
        out_specs=[keep(res), keep(dn)] + [piece] * 4,
        out_shape=outs,
        compiler_params=pltpu.CompilerParams(vmem_limit_bytes=VMEM),
        cost_estimate=pl.CostEstimate(
            flops=work, bytes_accessed=16 * pieces[0].size + 16 * res.size, transcendentals=0
        ),
    )(n, nt, dy, dyt, res, dn, *pieces)


def shards(
    nm,
    nd,
    block_input,
    memory,
    out_grad,
    decoder_segments,
    encoder_segments,
    distance_buckets,
    self_gain,
    cross_gain,
    ffn_gain,
    position_bias,
    self_query,
    self_key,
    self_value,
    self_out,
    cross_query,
    cross_key,
    cross_value,
    cross_out,
    ffn_gate,
    ffn_up,
    ffn_down,
):
    n = nm * nd
    length, width = block_input.shape[2:]
    span = encoder_segments.shape[2]
    keys = self_key.shape[1]
    rows = self_query.shape[0]
    heads = position_bias.shape[1]
    buckets = position_bias.shape[0]
    hidden = ffn_gate.shape[1]
    place = lax.axis_index("mem")
    me = place * nd + lax.axis_index("dp")

    tiles = hidden // TILE
    first = (tiles + 1) // 2
    split = lambda w: w.reshape(rows, tiles, 1, TILE)
    ffn_shard = jnp.concatenate([split(ffn_gate), split(ffn_up), split(ffn_down)], axis=2)
    ffn_shard = ffn_shard.reshape(rows, 3 * hidden)
    cut = first * 3 * TILE
    self_w = gather(jnp.concatenate([self_query, self_key, self_value, self_out], axis=1), n)
    cross_w = gather(jnp.concatenate([cross_query, cross_out, cross_key, cross_value], axis=1), n)
    ffn_a = gather(ffn_shard[:, :cut], n)
    ffn_b = gather(ffn_shard[:, cut:], n)

    src = source(n, me)
    feature = (src[:, None] * rows + lax.iota(jnp.int32, rows)[None, :]).reshape(width)
    order = (lax.iota(jnp.int32, width)[:, None] == feature[None, :]).astype(BF16)
    small = (lax.iota(jnp.int32, n)[:, None] == src[None, :]).astype(F32)

    def reorder(value):
        return jnp.dot(value, order, preferred_element_type=F32).astype(BF16)

    def reorder_gain(gain):
        return jnp.dot(small.T, gain.reshape(n, rows), precision=HIGHEST).reshape(1, width)

    x = reorder(block_input.reshape(length, width))
    dy = reorder(out_grad.reshape(length, width))
    dyt = dy.T
    gains = [reorder_gain(g) for g in (self_gain, cross_gain, ffn_gain)]
    wide = x.astype(F32)
    scale = lax.rsqrt(jnp.mean(wide * wide, axis=1, keepdims=True) + EPSILON)
    self_normed = (wide * scale * gains[0]).astype(BF16)
    self_normed_t = self_normed.T
    local = memory.reshape(nm, span // nm, width)
    local = jnp.concatenate(
        [lax.dynamic_index_in_dim(local, place ^ t, 0, keepdims=False) for t in range(nm)], axis=0
    )
    local = reorder(local)
    local_t = local.T
    seg_col = decoder_segments.reshape(length, 1)
    seg_row = decoder_segments.reshape(1, length)
    key_seg = encoder_segments.reshape(nm, span // nm)
    key_seg = jnp.concatenate(
        [lax.dynamic_index_in_dim(key_seg, place ^ t, 0, keepdims=True) for t in range(nm)], axis=1
    )
    one_hot = (distance_buckets[:, None] == lax.iota(jnp.int32, buckets)[None, :]).astype(F32)
    distance_bias = jnp.dot(one_hot, position_bias, precision=HIGHEST).T
    line = jnp.roll(distance_bias[:, ::-1], 1, axis=1)
    start = jnp.stack([jnp.roll(line, i, axis=1) for i in range(8)], axis=1)

    stream = (length, width)
    kv = keys
    groups = kv // DH
    q, kt, vt, p, mixed, middle, cross_normed = call(
        self_forward,
        [
            shape(stream, BF16),
            shape((kv, length), BF16),
            shape((kv, length), BF16),
            shape((groups, length, 2 * length), BF16),
            shape(stream, BF16),
            shape(stream, F32),
            shape(stream, BF16),
        ],
        (x, self_normed, start, seg_col, seg_row, gains[1], *self_w),
        flops=2 * length * width * 3 * width,
    )
    pair_spec = [columns(w, 2 * kv, 2 * width // (2 * kv)) for w in cross_w]
    (pair_t,) = call(
        memory_forward,
        [shape((2 * kv, span), BF16)],
        (local, *cross_w),
        [None] + pair_spec,
        flops=2 * span * width * 2 * kv,
    )
    part = span // nm
    pair_t = jnp.concatenate(
        swap_rows([pair_t[:, t * part : (t + 1) * part] for t in range(nm)], nm, nd), axis=1
    )
    cross_q, cross_p, cross_mixed, second, ffn_normed, ffn_normed_t = call(
        cross_forward,
        [
            shape(stream, BF16),
            shape((groups, length, 2 * span), BF16),
            shape(stream, BF16),
            shape(stream, F32),
            shape(stream, BF16),
            shape((width, length), BF16),
        ],
        (middle, cross_normed, pair_t, seg_col, key_seg, gains[2], *cross_w),
        [None] * 6 + [columns(w, 2 * width, 0) for w in cross_w],
        flops=2 * length * width * 2 * width,
    )

    zero = jnp.zeros(stream, F32)
    res, dn, *grads_a = ffn(ffn_normed, ffn_normed_t, dy, dyt, zero, zero, ffn_a)
    res, dn, *grads_b = ffn(ffn_normed, ffn_normed_t, dy, dyt, res, dn, ffn_b)
    done_a = scatter(grads_a, n)
    done_b = scatter(grads_b, n)

    result, grad, ffn_gain_grad, branch, mixed_grad = call(
        ffn_end,
        [
            shape(stream, BF16),
            shape(stream, F32),
            shape((1, width), F32),
            shape(stream, BF16),
            shape(stream, BF16),
        ],
        (second, res, dn, dy, gains[2], *cross_w),
        [None] * 5 + [columns(w, width, 1) for w in cross_w],
        flops=2 * length * width * width,
    )
    cross_q_grad, pair_grad_t = call(
        cross_back,
        [shape(stream, BF16), shape((2 * kv, span), BF16)],
        (cross_q, pair_t, cross_p, mixed_grad),
        flops=2 * length * span * width * 8,
    )
    pair_grad_t = jnp.concatenate(
        swap_rows([pair_grad_t[:, t * part : (t + 1) * part] for t in range(nm)], nm, nd), axis=1
    )
    pieces = [shape((width // 4, 2 * width), BF16)] * 4
    grad, cross_gain_grad, branch, mixed_grad, *grads_c = call(
        cross_grads,
        [shape(stream, F32), shape((1, width), F32), shape(stream, BF16), shape(stream, BF16)] + pieces,
        (branch, cross_mixed, cross_normed, cross_q_grad, middle, grad, gains[1], *cross_w, *self_w),
        [None] * 7 + [columns(w, width, 0) for w in cross_w] + [columns(w, width, 2) for w in self_w],
        flops=2 * length * width * width * 4,
    )
    done_c = scatter(grads_c, n)
    grads_m = call(
        memory_grads,
        [shape((width // 4, 2 * kv + width), BF16)] * 4,
        (local_t, pair_grad_t, branch, mixed),
        flops=2 * (span + length) * width * width,
    )
    done_m = scatter(grads_m, n)
    grads, diagonal = call(
        self_back,
        [shape((length, width + 2 * kv), BF16), shape((heads, 8, length), F32)],
        (q, kt, vt, p, mixed_grad),
        flops=2 * length * length * width * 8,
    )
    grads_s = call(
        self_grads,
        [shape((width // 4, width + 2 * kv), BF16)] * 4,
        (self_normed_t, grads),
        flops=2 * length * width * 2 * width,
    )
    done_s = scatter(grads_s, n)
    input_grad, self_gain_grad = call(
        self_end,
        [shape(stream, F32), shape((1, width), F32)],
        (x, grad, grads, gains[0], order, *self_w),
        [None] * 5 + [columns(w, width + 2 * kv, 0) for w in self_w],
        flops=2 * length * width * 4 * width,
    )
    (memory_grad,) = call(
        memory_end,
        [shape((span, width), F32)],
        (pair_grad_t, order, *cross_w),
        [None] * 2 + pair_spec,
        flops=2 * span * width * 3 * width,
    )
    memory_grad = memory_grad.reshape(nm, part, width)
    memory_grad = jnp.stack(
        [lax.dynamic_index_in_dim(memory_grad, place ^ t, 0, keepdims=False) for t in range(nm)]
    )
    result = lax.dot_general(
        result, order, (((1,), (1,)), ((), ())), preferred_element_type=F32
    ).astype(BF16)

    by_row = sum(jnp.roll(diagonal[:, i], -i, axis=1) for i in range(8))
    by_distance = jnp.roll(by_row, -1, axis=1)[:, ::-1]
    table = jnp.dot(by_distance, one_hot, precision=HIGHEST).T
    gain_grads = jnp.concatenate([self_gain_grad, cross_gain_grad, ffn_gain_grad], axis=0)
    gain_grads = jnp.einsum("sd,gdr->gsr", small, gain_grads.reshape(3, n, rows), precision=HIGHEST)
    packed = jnp.concatenate([gain_grads.reshape(-1, 128), table.reshape(-1, 128)], axis=0)
    packed = sum_all(packed, n)
    gain_grads = packed[: 3 * width // 128].reshape(3, width)
    table = packed[3 * width // 128 :].reshape(buckets, heads)

    ffn_done = jnp.concatenate([done_a, done_b], axis=1).reshape(rows, tiles, 3, TILE)
    return (
        result.reshape(block_input.shape),
        input_grad.reshape(block_input.shape),
        memory_grad.reshape(memory.shape),
        gain_grads[0],
        gain_grads[1],
        gain_grads[2],
        table,
        done_s[:, :width],
        done_s[:, width : width + kv],
        done_s[:, width + kv :],
        done_m[:, 2 * kv :],
        done_c[:, :width],
        done_m[:, :kv],
        done_m[:, kv : 2 * kv],
        done_c[:, width:],
        ffn_done[:, :, 0].reshape(rows, hidden),
        ffn_done[:, :, 1].reshape(rows, hidden),
        ffn_done[:, :, 2].reshape(rows, hidden),
    )


def solution(mesh):
    stream = P("dp", "mem", None, None)
    segments = P("dp", "mem", None)
    shard = P(AXES, None)
    in_specs = (stream, P("dp", None, "mem", None), stream, segments, segments) + (P(),) * 5 + (shard,) * 11
    out_specs = (stream, stream, P("dp", None, "mem", None)) + (P(),) * 4 + (shard,) * 11
    body = functools.partial(shards, mesh.shape["mem"], mesh.shape["dp"])
    return jax.shard_map(body, mesh=mesh, in_specs=in_specs, out_specs=out_specs, check_vma=False)
```

```python
import functools

import jax
import jax.numpy as jnp
import numpy as np
from jax import lax
from jax.experimental import pallas as pl
from jax.experimental.pallas import tpu as pltpu
from jax.sharding import PartitionSpec as P

DH = 64
TILE = 256
EPSILON = 1e-06
NEGATIVE = -1e30
AXES = ("mem", "dp")
F32 = jnp.float32
BF16 = jnp.bfloat16
HIGHEST = lax.Precision.HIGHEST
VMEM = 58 * 1024 * 1024


def steps(n):
    high = list(range(n.bit_length() - 2, 2, -1))
    return (high + [2, 1], high + [1, 2])


def exchange(n, k):
    order = steps(n)
    return [(d, d ^ (1 << order[d & 1][k])) for d in range(n)]


def sibling(n):
    return [(d, d ^ 1) for d in range(n)]


def source(n, me):
    order = steps(n)
    half = n // 2
    table = np.zeros((2, half), np.int32)
    for core in range(2):
        for slot in range(half):
            for k in range(len(order[core])):
                if slot >> k & 1:
                    table[core, slot] ^= 1 << order[core][k]
    odd = (me & 1) == 1
    own = jnp.where(odd, table[1], table[0])
    other = jnp.where(odd, table[0], table[1])
    return jnp.concatenate([me ^ own, me ^ 1 ^ other])


class Order:
    def __init__(self, token):
        self.token = token

    def tie(self, value):
        value, self.token = lax.optimization_barrier((value, self.token))
        return value

    wait = tie


class Gather:
    def __init__(self, shard, n, order):
        self.n = n
        self.order = order
        self.held = shard
        self.last = n.bit_length() - 3
        self.k = 0
        self.flying = None

    def start(self):
        held = self.order.tie(self.held) if self.k == 0 else self.held
        self.flying = lax.ppermute(held, AXES, exchange(self.n, self.k))

    def wait(self):
        came = self.order.wait(self.flying)
        if self.k < self.last:
            self.held = jnp.concatenate([self.held, came], axis=0)
        else:
            self.pieces = [self.held, came]
        self.k += 1

    def start_twin(self):
        self.flying = [lax.ppermute(p, AXES, sibling(self.n)) for p in self.pieces]

    def wait_twin(self):
        self.pieces = self.pieces + [self.order.wait(p) for p in self.flying]
        return self.pieces


class Scatter:
    def __init__(self, pieces, n, order):
        self.n = n
        self.order = order
        self.pieces = pieces
        self.k = n.bit_length() - 3

    def start_twin(self):
        self.flying = [lax.ppermute(p, AXES, sibling(self.n)) for p in self.pieces[2:]]

    def wait_twin(self):
        there = [self.order.wait(p) for p in self.flying]
        self.send = (self.pieces[1].astype(F32) + there[1].astype(F32)).astype(BF16)
        self.held = self.pieces[0].astype(F32) + there[0].astype(F32)

    def start(self):
        self.flying = lax.ppermute(self.send, AXES, exchange(self.n, self.k))

    def wait(self):
        came = self.order.wait(self.flying)
        held = self.held + came.astype(F32)
        self.k -= 1
        if self.k >= 0:
            half = held.shape[0] // 2
            self.send = held[half:].astype(BF16)
            held = held[:half]
        self.held = held


class Total:
    def __init__(self, value, n, order):
        self.value = value
        self.n = n
        self.order = order
        self.bit = 0

    def start(self):
        pairs = [(d, d ^ (1 << self.bit)) for d in range(self.n)]
        self.flying = lax.ppermute(self.value, AXES, pairs)

    def wait(self):
        self.value = self.value + self.order.wait(self.flying)
        self.bit += 1


def swap_rows(blocks, nm, nd):
    n = nm * nd
    return [blocks[0]] + [
        lax.ppermute(blocks[t], AXES, [(d, d ^ (t * nd)) for d in range(n)]) for t in range(1, nm)
    ]


def dot(left, right, a=1, b=0):
    return lax.dot_general(left, right, (((a,), (b,)), ((), ())), preferred_element_type=F32)


def rows_of(left, p):
    size = left.shape[1] // 4
    return left[:, p * size : (p + 1) * size]


def project(left, weights):
    total = dot(rows_of(left, 0), weights[0])
    for p in range(1, 4):
        total = total + dot(rows_of(left, p), weights[p])
    return total


def project_back(left, weights):
    return jnp.concatenate([dot(left, w, 1, 1) for w in weights], axis=1)


def scale_of(stream):
    return lax.rsqrt(jnp.mean(stream * stream, axis=1, keepdims=True) + EPSILON)


def norm_back(stream, gain, grad):
    scale = scale_of(stream)
    weighted = grad * gain
    inner = jnp.mean(weighted * stream, axis=1, keepdims=True)
    out = scale * weighted - stream * (scale * scale * scale) * inner
    return out, jnp.sum(grad * stream * scale, axis=0, keepdims=True)


def transposed(value):
    return value.astype(F32).T.astype(BF16)


def spread(part):
    zero = jnp.zeros_like(part)
    top = jnp.concatenate([part, zero], axis=1)
    low = jnp.concatenate([zero, part], axis=1)
    return jnp.concatenate([top, low], axis=0)


def softmax(scores):
    expo = jnp.exp(scores - jnp.max(scores, axis=1, keepdims=True))
    return (expo / jnp.sum(expo, axis=1, keepdims=True)).astype(BF16)


def line_of(buckets, count):
    rows = lax.broadcasted_iota(jnp.int32, (count, buckets.shape[1]), 0)
    return (rows == buckets).astype(F32)


def pick(value, row):
    return lax.broadcasted_iota(jnp.int32, value.shape, 0) == row


def toeplitz(line):
    first = jnp.broadcast_to(line, (8, line.shape[1]))
    block = first
    for i in range(1, 8):
        block = jnp.where(pick(block, i), pltpu.roll(first, i, 1), block)
    size = 8
    while size < line.shape[1]:
        block = jnp.concatenate([block, pltpu.roll(block, size, 1)], axis=0)
        size *= 2
    return block


def diagonals(block):
    size = block.shape[0]
    while size > 8:
        size //= 2
        block = block[:size] + pltpu.roll(block[size:], block.shape[1] - size, 1)
    total = block
    for i in range(1, 8):
        total = jnp.where(pick(block, i), pltpu.roll(block, block.shape[1] - i, 1), total)
    return jnp.sum(total, axis=0, keepdims=True)


def split_dot(value, order, b):
    total = None
    for _ in range(3):
        high = value.astype(BF16)
        part = dot(high, order, 1, b)
        total = part if total is None else total + part
        value = value - high.astype(F32)
    return total


def pack(tiles, first, sq, sk, sv, so, cq, ck, cv, co, fg, fu, fd, self_out, cross_out, a_out, b_out):
    for out, parts in ((self_out, (sq, sk, sv, so)), (cross_out, (cq, co, ck, cv))):
        at = 0
        for part in parts:
            size = part.shape[1]
            out[:, at : at + size] = part[...]
            at += size
    for j in range(tiles):
        out = a_out if j < first else b_out
        at = (j if j < first else j - first) * 3 * TILE
        for i, part in enumerate((fg, fu, fd)):
            out[:, at + i * TILE : at + (i + 1) * TILE] = part[:, j * TILE : (j + 1) * TILE]


def arrange(places, x_in, dy_in, feature, gains_in, x_out, dy_out, dyt_out, n_out, nt_out, gains_out, order_out):
    width = feature.shape[1]
    rows = lax.broadcasted_iota(jnp.int32, (width, width), 0)
    order = (rows == feature[...]).astype(F32).astype(BF16)
    order_out[...] = order
    gains = split_dot(gains_in[...], order, 0)
    gains_out[...] = gains
    x = dot(x_in[...], order)
    x_out[...] = x.astype(BF16)
    n = x * scale_of(x) * gains[0:1]
    n_out[...] = n.astype(BF16)
    nt_out[...] = n.T.astype(BF16)
    dy = dot(dy_in[...], order)
    dy_out[...] = dy.astype(BF16)
    dyt_out[...] = dy.T.astype(BF16)


def arrange_memory(places, memory, order, out, out_t):
    part = memory.shape[1]
    for t in range(memory.shape[0]):
        block = dot(memory[places[t]], order[...])
        out[t * part : (t + 1) * part] = block.astype(BF16)
    out_t[...] = out[...].astype(F32).T.astype(BF16)


def self_forward(x, normed, bias, buckets, seg_col, seg_row, gains, w0, w1, w2, w3,
                 q_out, kt_out, vt_out, p_out, mixed_out, middle_out, n_out):
    weights = (w0, w1, w2, w3)
    width = x.shape[1]
    keys = w0.shape[1] - 2 * width
    kv = keys // 2
    length = x.shape[0]
    n = normed[...]
    q_out[...] = (project(n, [w[:, :width] for w in weights]).astype(BF16).astype(F32) * 0.125).astype(BF16)
    pair = project(n, [w[:, width : width + keys] for w in weights])
    pair_t = pair.T.astype(BF16)
    kt_out[...] = pair_t[:kv]
    vt_out[...] = pair_t[kv:]
    row = lax.broadcasted_iota(jnp.int32, (length, length), 0)
    column = lax.broadcasted_iota(jnp.int32, (length, length), 1)
    allowed = (column <= row) & (seg_col[...] == seg_row[...])
    lines = jnp.dot(bias[...], line_of(buckets[...], bias.shape[1]), precision=HIGHEST)
    for g in range(kv // DH):
        kk = spread(kt_out[g * DH : (g + 1) * DH])
        vv = spread(vt_out[g * DH : (g + 1) * DH])
        scores = dot(q_out[:, g * 2 * DH : (g + 1) * 2 * DH], kk)
        for h in range(2):
            part = scores[:, h * length : (h + 1) * length] + toeplitz(lines[2 * g + h : 2 * g + h + 1])
            p_out[g, :, h * length : (h + 1) * length] = softmax(jnp.where(allowed, part, NEGATIVE))
        mixed_out[:, g * 2 * DH : (g + 1) * 2 * DH] = dot(p_out[g], vv, 1, 1).astype(BF16)
    middle = x[...].astype(F32) + project_back(mixed_out[...], [w[:, width + keys :] for w in weights])
    middle_out[...] = middle
    n_out[...] = (middle * scale_of(middle) * gains[1:2]).astype(BF16)


def memory_forward(memory, w0, w1, w2, w3, pair_out):
    pair = project(memory[...], [w[...] for w in (w0, w1, w2, w3)])
    pair_out[...] = pair.T.astype(BF16)


def cross_forward(middle, normed, pair, seg_col, seg_row, gains, w0, w1, w2, w3,
                  q_out, p_out, mixed_out, second_out, n_out, nt_out):
    weights = (w0, w1, w2, w3)
    width = middle.shape[1]
    kv = pair.shape[0] // 2
    span = pair.shape[1]
    q = project(normed[...], [w[:, :width] for w in weights])
    q_out[...] = (q.astype(BF16).astype(F32) * 0.125).astype(BF16)
    allowed = seg_col[...] == seg_row[...]
    for g in range(kv // DH):
        kk = spread(pair[g * DH : (g + 1) * DH])
        vv = spread(pair[kv + g * DH : kv + (g + 1) * DH])
        scores = dot(q_out[:, g * 2 * DH : (g + 1) * 2 * DH], kk)
        for h in range(2):
            part = scores[:, h * span : (h + 1) * span]
            p_out[g, :, h * span : (h + 1) * span] = softmax(jnp.where(allowed, part, NEGATIVE))
        mixed_out[:, g * 2 * DH : (g + 1) * 2 * DH] = dot(p_out[g], vv, 1, 1).astype(BF16)
    second = middle[...] + project_back(mixed_out[...], [w[:, width:] for w in weights])
    second_out[...] = second
    n = second * scale_of(second) * gains[2:3]
    n_out[...] = n.astype(BF16)
    nt_out[...] = n.T.astype(BF16)


def ffn_tile(n, nt, dy, dyt, res_in, dn_in, w0, w1, w2, w3, res_out, dn_out, g0, g1, g2, g3):
    weights = (w0, w1, w2, w3)

    @pl.when(pl.program_id(0) == 0)
    def _():
        res_out[...] = res_in[...]
        dn_out[...] = dn_in[...]

    pair = project(n[...], [w[:, : 2 * TILE] for w in weights])
    gate = pair[:, :TILE]
    lifted = pair[:, TILE:]
    hidden_grad = project(dy[...], [w[:, 2 * TILE :] for w in weights])
    root = 0.7978845608028654
    square = gate * gate
    tanh = jnp.tanh(root * gate * (1.0 + 0.044715 * square))
    half = 0.5 * (1.0 + tanh)
    gelu = gate * half
    slope = half + 0.5 * gate * (1.0 - tanh * tanh) * (root * (1.0 + 3.0 * 0.044715 * square))
    hidden = (gelu * lifted).astype(BF16)
    pair_grad = jnp.concatenate(
        [(hidden_grad * lifted * slope).astype(BF16), (hidden_grad * gelu).astype(BF16)], axis=1
    )
    res_out[...] += project_back(hidden, [w[:, 2 * TILE :] for w in weights])
    dn_out[...] += project_back(pair_grad, [w[:, : 2 * TILE] for w in weights])
    size = n.shape[1] // 4
    for p, g in enumerate((g0, g1, g2, g3)):
        g[:, : 2 * TILE] = dot(nt[p * size : (p + 1) * size], pair_grad).astype(BF16)
        g[:, 2 * TILE :] = dot(dyt[p * size : (p + 1) * size], hidden).astype(BF16)


def ffn_end(second, res, dn, dy, gains, w0, w1, w2, w3, result_out, grad_out, gain_out, branch_out, mixed_out):
    result_out[...] = (second[...] + res[...]).astype(BF16)
    back, gain_grad = norm_back(second[...], gains[2:3], dn[...])
    grad = dy[...].astype(F32) + back
    grad_out[...] = grad
    gain_out[...] = gain_grad
    branch = grad.astype(BF16)
    branch_out[...] = branch
    mixed_out[...] = project(branch, [w[...] for w in (w0, w1, w2, w3)]).astype(BF16)


def attention_back(q, kt, vt, p, mixed_grad, span, g, head):
    lanes = slice(g * 2 * DH, (g + 1) * 2 * DH)
    kk = spread(kt)
    vv = spread(vt)
    queries = q[:, lanes]
    grad = mixed_grad[:, lanes]
    prob_grad = dot(grad, vv)
    probs = p[g]
    parts = []
    for h in range(2):
        one = probs[:, h * span : (h + 1) * span].astype(F32)
        change = prob_grad[:, h * span : (h + 1) * span]
        score = one * (change - jnp.sum(one * change, axis=1, keepdims=True))
        if head is not None:
            head(2 * g + h, score)
        parts.append(score.astype(BF16))
    score = jnp.concatenate(parts, axis=1)
    query_grad = (dot(score, kk, 1, 1) * 0.125).astype(BF16)
    key_grad = dot(queries, score, 0, 0)
    value_grad = dot(grad, probs, 0, 0)
    key_grad = key_grad[:DH, :span] + key_grad[DH:, span:]
    value_grad = value_grad[:DH, :span] + value_grad[DH:, span:]
    return query_grad, key_grad, value_grad


def cross_back(q, pair, p, mixed_grad, q_out, pair_out):
    kv = pair.shape[0] // 2
    span = pair.shape[1]
    for g in range(kv // DH):
        mine = slice(g * DH, (g + 1) * DH)
        far = slice(kv + g * DH, kv + (g + 1) * DH)
        query_grad, key_grad, value_grad = attention_back(
            q, pair[mine], pair[far], p, mixed_grad, span, g, None
        )
        q_out[:, g * 2 * DH : (g + 1) * 2 * DH] = query_grad
        pair_out[mine] = key_grad.astype(BF16)
        pair_out[far] = value_grad.astype(BF16)


def cross_grads(branch, mixed, normed, q_grad, middle, grad, gains, w0, w1, w2, w3, s0, s1, s2, s3,
                grad_out, gain_out, branch_out, mixed_out, g0, g1, g2, g3):
    width = middle.shape[1]
    size = width // 4
    dq = q_grad[...]
    for p, g in enumerate((g0, g1, g2, g3)):
        g[:, :width] = dot(rows_of(normed, p), dq, 0, 0).astype(BF16)
        g[:, width:] = dot(rows_of(branch, p), mixed[...], 0, 0).astype(BF16)
    dn = project_back(dq, [w[...] for w in (w0, w1, w2, w3)])
    back, gain_grad = norm_back(middle[...], gains[1:2], dn)
    total = grad[...] + back
    grad_out[...] = total
    gain_out[...] = gain_grad
    low = total.astype(BF16)
    branch_out[...] = low
    mixed_out[...] = project(low, [s[...] for s in (s0, s1, s2, s3)]).astype(BF16)


def self_back(q, kt, vt, p, mixed_grad, buckets, out, table_out, lines):
    length = q.shape[0]
    width = q.shape[1]
    kv = kt.shape[0]

    def head(h, score):
        lines[h : h + 1] = diagonals(score)

    keys = []
    values = []
    for g in range(kv // DH):
        mine = slice(g * DH, (g + 1) * DH)
        query_grad, key_grad, value_grad = attention_back(
            q, kt[mine], vt[mine], p, mixed_grad, length, g, head
        )
        out[:, g * 2 * DH : (g + 1) * 2 * DH] = query_grad
        keys.append(key_grad)
        values.append(value_grad)
    out[:, width:] = jnp.concatenate(keys + values, axis=0).T.astype(BF16)
    table_out[...] = lax.dot_general(
        lines[...],
        line_of(buckets[...], table_out.shape[1]),
        (((1,), (1,)), ((), ())),
        precision=HIGHEST,
        preferred_element_type=F32,
    )


def restore(value, order):
    high = value.astype(BF16)
    low = (value - high.astype(F32)).astype(BF16)
    return dot(high, order, 1, 1) + dot(low, order, 1, 1)


def self_end(x, grad, grads, gains, order, cross_gain, ffn_gain, table, w0, w1, w2, w3, input_out, packed_out):
    dn = project_back(grads[...], [w[...] for w in (w0, w1, w2, w3)])
    back, gain_grad = norm_back(x[...].astype(F32), gains[0:1], dn)
    input_out[...] = restore(grad[...] + back, order[...])
    width = x.shape[1]
    found = jnp.concatenate([gain_grad, cross_gain[...], ffn_gain[...], jnp.zeros((5, width), F32)], axis=0)
    found = split_dot(found, order[...], 1)
    packed_out[...] = jnp.zeros_like(packed_out)
    lines = width // 128
    for i in range(3):
        for j in range(lines):
            packed_out[i * lines + j : i * lines + j + 1] = found[i : i + 1, j * 128 : (j + 1) * 128]
    packed_out[3 * lines :, : table.shape[1]] = table[...]


def last_grads(normed_t, grads, memory_t, pair_t, branch, mixed, g0, g1, g2, g3):
    size = memory_t.shape[0] // 4
    width = grads.shape[1]
    keys = pair_t.shape[0]
    pair = transposed(pair_t[...])
    for p, g in enumerate((g0, g1, g2, g3)):
        mine = slice(p * size, (p + 1) * size)
        g[:, :width] = dot(normed_t[mine], grads[...]).astype(BF16)
        g[:, width : width + keys] = dot(memory_t[mine], pair).astype(BF16)
        g[:, width + keys :] = dot(rows_of(branch, p), mixed[...], 0, 0).astype(BF16)


def memory_end(places, pair_t, order, result, w0, w1, w2, w3, out, result_out):
    pair = transposed(pair_t[...])
    grad = restore(project_back(pair, [w[...] for w in (w0, w1, w2, w3)]), order[...])
    part = out.shape[1]
    for t in range(out.shape[0]):
        out[places[t]] = grad[t * part : (t + 1) * part]
    result_out[...] = dot(result[...], order[...], 1, 1).astype(BF16)


def finish(held, came, token, out):
    out[...] = held[...] + came[...].astype(F32)


def shape(dims, kind):
    return jax.ShapeDtypeStruct(dims, kind)


def full(value):
    return pl.BlockSpec(value.shape, lambda i, rank=len(value.shape): (0,) * rank)


def columns(value, size, place):
    return pl.BlockSpec((value.shape[0], size), lambda i, place=place: (0, place))


SCALARS = pl.BlockSpec(memory_space=pltpu.SMEM)


def call(body, outs, args, specs=None, flops=0, scratch=()):
    specs = [full(a) if s is None else s for a, s in zip(args, specs or [None] * len(args))]
    moved = sum(int(np.prod(o.shape)) * o.dtype.itemsize for o in outs)
    moved += sum(int(np.prod(s.block_shape or a.shape)) * a.dtype.itemsize for a, s in zip(args, specs))
    return pl.pallas_call(
        body,
        grid=(1,),
        in_specs=specs,
        out_specs=[full(o) for o in outs],
        out_shape=outs,
        scratch_shapes=scratch,
        compiler_params=pltpu.CompilerParams(vmem_limit_bytes=VMEM),
        cost_estimate=pl.CostEstimate(flops=flops, bytes_accessed=moved, transcendentals=0),
    )(*args)


def ffn(n, nt, dy, dyt, res, dn, pieces):
    tiles = pieces[0].shape[1] // (3 * TILE)
    piece = pl.BlockSpec((pieces[0].shape[0], 3 * TILE), lambda j: (0, j))
    keep = lambda v: pl.BlockSpec(v.shape, lambda j: (0, 0))
    outs = [shape(res.shape, F32), shape(dn.shape, F32)] + [shape(w.shape, BF16) for w in pieces]
    work = n.shape[0] * n.shape[1] * TILE * 3 * 3 * 2 * tiles
    return pl.pallas_call(
        ffn_tile,
        grid=(tiles,),
        in_specs=[keep(n), keep(nt), keep(dy), keep(dyt), keep(res), keep(dn)] + [piece] * 4,
        out_specs=[keep(res), keep(dn)] + [piece] * 4,
        out_shape=outs,
        compiler_params=pltpu.CompilerParams(vmem_limit_bytes=VMEM),
        cost_estimate=pl.CostEstimate(
            flops=work, bytes_accessed=16 * pieces[0].size, transcendentals=0
        ),
    )(n, nt, dy, dyt, res, dn, *pieces)


def shards(
    nm,
    nd,
    block_input,
    memory,
    out_grad,
    decoder_segments,
    encoder_segments,
    distance_buckets,
    self_gain,
    cross_gain,
    ffn_gain,
    position_bias,
    self_query,
    self_key,
    self_value,
    self_out,
    cross_query,
    cross_key,
    cross_value,
    cross_out,
    ffn_gate,
    ffn_up,
    ffn_down,
):
    n = nm * nd
    length, width = block_input.shape[2:]
    span = encoder_segments.shape[2]
    keys = self_key.shape[1]
    rows = self_query.shape[0]
    heads = position_bias.shape[1]
    buckets = position_bias.shape[0]
    hidden = ffn_gate.shape[1]
    place = lax.axis_index("mem")
    me = place * nd + lax.axis_index("dp")

    tiles = hidden // TILE
    first = (tiles + 1) // 2
    shard_a = shape((rows, first * 3 * TILE), BF16)
    shard_b = shape((rows, (tiles - first) * 3 * TILE), BF16)
    both = shape((rows, 2 * width + 2 * keys), BF16)
    packed = call(
        functools.partial(pack, tiles, first),
        [both, both, shard_a, shard_b],
        (self_query, self_key, self_value, self_out, cross_query, cross_key, cross_value, cross_out, ffn_gate, ffn_up, ffn_down),
    )
    run = Order(jnp.full((8, 128), me, F32))
    gs, gc, ga, gb = (Gather(value, n, run) for value in packed)
    gs.start()

    src = source(n, me)
    feature = (src[:, None] * rows + lax.iota(jnp.int32, rows)[None, :]).reshape(1, width)
    places = place ^ lax.iota(jnp.int32, nm)
    stream = (length, width)
    turned = (width, length)
    gains = jnp.concatenate([jnp.stack([self_gain, cross_gain, ffn_gain]), jnp.zeros((5, width), F32)])
    x, dy, dyt, self_normed, self_normed_t, gains, order = call(
        arrange,
        [
            shape(stream, BF16),
            shape(stream, BF16),
            shape(turned, BF16),
            shape(stream, BF16),
            shape(turned, BF16),
            shape((8, width), F32),
            shape((width, width), BF16),
        ],
        (places, block_input.reshape(stream), out_grad.reshape(stream), feature, gains),
        [SCALARS, None, None, None, None],
    )
    part = span // nm
    local, local_t = call(
        arrange_memory,
        [shape((span, width), BF16), shape((width, span), BF16)],
        (places, memory.reshape(nm, part, width), order),
        [SCALARS, None, None],
    )
    seg_col = decoder_segments.reshape(length, 1)
    seg_row = decoder_segments.reshape(1, length)
    key_seg = encoder_segments.reshape(nm, part)
    key_seg = jnp.concatenate(
        [lax.dynamic_index_in_dim(key_seg, place ^ t, 0, keepdims=True) for t in range(nm)], axis=1
    )
    bucket_line = jnp.roll(distance_buckets[::-1], 1).reshape(1, length)

    kv = keys
    groups = kv // DH
    more = n.bit_length() - 5
    gs.wait()
    gs.start()
    for _ in range(more - 1):
        gs.wait()
        gs.start()
    self_normed = run.wait(self_normed)
    gs.wait()
    gs.start()
    gc.start()
    local = run.wait(local)
    gc.wait()
    gs.wait()
    gs.start()
    gc.start()
    for _ in range(more - 1):
        gc.wait()
        gc.start()
    gc.wait()
    gc.start()
    ga.start()
    gs.wait()
    gs.start_twin()
    for _ in range(more):
        ga.wait()
        ga.start()
    gc.wait()
    gc.start()
    self_w = gs.wait_twin()
    q, kt, vt, p, mixed, middle, cross_normed = call(
        self_forward,
        [
            shape(stream, BF16),
            shape((kv, length), BF16),
            shape((kv, length), BF16),
            shape((groups, length, 2 * length), BF16),
            shape(stream, BF16),
            shape(stream, F32),
            shape(stream, BF16),
        ],
        (x, run.tie(self_normed), position_bias.T, bucket_line, seg_col, seg_row, gains, *self_w),
        flops=2 * length * width * 3 * width,
    )
    run.wait(cross_normed)
    ga.wait()
    ga.start()
    gb.start()
    gc.wait()
    gc.start_twin()
    for _ in range(more):
        gb.wait()
        gb.start()
    ga.wait()
    ga.start()
    cross_w = gc.wait_twin()
    pair_spec = [columns(w, 2 * kv, 2 * width // (2 * kv)) for w in cross_w]
    (pair_t,) = call(
        memory_forward,
        [shape((2 * kv, span), BF16)],
        (run.tie(local), *cross_w),
        [None] + pair_spec,
        flops=2 * span * width * 2 * kv,
    )
    pair_t = run.wait(pair_t)
    blocks = swap_rows([pair_t[:, t * part : (t + 1) * part] for t in range(nm)], nm, nd)
    gb.wait()
    gb.start()
    ga.wait()
    ga.start_twin()
    pair_t = jnp.concatenate([run.wait(block) for block in blocks], axis=1)
    cross_q, cross_p, cross_mixed, second, ffn_normed, ffn_normed_t = call(
        cross_forward,
        [
            shape(stream, BF16),
            shape((groups, length, 2 * span), BF16),
            shape(stream, BF16),
            shape(stream, F32),
            shape(stream, BF16),
            shape(turned, BF16),
        ],
        (middle, run.tie(cross_normed), pair_t, seg_col, key_seg, gains, *cross_w),
        [None] * 6 + [columns(w, 2 * width, 0) for w in cross_w],
        flops=2 * length * width * 2 * width,
    )
    run.wait(ffn_normed)
    gb.wait()
    gb.start()

    ffn_w = ga.wait_twin()
    zero = jnp.zeros(stream, F32)
    res, dn, *pieces = ffn(run.tie(ffn_normed), ffn_normed_t, dy, dyt, zero, zero, ffn_w)
    ra = Scatter(pieces, n, run)
    run.wait(res)
    ra.start_twin()
    gb.wait()
    gb.start_twin()
    ra.wait_twin()
    ra.start()
    ffn_w = gb.wait_twin()
    res, dn, *pieces = ffn(run.tie(ffn_normed), ffn_normed_t, dy, dyt, res, dn, ffn_w)
    rb = Scatter(pieces, n, run)
    run.wait(res)
    rb.start_twin()

    result, grad, ffn_gain_grad, branch, mixed_grad = call(
        ffn_end,
        [
            shape(stream, BF16),
            shape(stream, F32),
            shape((1, width), F32),
            shape(stream, BF16),
            shape(stream, BF16),
        ],
        (second, res, dn, dy, gains, *cross_w),
        [None] * 5 + [columns(w, width, 1) for w in cross_w],
        flops=2 * length * width * width,
    )
    cross_q_grad, pair_grad_t = call(
        cross_back,
        [shape(stream, BF16), shape((2 * kv, span), BF16)],
        (cross_q, pair_t, cross_p, mixed_grad),
        flops=2 * length * span * width * 8,
    )
    pair_grad_t = run.wait(pair_grad_t)
    ra.wait()
    ra.start()
    rb.wait_twin()
    rb.start()
    pair_grad_t = run.tie(pair_grad_t)
    blocks = swap_rows([pair_grad_t[:, t * part : (t + 1) * part] for t in range(nm)], nm, nd)
    pieces = [shape((width // 4, 2 * width), BF16)] * 4
    grad, cross_gain_grad, branch, mixed_grad, *pieces = call(
        cross_grads,
        [shape(stream, F32), shape((1, width), F32), shape(stream, BF16), shape(stream, BF16)] + pieces,
        (branch, cross_mixed, cross_normed, run.tie(cross_q_grad), middle, grad, gains, *cross_w, *self_w),
        [None] * 7 + [columns(w, width, 0) for w in cross_w] + [columns(w, width, 2) for w in self_w],
        flops=2 * length * width * width * 4,
    )
    run.wait(mixed_grad)
    rc = Scatter(pieces, n, run)
    rc.start_twin()
    ra.wait()
    ra.start()
    grads, table = call(
        self_back,
        [shape((length, width + 2 * kv), BF16), shape((heads, buckets), F32)],
        (q, kt, vt, p, run.tie(mixed_grad), bucket_line),
        flops=2 * length * length * width * 8,
        scratch=[pltpu.VMEM((heads, length), F32)],
    )
    run.wait(table)
    rb.wait()
    rb.start()
    rc.wait_twin()
    rc.start()
    pair_grad_t = jnp.concatenate([run.wait(block) for block in blocks], axis=1)
    pieces = call(
        last_grads,
        [shape((width // 4, 2 * width + 4 * kv), BF16)] * 4,
        (self_normed_t, grads, local_t, pair_grad_t, branch, mixed),
        flops=2 * (span + 3 * length) * width * width,
    )
    run.wait(pieces[0])
    rs = Scatter(pieces, n, run)
    rs.start_twin()
    for _ in range(more):
        ra.wait()
        ra.start()
    input_grad, packed = call(
        self_end,
        [shape(stream, F32), shape((3 * width // 128 + heads, 128), F32)],
        (x, grad, run.tie(grads), gains, order, cross_gain_grad, ffn_gain_grad, table, *self_w),
        [None] * 8 + [columns(w, width + 2 * kv, 0) for w in self_w],
        flops=2 * length * width * 4 * width,
    )
    packed = run.wait(packed)
    total = Total(packed, n, run)
    total.start()
    rb.wait()
    rb.start()
    rs.wait_twin()
    rs.start()
    total.wait()
    total.start()
    rc.wait()
    rc.start()
    ra.wait()
    total.wait()
    total.start()
    memory_grad, result = call(
        memory_end,
        [shape((nm, part, width), F32), shape(stream, BF16)],
        (places, run.tie(pair_grad_t), order, result, *cross_w),
        [SCALARS] + [None] * 3 + pair_spec,
        flops=2 * span * width * 3 * width,
    )
    run.wait(memory_grad)
    rc.wait()
    rc.start()
    total.wait()
    total.start()
    for _ in range(more):
        rb.wait()
        rb.start()
    rs.wait()
    rs.start()
    for _ in range(n.bit_length() - 5):
        total.wait()
        total.start()
    for _ in range(more):
        rc.wait()
        rc.start()
    rb.wait()
    rc.wait()
    for _ in range(more + 1):
        rs.wait()
        rs.start()
    total.wait()
    came = run.wait(rs.flying)
    (done_s,) = call(
        finish, [shape(rs.held.shape, F32)], (rs.held, came, run.token), [None, None, pl.BlockSpec(memory_space=pl.ANY)]
    )
    done_a, done_b, done_c = (group.held for group in (ra, rb, rc))

    gain_lines = 3 * width // 128
    packed = total.value
    gain_grads = packed[:gain_lines].reshape(3, width)
    table = packed[gain_lines:, :buckets].T

    ffn_done = jnp.concatenate([done_a, done_b], axis=1).reshape(rows, tiles, 3, TILE)
    return (
        result.reshape(block_input.shape),
        input_grad.reshape(block_input.shape),
        memory_grad.reshape(memory.shape),
        gain_grads[0],
        gain_grads[1],
        gain_grads[2],
        table,
        done_s[:, :width],
        done_s[:, width : width + kv],
        done_s[:, width + kv : width + 2 * kv],
        done_s[:, width + 4 * kv :],
        done_c[:, :width],
        done_s[:, width + 2 * kv : width + 3 * kv],
        done_s[:, width + 3 * kv : width + 4 * kv],
        done_c[:, width:],
        ffn_done[:, :, 0].reshape(rows, hidden),
        ffn_done[:, :, 1].reshape(rows, hidden),
        ffn_done[:, :, 2].reshape(rows, hidden),
    )


def solution(mesh):
    stream = P("dp", "mem", None, None)
    segments = P("dp", "mem", None)
    shard = P(AXES, None)
    in_specs = (stream, P("dp", None, "mem", None), stream, segments, segments) + (P(),) * 5 + (shard,) * 11
    out_specs = (stream, stream, P("dp", None, "mem", None)) + (P(),) * 4 + (shard,) * 11
    body = functools.partial(shards, mesh.shape["mem"], mesh.shape["dp"])
    return jax.shard_map(body, mesh=mesh, in_specs=in_specs, out_specs=out_specs, check_vma=False)
```

```python
import functools
import types

import jax
import jax.numpy as jnp
import numpy as np
from jax import lax
from jax.experimental import pallas as pl
from jax.experimental.pallas import tpu as pltpu
from jax.sharding import PartitionSpec as P

DH = 64
LANES = 128
EARLY = 1
EPSILON = 1e-06
NEGATIVE = -1e30
AXES = ("mem", "dp")
F32 = jnp.float32
BF16 = jnp.bfloat16
HIGHEST = lax.Precision.HIGHEST
MIB = 1024 * 1024


PLAN = """
s x1 s c x2 c s x3 c a a p s p c s K1 c a b b a c K2
b a w2 b K3 K4 b A K5 B K6 K7 A m7 K8 K9 A w7 K10 B K11 S A p
K12 B A C t S K13 t B S C t t B S C t S C C u
""".split()


def steps(n):
    high = list(range(n.bit_length() - 2, 2, -1))
    return (high + [2, 1], high + [1, 2])


def exchange(n, k):
    order = steps(n)
    return [(d, d ^ (1 << order[d & 1][k])) for d in range(n)]


def sibling(n):
    return [(d, d ^ 1) for d in range(n)]


def source(n, me):
    order = steps(n)
    half = n // 2
    table = np.zeros((2, half), np.int32)
    for core in range(2):
        for slot in range(half):
            for k in range(len(order[core])):
                if slot >> k & 1:
                    table[core, slot] ^= 1 << order[core][k]
    odd = (me & 1) == 1
    own = jnp.where(odd, table[1], table[0])
    other = jnp.where(odd, table[0], table[1])
    return jnp.concatenate([me ^ own, me ^ 1 ^ other])


class Order:
    def __init__(self, token):
        self.token = token

    def tie(self, value):
        value, self.token = lax.optimization_barrier((value, self.token))
        return value

    wait = tie

    def pace(self, micros):
        spec = pl.BlockSpec(memory_space=pl.ANY)
        self.token = pl.pallas_call(
            idle,
            in_specs=[spec],
            out_specs=spec,
            out_shape=shape(self.token.shape, self.token.dtype),
            input_output_aliases={0: 0},
            cost_estimate=pl.CostEstimate(
                flops=micros * 1000 * 1000 * 1000, bytes_accessed=0, transcendentals=0
            ),
        )(self.token)


class Gather:
    def __init__(self, shard, n, order, twin=True):
        self.n = n
        self.order = order
        self.held = shard
        self.last = n.bit_length() - 3
        self.k = 0
        self.flying = None
        self.twin = twin
        self.pieces = None

    def send(self):
        self.flying = lax.ppermute(self.held, AXES, exchange(self.n, self.k))

    def grow(self):
        came = self.order.wait(self.flying)
        self.held = jnp.concatenate([self.held, came], axis=self.held.ndim - 2)
        self.k += 1

    def go(self):
        if self.flying is None:
            self.held = self.order.tie(self.held)
            self.send()
        elif self.pieces is not None:
            self.pieces = self.pieces + [self.order.wait(p) for p in self.flying]
        elif self.k == self.last:
            self.pieces = [self.held, self.order.wait(self.flying)]
            if self.twin:
                self.flying = [lax.ppermute(p, AXES, sibling(self.n)) for p in self.pieces]
        else:
            if self.k == 0:
                for _ in range(self.n.bit_length() - 6):
                    self.grow()
                    self.send()
            self.grow()
            self.send()


class Scatter:
    def __init__(self, pieces, n, order):
        self.n = n
        self.order = order
        self.pieces = pieces
        self.k = n.bit_length() - 3
        self.flying = None
        self.both = len(pieces) == 4
        if not self.both:
            self.held = pieces[0]
            self.low = pieces[1]

    def send(self):
        self.flying = lax.ppermute(self.low, AXES, exchange(self.n, self.k))

    def shrink(self):
        came = self.order.wait(self.flying)
        self.k -= 1
        self.low, self.held = absorb(self.held, came)

    def go(self):
        if self.flying is None and self.both:
            self.flying = [lax.ppermute(p, AXES, sibling(self.n)) for p in self.pieces[2:]]
        elif self.both:
            there = [self.order.wait(p) for p in self.flying]
            self.low, self.held = absorb_twin(*self.pieces[:2], *there)
            self.both = False
            self.send()
        elif self.flying is None:
            self.send()
        elif self.k == 0:
            self.came = self.order.wait(self.flying)
        else:
            extra = self.n.bit_length() - 6
            if self.k == extra + 1:
                for _ in range(extra):
                    self.shrink()
                    self.send()
            self.shrink()
            self.send()

    def done(self):
        return self.held + self.came.astype(F32)


def absorb_step(held, came, low_out, held_out):
    half = low_out.shape[-2]
    low_out[...] = (held[..., half:, :].astype(F32) + came[..., half:, :].astype(F32)).astype(BF16)
    held_out[...] = held[..., :half, :].astype(F32) + came[..., :half, :].astype(F32)


def absorb_twin_step(held, low, held_came, low_came, low_out, held_out):
    low_out[...] = (low[...].astype(F32) + low_came[...].astype(F32)).astype(BF16)
    held_out[...] = held[...].astype(F32) + held_came[...].astype(F32)


def by_columns(body, args, dims):
    size = dims[-1]
    tiles = 3 if size % (3 * LANES) == 0 and dims[-2] >= 64 else 1

    def spec(whole):
        block = tuple(whole[:-1]) + (size // tiles,)
        return pl.BlockSpec(block, lambda j, rank=len(whole): (0,) * (rank - 1) + (j,))

    return pl.pallas_call(
        body,
        grid=(tiles,),
        in_specs=[spec(a.shape) for a in args],
        out_specs=[spec(dims), spec(dims)],
        out_shape=[shape(dims, BF16), shape(dims, F32)],
        compiler_params=pltpu.CompilerParams(vmem_limit_bytes=20 * MIB),
        cost_estimate=pl.CostEstimate(
            flops=2 * args[0].size, bytes_accessed=10 * args[0].size, transcendentals=0
        ),
    )(*args)


def absorb(held, came):
    dims = held.shape[:-2] + (held.shape[-2] // 2, held.shape[-1])
    return by_columns(absorb_step, (held, came), dims)


def absorb_twin(held, low, held_came, low_came):
    return by_columns(absorb_twin_step, (held, low, held_came, low_came), held.shape)


class Total:
    def __init__(self, value, n, order):
        self.value = value
        self.n = n
        self.order = order
        self.bit = 0

    def send(self):
        pairs = [(d, d ^ (1 << self.bit)) for d in range(self.n)]
        self.flying = lax.ppermute(self.value, AXES, pairs)

    def take(self):
        self.value = self.value + self.order.wait(self.flying)
        self.bit += 1

    def go(self):
        if self.bit == 4:
            for _ in range(self.n.bit_length() - 6):
                self.take()
                self.send()
        self.take()
        if self.bit < self.n.bit_length() - 1:
            self.send()


def swap_rows(blocks, nm, nd):
    n = nm * nd
    return [blocks[0]] + [
        lax.ppermute(blocks[t], AXES, [(d, d ^ (t * nd)) for d in range(n)]) for t in range(1, nm)
    ]


def dot(left, right, a=1, b=0):
    return lax.dot_general(left, right, (((a,), (b,)), ((), ())), preferred_element_type=F32)


def rows_of(left, p):
    size = left.shape[1] // 4
    return left[:, p * size : (p + 1) * size]


def project(left, weights):
    total = dot(rows_of(left, 0), weights[0])
    for p in range(1, 4):
        total = total + dot(rows_of(left, p), weights[p])
    return total


def project_back(left, weights):
    return jnp.concatenate([dot(left, w, 1, 1) for w in weights], axis=1)


def scale_of(stream):
    return lax.rsqrt(jnp.mean(stream * stream, axis=1, keepdims=True) + EPSILON)


def norm_back(stream, gain, grad):
    scale = scale_of(stream)
    weighted = grad * gain
    inner = jnp.mean(weighted * stream, axis=1, keepdims=True)
    out = scale * weighted - stream * (scale * scale * scale) * inner
    return out, jnp.sum(grad * stream * scale, axis=0, keepdims=True)


def transposed(value):
    return value.astype(F32).T.astype(BF16)


def spread(part):
    zero = jnp.zeros_like(part)
    top = jnp.concatenate([part, zero], axis=1)
    low = jnp.concatenate([zero, part], axis=1)
    return jnp.concatenate([top, low], axis=0)


def softmax(scores):
    expo = jnp.exp(scores - jnp.max(scores, axis=1, keepdims=True))
    return (expo / jnp.sum(expo, axis=1, keepdims=True)).astype(BF16)


def line_of(buckets, count):
    rows = lax.broadcasted_iota(jnp.int32, (count, buckets.shape[1]), 0)
    return (rows == buckets).astype(F32)


def pick(value, row):
    return lax.broadcasted_iota(jnp.int32, value.shape, 0) == row


def toeplitz(line):
    first = jnp.broadcast_to(line, (8, line.shape[1]))
    block = first
    for i in range(1, 8):
        block = jnp.where(pick(block, i), pltpu.roll(first, i, 1), block)
    size = 8
    while size < line.shape[1]:
        block = jnp.concatenate([block, pltpu.roll(block, size, 1)], axis=0)
        size *= 2
    return block


def diagonals(block):
    size = block.shape[0]
    while size > 8:
        size //= 2
        block = block[:size] + pltpu.roll(block[size:], block.shape[1] - size, 1)
    total = block
    for i in range(1, 8):
        total = jnp.where(pick(block, i), pltpu.roll(block, block.shape[1] - i, 1), total)
    return jnp.sum(total, axis=0, keepdims=True)


def split_dot(value, order, b):
    total = None
    for _ in range(3):
        high = value.astype(BF16)
        part = dot(high, order, 1, b)
        total = part if total is None else total + part
        value = value - high.astype(F32)
    return total


def pack(first, core, sq, sk, sv, so, cq, ck, cv, co, fg, fu, fd, self_out, cross_out, a_out, b_out, far_out):
    for out, parts in ((self_out, (sq, sk, sv, so)), (cross_out, (cq, co, ck, cv))):
        at = 0
        for part in parts:
            size = part.shape[1]
            out[:, at : at + size] = part[...]
            at += size
    odd = core[0] == 1
    half = fg.shape[1] // 2
    last = half - first
    for i, part in enumerate((fg, fu, fd)):
        low = part[:, :half].astype(F32)
        high = part[:, half:].astype(F32)
        mine = jnp.where(odd, high, low).astype(BF16)
        far = jnp.where(odd, low, high).astype(BF16)
        a_out[:, i * first : (i + 1) * first] = mine[:, :first]
        b_out[:, i * last : (i + 1) * last] = mine[:, first:]
        far_out[:, i * first : (i + 1) * first] = far[:, :first]
        far_out[:, 3 * first + i * last : 3 * first + (i + 1) * last] = far[:, first:]


def unpack(first, core, a, b, far, g_out, u_out, d_out):
    odd = core[0] == 1
    half = g_out.shape[1] // 2
    last = half - first
    for i, out in enumerate((g_out, u_out, d_out)):
        mine = jnp.concatenate(
            [a[:, i * first : (i + 1) * first], b[:, i * last : (i + 1) * last]], axis=1
        )
        other = jnp.concatenate(
            [
                far[:, i * first : (i + 1) * first],
                far[:, 3 * first + i * last : 3 * first + (i + 1) * last],
            ],
            axis=1,
        )
        out[:, :half] = jnp.where(odd, other, mine)
        out[:, half:] = jnp.where(odd, mine, other)


def turn(value):
    half = value.shape[1] // 2
    return jnp.concatenate([value[:, half:], value[:, :half]], axis=1)


def inner(value):
    b = value.shape[1] // 8
    return jnp.concatenate(
        [value[:, : 5 * b], value[:, 6 * b : 7 * b], value[:, 5 * b : 6 * b], value[:, 7 * b :]],
        axis=1,
    )


def both_cores(mine, other):
    return jnp.concatenate([inner(mine[...]), inner(turn(other[...]))], axis=0)


def pair_up(mine, other, out, out_t):
    value = both_cores(mine, other)
    out[...] = value
    out_t[...] = transposed(value)


def arrange(places, x_in, dy_in, feature, gains_in, x_out, dy_out, n_out, nt_out, gains_out, order_out):
    width = feature.shape[1]
    rows = lax.broadcasted_iota(jnp.int32, (width, width), 0)
    order = (rows == feature[...]).astype(F32).astype(BF16)
    order_out[...] = order
    gains = split_dot(gains_in[...], order, 0)
    gains_out[...] = gains
    x = dot(x_in[...], order)
    x_out[...] = x.astype(BF16)
    n = x * scale_of(x) * gains[0:1]
    n_out[...] = n.astype(BF16)
    nt_out[...] = n.T.astype(BF16)
    dy_out[...] = dot(dy_in[...], order).astype(BF16)


def arrange_memory(places, memory, order, out, out_t):
    part = memory.shape[1]
    for t in range(memory.shape[0]):
        block = dot(memory[places[t]], order[...])
        out[t * part : (t + 1) * part] = block.astype(BF16)
    out_t[...] = out[...].astype(F32).T.astype(BF16)


def self_forward(x, normed, bias, buckets, seg_col, seg_row, gains, w0, w1, w2, w3,
                 q_out, kt_out, vt_out, p_out, mixed_out, middle_out, n_out):
    weights = (w0, w1, w2, w3)
    width = x.shape[1]
    keys = w0.shape[1] - 2 * width
    kv = keys // 2
    length = x.shape[0]
    n = normed[...]
    q_out[...] = (project(n, [w[:, :width] for w in weights]).astype(BF16).astype(F32) * 0.125).astype(BF16)
    pair = project(n, [w[:, width : width + keys] for w in weights])
    pair_t = pair.T.astype(BF16)
    kt_out[...] = pair_t[:kv]
    vt_out[...] = pair_t[kv:]
    row = lax.broadcasted_iota(jnp.int32, (length, length), 0)
    column = lax.broadcasted_iota(jnp.int32, (length, length), 1)
    allowed = (column <= row) & (seg_col[...] == seg_row[...])
    lines = jnp.dot(bias[...], line_of(buckets[...], bias.shape[1]), precision=HIGHEST)
    for g in range(kv // DH):
        kk = spread(kt_out[g * DH : (g + 1) * DH])
        vv = spread(vt_out[g * DH : (g + 1) * DH])
        scores = dot(q_out[:, g * 2 * DH : (g + 1) * 2 * DH], kk)
        for h in range(2):
            part = scores[:, h * length : (h + 1) * length] + toeplitz(lines[2 * g + h : 2 * g + h + 1])
            p_out[g, :, h * length : (h + 1) * length] = softmax(jnp.where(allowed, part, NEGATIVE))
        mixed_out[:, g * 2 * DH : (g + 1) * 2 * DH] = dot(p_out[g], vv, 1, 1).astype(BF16)
    middle = x[...].astype(F32) + project_back(mixed_out[...], [w[:, width + keys :] for w in weights])
    middle_out[...] = middle
    n_out[...] = (middle * scale_of(middle) * gains[1:2]).astype(BF16)


def memory_forward(memory, w0, w1, w2, w3, pair_out):
    pair = project(memory[...], [w[...] for w in (w0, w1, w2, w3)])
    pair_out[...] = pair.T.astype(BF16)


def cross_forward(middle, normed, pair, seg_col, seg_row, gains, w0, w1, w2, w3,
                  q_out, p_out, mixed_out, second_out, n_out):
    weights = (w0, w1, w2, w3)
    width = middle.shape[1]
    kv = pair.shape[0] // 2
    span = pair.shape[1]
    q = project(normed[...], [w[:, :width] for w in weights])
    q_out[...] = (q.astype(BF16).astype(F32) * 0.125).astype(BF16)
    allowed = seg_col[...] == seg_row[...]
    for g in range(kv // DH):
        kk = spread(pair[g * DH : (g + 1) * DH])
        vv = spread(pair[kv + g * DH : kv + (g + 1) * DH])
        scores = dot(q_out[:, g * 2 * DH : (g + 1) * 2 * DH], kk)
        for h in range(2):
            part = scores[:, h * span : (h + 1) * span]
            p_out[g, :, h * span : (h + 1) * span] = softmax(jnp.where(allowed, part, NEGATIVE))
        mixed_out[:, g * 2 * DH : (g + 1) * 2 * DH] = dot(p_out[g], vv, 1, 1).astype(BF16)
    second = middle[...] + project_back(mixed_out[...], [w[:, width:] for w in weights])
    second_out[...] = second
    n_out[...] = (second * scale_of(second) * gains[2:3]).astype(BF16)


def ffn_work(n, nt, dy, dyt, w0, w1, g0, g1):
    weights = [w0[0], w1[0], w0[1], w1[1]]
    size = w0.shape[2] // 3
    pair = project(n[...], [w[:, : 2 * size] for w in weights])
    gate = pair[:, :size]
    lifted = pair[:, size:]
    hidden_grad = project(dy[...], [w[:, 2 * size :] for w in weights])
    root = 0.7978845608028654
    square = gate * gate
    tanh = jnp.tanh(root * gate * (1.0 + 0.044715 * square))
    half = 0.5 * (1.0 + tanh)
    gelu = gate * half
    slope = half + 0.5 * gate * (1.0 - tanh * tanh) * (root * (1.0 + 3.0 * 0.044715 * square))
    hidden = (gelu * lifted).astype(BF16)
    pair_grad = jnp.concatenate(
        [(hidden_grad * lifted * slope).astype(BF16), (hidden_grad * gelu).astype(BF16)], axis=1
    )
    rows = nt.shape[0] // 4
    for p in range(4):
        g = (g0, g1)[p % 2]
        mine = slice(p * rows, (p + 1) * rows)
        g[p // 2, :, : 2 * size] = dot(nt[mine], pair_grad).astype(BF16)
        g[p // 2, :, 2 * size :] = dot(dyt[mine], hidden).astype(BF16)
    res = project_back(hidden, [w[:, 2 * size :] for w in weights])
    dn = project_back(pair_grad, [w[:, : 2 * size] for w in weights])
    return res, dn


def ffn_first(mine, other, dy, dyt, w0, w1, n, nt, res, dn, g0, g1):
    value = both_cores(mine, other)
    n[...] = value
    nt[...] = transposed(value)
    res[...], dn[...] = ffn_work(n, nt, dy, dyt, w0, w1, g0, g1)


def ffn_second(n, nt, dy, dyt, res_in, dn_in, w0, w1, res_out, dn_out, res_far, dn_far, g0, g1):
    res, dn = ffn_work(n, nt, dy, dyt, w0, w1, g0, g1)
    length = res_out.shape[0]
    for part, start, out, far in ((res, res_in, res_out, res_far), (dn, dn_in, dn_out, dn_far)):
        out[...] = inner(start[:length] + part[:length])
        far[...] = turn(inner(start[length:] + part[length:])).astype(BF16)


def ffn_end(second, res, dn, res_far, dn_far, dy, gains, w0, w1, w2, w3, result_out, grad_out, gain_out, branch_out, mixed_out):
    result_out[...] = (second[...] + (res[...] + res_far[...].astype(F32))).astype(BF16)
    back, gain_grad = norm_back(
        second[...], gains[2:3], dn[...] + dn_far[...].astype(F32)
    )
    grad = dy[...].astype(F32) + back
    grad_out[...] = grad
    gain_out[...] = gain_grad
    branch = grad.astype(BF16)
    branch_out[...] = branch
    mixed_out[...] = project(branch, [w[...] for w in (w0, w1, w2, w3)]).astype(BF16)


def attention_back(q, kt, vt, p, mixed_grad, span, g, head):
    lanes = slice(g * 2 * DH, (g + 1) * 2 * DH)
    kk = spread(kt)
    vv = spread(vt)
    queries = q[:, lanes]
    grad = mixed_grad[:, lanes]
    prob_grad = dot(grad, vv)
    probs = p[g]
    parts = []
    for h in range(2):
        one = probs[:, h * span : (h + 1) * span].astype(F32)
        change = prob_grad[:, h * span : (h + 1) * span]
        score = one * (change - jnp.sum(one * change, axis=1, keepdims=True))
        if head is not None:
            head(2 * g + h, score)
        parts.append(score.astype(BF16))
    score = jnp.concatenate(parts, axis=1)
    query_grad = (dot(score, kk, 1, 1) * 0.125).astype(BF16)
    key_grad = dot(queries, score, 0, 0)
    value_grad = dot(grad, probs, 0, 0)
    key_grad = key_grad[:DH, :span] + key_grad[DH:, span:]
    value_grad = value_grad[:DH, :span] + value_grad[DH:, span:]
    return query_grad, key_grad, value_grad


def cross_back(q, pair, p, mixed_grad, q_out, *pair_out):
    kv = pair.shape[0] // 2
    span = pair.shape[1]
    for g in range(kv // DH):
        mine = slice(g * DH, (g + 1) * DH)
        far = slice(kv + g * DH, kv + (g + 1) * DH)
        query_grad, key_grad, value_grad = attention_back(
            q, pair[mine], pair[far], p, mixed_grad, span, g, None
        )
        q_out[:, g * 2 * DH : (g + 1) * 2 * DH] = query_grad
        part = span // len(pair_out)
        for t, out in enumerate(pair_out):
            out[mine] = key_grad[:, t * part : (t + 1) * part].astype(BF16)
            out[far] = value_grad[:, t * part : (t + 1) * part].astype(BF16)


def cross_mid(q_grad, middle, grad, gains, w0, w1, w2, w3, s0, s1, s2, s3, grad_out, gain_out, branch_out, mixed_out):
    dn = project_back(q_grad[...], [w[...] for w in (w0, w1, w2, w3)])
    back, gain_grad = norm_back(middle[...], gains[1:2], dn)
    total = grad[...] + back
    grad_out[...] = total
    gain_out[...] = gain_grad
    low = total.astype(BF16)
    branch_out[...] = low
    mixed_out[...] = project(low, [s[...] for s in (s0, s1, s2, s3)]).astype(BF16)


def cross_grads(normed, q_grad, branch, mixed, low, self_mixed, g0, g1, g2, g3):
    width = mixed.shape[1]
    for p, g in enumerate((g0, g1, g2, g3)):
        g[:, :width] = dot(rows_of(normed, p), q_grad[...], 0, 0).astype(BF16)
        g[:, width : 2 * width] = dot(rows_of(branch, p), mixed[...], 0, 0).astype(BF16)
        g[:, 2 * width :] = dot(rows_of(low, p), self_mixed[...], 0, 0).astype(BF16)


def self_back(q, kt, vt, p, mixed_grad, buckets, out, table_out, lines):
    length = q.shape[0]
    width = q.shape[1]
    kv = kt.shape[0]

    def head(h, score):
        lines[h : h + 1] = diagonals(score)

    keys = []
    values = []
    for g in range(kv // DH):
        mine = slice(g * DH, (g + 1) * DH)
        query_grad, key_grad, value_grad = attention_back(
            q, kt[mine], vt[mine], p, mixed_grad, length, g, head
        )
        out[:, g * 2 * DH : (g + 1) * 2 * DH] = query_grad
        keys.append(key_grad)
        values.append(value_grad)
    out[:, width:] = jnp.concatenate(keys + values, axis=0).T.astype(BF16)
    table_out[...] = lax.dot_general(
        lines[...],
        line_of(buckets[...], table_out.shape[1]),
        (((1,), (1,)), ((), ())),
        precision=HIGHEST,
        preferred_element_type=F32,
    )


def restore(value, order):
    high = value.astype(BF16)
    low = (value - high.astype(F32)).astype(BF16)
    return dot(high, order, 1, 1) + dot(low, order, 1, 1)


def self_end(x, grad, grads, gains, order, cross_gain, ffn_gain, table, w0, w1, w2, w3, input_out, packed_out):
    dn = project_back(grads[...], [w[...] for w in (w0, w1, w2, w3)])
    back, gain_grad = norm_back(x[...].astype(F32), gains[0:1], dn)
    input_out[...] = restore(grad[...] + back, order[...])
    width = x.shape[1]
    found = jnp.concatenate([gain_grad, cross_gain[...], ffn_gain[...], jnp.zeros((5, width), F32)], axis=0)
    found = split_dot(found, order[...], 1)
    packed_out[...] = jnp.zeros_like(packed_out)
    lines = width // 128
    for i in range(3):
        for j in range(lines):
            packed_out[i * lines + j : i * lines + j + 1] = found[i : i + 1, j * 128 : (j + 1) * 128]
    packed_out[3 * lines :, : table.shape[1]] = table[...]


def self_grads(normed_t, grads, memory_t, *refs):
    size = normed_t.shape[0] // 4
    width = grads.shape[1]
    pair = jnp.concatenate([transposed(block[...]) for block in refs[:-4]], axis=0)
    for p, g in enumerate(refs[-4:]):
        mine = slice(p * size, (p + 1) * size)
        g[:, :width] = dot(normed_t[mine], grads[...]).astype(BF16)
        g[:, width:] = dot(memory_t[mine], pair).astype(BF16)


def memory_end(places, order, result, w0, w1, w2, w3, *refs):
    pair = jnp.concatenate([transposed(block[...]) for block in refs[:-2]], axis=0)
    out, result_out = refs[-2:]
    grad = restore(project_back(pair, [w[...] for w in (w0, w1, w2, w3)]), order[...])
    part = out.shape[1]
    for t in range(out.shape[0]):
        out[places[t]] = grad[t * part : (t + 1) * part]
    result_out[...] = dot(result[...], order[...], 1, 1).astype(BF16)


def idle(token, out):
    del token, out


def finish(held, came, token, out):
    out[...] = held[...] + came[...].astype(F32)


def shape(dims, kind):
    return jax.ShapeDtypeStruct(dims, kind)


def full(value):
    return pl.BlockSpec(value.shape, lambda i, rank=len(value.shape): (0,) * rank)


def columns(value, size, place):
    return pl.BlockSpec((value.shape[0], size), lambda i, place=place: (0, place))


SCALARS = pl.BlockSpec(memory_space=pltpu.SMEM)


def call(body, outs, args, specs=None, flops=0, scratch=(), room=12):
    specs = [full(a) if s is None else s for a, s in zip(args, specs or [None] * len(args))]
    moved = sum(int(np.prod(o.shape)) * o.dtype.itemsize for o in outs)
    moved += sum(int(np.prod(s.block_shape or a.shape)) * a.dtype.itemsize for a, s in zip(args, specs))
    return pl.pallas_call(
        body,
        grid=(1,),
        in_specs=specs,
        out_specs=[full(o) for o in outs],
        out_shape=outs,
        scratch_shapes=scratch,
        compiler_params=pltpu.CompilerParams(vmem_limit_bytes=min(2 * moved + room * MIB, 58 * MIB)),
        cost_estimate=pl.CostEstimate(
            flops=flops // EARLY, bytes_accessed=moved // EARLY, transcendentals=0
        ),
    )(*args)


def shards(
    nm,
    nd,
    block_input,
    memory,
    out_grad,
    decoder_segments,
    encoder_segments,
    distance_buckets,
    self_gain,
    cross_gain,
    ffn_gain,
    position_bias,
    self_query,
    self_key,
    self_value,
    self_out,
    cross_query,
    cross_key,
    cross_value,
    cross_out,
    ffn_gate,
    ffn_up,
    ffn_down,
):
    n = nm * nd
    length, width = block_input.shape[2:]
    span = encoder_segments.shape[2]
    keys = self_key.shape[1]
    rows = self_query.shape[0]
    heads = position_bias.shape[1]
    buckets = position_bias.shape[0]
    hidden = ffn_gate.shape[1]
    place = lax.axis_index("mem")
    me = place * nd + lax.axis_index("dp")

    half = hidden // 2
    first = (half // LANES + 1) // 2 * LANES
    last = half - first
    core = (me & 1).reshape(1)
    both = shape((rows, 2 * width + 2 * keys), BF16)
    shard_s, shard_c, shard_a, shard_b, far = call(
        functools.partial(pack, first),
        [both, both, shape((rows, 3 * first), BF16), shape((rows, 3 * last), BF16), shape((rows, 3 * half), BF16)],
        (core, self_query, self_key, self_value, self_out, cross_query, cross_key, cross_value, cross_out, ffn_gate, ffn_up, ffn_down),
        [SCALARS] + [None] * 11,
        room=58,
    )
    run = Order(jnp.full((8, 128), me, F32))
    gs = Gather(shard_s, n, run)
    gc = Gather(shard_c, n, run)
    gs.go()
    far = run.wait(lax.ppermute(run.tie(far), AXES, sibling(n)))
    ga = Gather(jnp.stack([shard_a, far[:, : 3 * first]]), n, run, False)
    gb = Gather(jnp.stack([shard_b, far[:, 3 * first :]]), n, run, False)

    src = source(n, me)
    feature = (src[:, None] * rows + lax.iota(jnp.int32, rows)[None, :]).reshape(1, width)
    places = place ^ lax.iota(jnp.int32, nm)
    stream = (length, width)
    turned = (width, length)
    gains = jnp.concatenate([jnp.stack([self_gain, cross_gain, ffn_gain]), jnp.zeros((5, width), F32)])
    x, dy, self_normed, self_normed_t, gains, order = call(
        arrange,
        [
            shape(stream, BF16),
            shape(stream, BF16),
            shape(stream, BF16),
            shape(turned, BF16),
            shape((8, width), F32),
            shape((width, width), BF16),
        ],
        (places, block_input.reshape(stream), out_grad.reshape(stream), feature, gains),
        [SCALARS, None, None, None, None],
    )
    part = span // nm
    local, local_t = call(
        arrange_memory,
        [shape((span, width), BF16), shape((width, span), BF16)],
        (places, memory.reshape(nm, part, width), order),
        [SCALARS, None, None],
    )
    seg_col = decoder_segments.reshape(length, 1)
    seg_row = decoder_segments.reshape(1, length)
    key_seg = encoder_segments.reshape(nm, part)
    key_seg = jnp.concatenate(
        [lax.dynamic_index_in_dim(key_seg, place ^ t, 0, keepdims=True) for t in range(nm)], axis=1
    )
    bucket_line = jnp.roll(distance_buckets[::-1], 1).reshape(1, length)

    kv = keys
    groups = kv // DH
    two = (2 * length, width)
    work = 2 * 2 * length * width * 9
    narrow = part % LANES != 0
    v = types.SimpleNamespace()

    def prepare():
        v.normed = run.wait(self_normed)
        v.dy_far = lax.ppermute(dy, AXES, sibling(n))

    def prepare_grad():
        v.dy_far = run.wait(v.dy_far)
        v.dy_two, v.dyt_two = call(
            pair_up, [shape(two, BF16), shape((width, 2 * length), BF16)], (dy, v.dy_far)
        )
        v.dyt_two = run.wait(v.dyt_two)

    def prepare_memory():
        v.local = run.wait(local)

    def self_part():
        v.q, v.kt, v.vt, v.p, v.mixed, v.middle, normed = call(
            self_forward,
            [
                shape(stream, BF16),
                shape((kv, length), BF16),
                shape((kv, length), BF16),
                shape((groups, length, 2 * length), BF16),
                shape(stream, BF16),
                shape(stream, F32),
                shape(stream, BF16),
            ],
            (x, run.tie(v.normed), position_bias.T, bucket_line, seg_col, seg_row, gains, *gs.pieces),
            flops=2 * length * width * 3 * width,
        )
        v.cross_normed = run.wait(normed)

    def memory_part():
        v.pair_spec = [columns(w, 2 * kv, 2 * width // (2 * kv)) for w in gc.pieces]
        (pair_t,) = call(
            memory_forward,
            [shape((2 * kv, span), BF16)],
            (run.tie(v.local), *gc.pieces),
            [None] + v.pair_spec,
            flops=2 * span * width * 2 * kv,
        )
        pair_t = run.wait(pair_t)
        v.blocks = swap_rows([pair_t[:, t * part : (t + 1) * part] for t in range(nm)], nm, nd)

    def memory_there():
        v.pair_t = jnp.concatenate([run.wait(block) for block in v.blocks], axis=1)

    def cross_part():
        v.cross_q, v.cross_p, v.cross_mixed, v.second, normed = call(
            cross_forward,
            [
                shape(stream, BF16),
                shape((groups, length, 2 * span), BF16),
                shape(stream, BF16),
                shape(stream, F32),
                shape(stream, BF16),
            ],
            (v.middle, run.tie(v.cross_normed), v.pair_t, seg_col, key_seg, gains, *gc.pieces),
            [None] * 6 + [columns(w, 2 * width, 0) for w in gc.pieces],
            flops=2 * length * width * 2 * width,
        )
        v.ffn_normed = run.wait(normed)
        v.normed_far = lax.ppermute(v.ffn_normed, AXES, sibling(n))

    def ffn_part():
        outs = [shape(two, BF16), shape((width, 2 * length), BF16), shape(two, F32), shape(two, F32)]
        v.n_two, v.nt_two, res, v.dn, *pieces = call(
            ffn_first,
            outs + [shape(w.shape, BF16) for w in ga.pieces],
            (v.ffn_normed, run.wait(v.normed_far), v.dy_two, v.dyt_two, *ga.pieces),
            flops=work * first,
        )
        v.ra = Scatter(pieces, n, run)
        v.res = run.wait(res)

    def ffn_rest():
        outs = [shape(stream, F32), shape(stream, F32), shape(stream, BF16), shape(stream, BF16)]
        v.res, v.dn, res_far, dn_far, *pieces = call(
            ffn_second,
            outs + [shape(w.shape, BF16) for w in gb.pieces],
            (v.n_two, v.nt_two, v.dy_two, v.dyt_two, run.tie(v.res), v.dn, *gb.pieces),
            flops=work * last,
        )
        v.rb = Scatter(pieces, n, run)
        dn_far = run.wait(dn_far)
        v.dn_far = lax.ppermute(dn_far, AXES, sibling(n))
        v.res_far = lax.ppermute(res_far, AXES, sibling(n))

    def ffn_back():
        v.dn_far = run.wait(v.dn_far)
        v.res_far = run.wait(v.res_far)
        v.result, v.grad, v.ffn_gain_grad, v.branch, v.mixed_grad = call(
            ffn_end,
            [
                shape(stream, BF16),
                shape(stream, F32),
                shape((1, width), F32),
                shape(stream, BF16),
                shape(stream, BF16),
            ],
            (v.second, v.res, v.dn, v.res_far, v.dn_far, dy, gains, *gc.pieces),
            [None] * 7 + [columns(w, width, 1) for w in gc.pieces],
            flops=2 * length * width * width,
        )

    def cross_back_part():
        outs = [shape((2 * kv, part), BF16)] * nm
        if narrow:
            outs = [shape((2 * kv, span), BF16)]
        q_grad, *blocks = call(
            cross_back,
            [shape(stream, BF16)] + outs,
            (v.cross_q, v.pair_t, v.cross_p, run.tie(v.mixed_grad)),
            flops=2 * length * span * width * 8,
        )
        v.cross_q_grad = run.wait(q_grad)
        if narrow:
            blocks = [blocks[0][:, t * part : (t + 1) * part] for t in range(nm)]
        v.parts = blocks

    def memory_back():
        v.sent = swap_rows([v.parts[0]] + [run.tie(b) for b in v.parts[1:]], nm, nd)

    def memory_back_there():
        v.there = [run.wait(block) for block in v.sent]

    def cross_mid_part():
        v.grad, v.cross_gain_grad, v.low, v.mixed_grad = call(
            cross_mid,
            [shape(stream, F32), shape((1, width), F32), shape(stream, BF16), shape(stream, BF16)],
            (run.tie(v.cross_q_grad), v.middle, v.grad, gains, *gc.pieces, *gs.pieces),
            [None] * 4 + [columns(w, width, 0) for w in gc.pieces] + [columns(w, width, 2) for w in gs.pieces],
            flops=2 * length * width * width * 2,
        )
        v.mixed_grad = run.wait(v.mixed_grad)

    def cross_grads_part():
        pieces = call(
            cross_grads,
            [shape((width // 4, 3 * width), BF16)] * 4,
            (v.cross_normed, run.tie(v.cross_q_grad), v.branch, v.cross_mixed, v.low, v.mixed),
            flops=2 * length * width * width * 3,
        )
        run.wait(pieces[0])
        v.rc = Scatter(pieces, n, run)
        v.rc.go()

    def self_back_part():
        v.grads, table = call(
            self_back,
            [shape((length, width + 2 * kv), BF16), shape((heads, buckets), F32)],
            (v.q, v.kt, v.vt, v.p, run.tie(v.mixed_grad), bucket_line),
            flops=2 * length * length * width * 8,
            scratch=[pltpu.VMEM((heads, length), F32)],
        )
        v.table = run.wait(table)

    def self_grads_part():
        pieces = call(
            self_grads,
            [shape((width // 4, width + 4 * kv), BF16)] * 4,
            (self_normed_t, run.tie(v.grads), local_t, *v.there),
            flops=2 * (length + span // 2) * width * 2 * width,
        )
        run.wait(pieces[0])
        v.rs = Scatter(pieces, n, run)
        v.rs.go()

    def self_end_part():
        v.input_grad, packed = call(
            self_end,
            [shape(stream, F32), shape((3 * width // 128 + heads, 128), F32)],
            (x, v.grad, run.tie(v.grads), gains, order, v.cross_gain_grad, v.ffn_gain_grad, v.table, *gs.pieces),
            [None] * 8 + [columns(w, width + 2 * kv, 0) for w in gs.pieces],
            flops=2 * length * width * 4 * width,
        )
        v.total = Total(run.wait(packed), n, run)
        v.total.send()

    def memory_end_part():
        memory_grad, v.result = call(
            memory_end,
            [shape((nm, part, width), F32), shape(stream, BF16)],
            (places, run.tie(order), v.result, *gc.pieces, *v.there),
            [SCALARS] + [None] * 2 + v.pair_spec + [None] * nm,
            flops=2 * span * width * 3 * width,
        )
        v.memory_grad = run.wait(memory_grad)

    def columns_back():
        v.far = jnp.concatenate([v.ra.done()[1], v.rb.done()[1]], axis=1)
        v.far = lax.ppermute(v.far, AXES, sibling(n))

    actions = {
        "p": lambda: run.pace(20),
        "s": gs.go,
        "c": gc.go,
        "a": ga.go,
        "b": gb.go,
        "x1": prepare,
        "x2": prepare_grad,
        "x3": prepare_memory,
        "K1": self_part,
        "K2": memory_part,
        "w2": memory_there,
        "K3": cross_part,
        "K4": ffn_part,
        "K5": ffn_rest,
        "K6": ffn_back,
        "K7": cross_back_part,
        "m7": memory_back,
        "w7": memory_back_there,
        "K8": cross_mid_part,
        "K9": self_back_part,
        "K10": self_grads_part,
        "K11": cross_grads_part,
        "K12": self_end_part,
        "K13": memory_end_part,
        "A": lambda: v.ra.go(),
        "B": lambda: v.rb.go(),
        "C": lambda: v.rc.go(),
        "S": lambda: v.rs.go(),
        "t": lambda: v.total.go(),
        "u": columns_back,
    }
    for name in PLAN:
        actions[name]()

    memory_grad, result, input_grad = v.memory_grad, v.result, v.input_grad
    done_a, done_b, done_c = (group.done() for group in (v.ra, v.rb, v.rc))
    (done_s,) = call(
        finish,
        [shape(v.rs.held.shape, F32)],
        (v.rs.held, v.rs.came, run.token),
        [None, None, pl.BlockSpec(memory_space=pl.ANY)],
    )
    whole = shape((rows, hidden), F32)
    gate_done, up_done, down_done = call(
        functools.partial(unpack, first),
        [whole, whole, whole],
        (core, done_a[0], done_b[0], v.far),
        [SCALARS] + [None] * 3,
    )

    gain_lines = 3 * width // 128
    packed = v.total.value
    gain_grads = packed[:gain_lines].reshape(3, width)
    table = packed[gain_lines:, :buckets].T

    return (
        result.reshape(block_input.shape),
        input_grad.reshape(block_input.shape),
        memory_grad.reshape(memory.shape),
        gain_grads[0],
        gain_grads[1],
        gain_grads[2],
        table,
        done_s[:, :width],
        done_s[:, width : width + kv],
        done_s[:, width + kv : width + 2 * kv],
        done_c[:, 2 * width :],
        done_c[:, :width],
        done_s[:, width + 2 * kv : width + 3 * kv],
        done_s[:, width + 3 * kv :],
        done_c[:, width : 2 * width],
        gate_done,
        up_done,
        down_done,
    )


def solution(mesh):
    stream = P("dp", "mem", None, None)
    segments = P("dp", "mem", None)
    shard = P(AXES, None)
    in_specs = (stream, P("dp", None, "mem", None), stream, segments, segments) + (P(),) * 5 + (shard,) * 11
    out_specs = (stream, stream, P("dp", None, "mem", None)) + (P(),) * 4 + (shard,) * 11
    body = functools.partial(shards, mesh.shape["mem"], mesh.shape["dp"])
    return jax.shard_map(body, mesh=mesh, in_specs=in_specs, out_specs=out_specs, check_vma=False)
```

```python
import functools
import types

import jax
import jax.numpy as jnp
import numpy as np
from jax import lax
from jax.experimental import pallas as pl
from jax.experimental.pallas import tpu as pltpu
from jax.sharding import PartitionSpec as P

DH = 64
LANES = 128
EPSILON = 1e-06
NEGATIVE = -1e30
AXES = ("mem", "dp")
F32 = jnp.float32
BF16 = jnp.bfloat16
HIGHEST = lax.Precision.HIGHEST
MIB = 1024 * 1024


PLAN = " ".join((
    "s x1 s c",
    "x2 c s x3",
    "c a a p",
    "s p c s",
    "K1 c a b",
    "b a c K2",
    "b a w2 b",
    "K3 K4 b A",
    "K5 B K6 K7",
    "A m7 K8 K9",
    "B A w7 K10",
    "K11 S C K12",
    "A B K13 t",
    "S t C A",
    "B t S t",
    "C S C B",
    "u t S C",
)).split()


def steps(n):
    high = list(range(n.bit_length() - 2, 2, -1))
    return (high + [2, 1], high + [1, 2])


def exchange(n, k):
    order = steps(n)
    return [(d, d ^ (1 << order[d & 1][k])) for d in range(n)]


def sibling(n):
    return [(d, d ^ 1) for d in range(n)]


def source(n, me):
    order = steps(n)
    half = n // 2
    table = np.zeros((2, half), np.int32)
    for core in range(2):
        for slot in range(half):
            for k in range(len(order[core])):
                if slot >> k & 1:
                    table[core, slot] ^= 1 << order[core][k]
    odd = (me & 1) == 1
    own = jnp.where(odd, table[1], table[0])
    other = jnp.where(odd, table[0], table[1])
    return jnp.concatenate([me ^ own, me ^ 1 ^ other])


class Order:
    def __init__(self, token):
        self.token = token

    def tie(self, value):
        value, self.token = lax.optimization_barrier((value, self.token))
        return value

    wait = tie

    def pace(self, micros):
        spec = pl.BlockSpec(memory_space=pl.ANY)
        self.token = pl.pallas_call(
            idle,
            in_specs=[spec],
            out_specs=spec,
            out_shape=shape(self.token.shape, self.token.dtype),
            input_output_aliases={0: 0},
            cost_estimate=pl.CostEstimate(
                flops=micros * 1000 * 1000 * 1000, bytes_accessed=0, transcendentals=0
            ),
        )(self.token)


class Gather:
    def __init__(self, shard, n, order, twin=True):
        self.n = n
        self.order = order
        self.held = shard
        self.last = n.bit_length() - 3
        self.k = 0
        self.flying = None
        self.twin = twin
        self.pieces = None

    def send(self):
        self.flying = lax.ppermute(self.held, AXES, exchange(self.n, self.k))

    def grow(self):
        came = self.order.wait(self.flying)
        self.held = jnp.concatenate([self.held, came], axis=self.held.ndim - 2)
        self.k += 1

    def go(self):
        if self.flying is None:
            self.held = self.order.tie(self.held)
            self.send()
        elif self.pieces is not None:
            self.pieces = self.pieces + [self.order.wait(p) for p in self.flying]
        elif self.k == self.last:
            self.pieces = [self.held, self.order.wait(self.flying)]
            if self.twin:
                self.flying = [lax.ppermute(p, AXES, sibling(self.n)) for p in self.pieces]
        else:
            if self.k == 0:
                for _ in range(self.n.bit_length() - 6):
                    self.grow()
                    self.send()
            self.grow()
            self.send()


class Scatter:
    def __init__(self, pieces, n, order):
        self.n = n
        self.order = order
        self.pieces = pieces
        self.k = n.bit_length() - 3
        self.flying = None
        self.both = len(pieces) == 4
        if not self.both:
            self.held = pieces[0]
            self.low = pieces[1]

    def send(self):
        self.flying = lax.ppermute(self.low, AXES, exchange(self.n, self.k))

    def shrink(self):
        came = self.order.wait(self.flying)
        self.k -= 1
        self.low, self.held = absorb(self.held, came)

    def go(self):
        if self.flying is None and self.both:
            self.flying = [lax.ppermute(p, AXES, sibling(self.n)) for p in self.pieces[2:]]
        elif self.both:
            there = [self.order.wait(p) for p in self.flying]
            self.low, self.held = absorb_twin(*self.pieces[:2], *there)
            self.both = False
            self.send()
        elif self.flying is None:
            self.send()
        elif self.k == 0:
            self.came = self.order.wait(self.flying)
        else:
            extra = self.n.bit_length() - 6
            if self.k == extra + 1:
                for _ in range(extra):
                    self.shrink()
                    self.send()
            self.shrink()
            self.send()

    def done(self):
        return self.held + self.came.astype(F32)


def absorb_step(held, came, low_out, held_out):
    half = low_out.shape[-2]
    low_out[...] = (held[..., half:, :].astype(F32) + came[..., half:, :].astype(F32)).astype(BF16)
    held_out[...] = held[..., :half, :].astype(F32) + came[..., :half, :].astype(F32)


def absorb_twin_step(held, low, held_came, low_came, low_out, held_out):
    low_out[...] = (low[...].astype(F32) + low_came[...].astype(F32)).astype(BF16)
    held_out[...] = held[...].astype(F32) + held_came[...].astype(F32)


def by_columns(body, args, dims):
    size = dims[-1]
    tiles = 3 if size % (3 * LANES) == 0 and dims[-2] >= 64 else 1

    def spec(whole):
        block = tuple(whole[:-1]) + (size // tiles,)
        return pl.BlockSpec(block, lambda j, rank=len(whole): (0,) * (rank - 1) + (j,))

    return pl.pallas_call(
        body,
        grid=(tiles,),
        in_specs=[spec(a.shape) for a in args],
        out_specs=[spec(dims), spec(dims)],
        out_shape=[shape(dims, BF16), shape(dims, F32)],
        compiler_params=pltpu.CompilerParams(vmem_limit_bytes=20 * MIB),
        cost_estimate=pl.CostEstimate(
            flops=2 * args[0].size, bytes_accessed=10 * args[0].size, transcendentals=0
        ),
    )(*args)


def absorb(held, came):
    dims = held.shape[:-2] + (held.shape[-2] // 2, held.shape[-1])
    return by_columns(absorb_step, (held, came), dims)


def absorb_twin(held, low, held_came, low_came):
    return by_columns(absorb_twin_step, (held, low, held_came, low_came), held.shape)


class Total:
    def __init__(self, value, n, order):
        self.value = value
        self.n = n
        self.order = order
        self.bit = 0

    def send(self):
        pairs = [(d, d ^ (1 << self.bit)) for d in range(self.n)]
        self.flying = lax.ppermute(self.value, AXES, pairs)

    def take(self):
        self.value = self.value + self.order.wait(self.flying)
        self.bit += 1

    def go(self):
        if self.bit == 4:
            for _ in range(self.n.bit_length() - 6):
                self.take()
                self.send()
        self.take()
        if self.bit < self.n.bit_length() - 1:
            self.send()


def swap_rows(blocks, nm, nd):
    n = nm * nd
    return [blocks[0]] + [
        lax.ppermute(blocks[t], AXES, [(d, d ^ (t * nd)) for d in range(n)]) for t in range(1, nm)
    ]


def dot(left, right, a=1, b=0):
    return lax.dot_general(left, right, (((a,), (b,)), ((), ())), preferred_element_type=F32)


def rows_of(left, p):
    size = left.shape[1] // 4
    return left[:, p * size : (p + 1) * size]


def project(left, weights):
    total = dot(rows_of(left, 0), weights[0])
    for p in range(1, 4):
        total = total + dot(rows_of(left, p), weights[p])
    return total


def project_back(left, weights):
    return jnp.concatenate([dot(left, w, 1, 1) for w in weights], axis=1)


def scale_of(stream):
    return lax.rsqrt(jnp.mean(stream * stream, axis=1, keepdims=True) + EPSILON)


def norm_back(stream, gain, grad):
    scale = scale_of(stream)
    weighted = grad * gain
    inner = jnp.mean(weighted * stream, axis=1, keepdims=True)
    out = scale * weighted - stream * (scale * scale * scale) * inner
    return out, jnp.sum(grad * stream * scale, axis=0, keepdims=True)


def transposed(value):
    return value.astype(F32).T.astype(BF16)


def spread(part):
    zero = jnp.zeros_like(part)
    top = jnp.concatenate([part, zero], axis=1)
    low = jnp.concatenate([zero, part], axis=1)
    return jnp.concatenate([top, low], axis=0)


def softmax(scores):
    expo = jnp.exp(scores - jnp.max(scores, axis=1, keepdims=True))
    return (expo / jnp.sum(expo, axis=1, keepdims=True)).astype(BF16)


def line_of(buckets, count):
    rows = lax.broadcasted_iota(jnp.int32, (count, buckets.shape[1]), 0)
    return (rows == buckets).astype(F32)


def pick(value, row):
    return lax.broadcasted_iota(jnp.int32, value.shape, 0) == row


def toeplitz(line):
    first = jnp.broadcast_to(line, (8, line.shape[1]))
    block = first
    for i in range(1, 8):
        block = jnp.where(pick(block, i), pltpu.roll(first, i, 1), block)
    size = 8
    while size < line.shape[1]:
        block = jnp.concatenate([block, pltpu.roll(block, size, 1)], axis=0)
        size *= 2
    return block


def diagonals(block):
    size = block.shape[0]
    while size > 8:
        size //= 2
        block = block[:size] + pltpu.roll(block[size:], block.shape[1] - size, 1)
    total = block
    for i in range(1, 8):
        total = jnp.where(pick(block, i), pltpu.roll(block, block.shape[1] - i, 1), total)
    return jnp.sum(total, axis=0, keepdims=True)


def split_dot(value, order, b):
    total = None
    for _ in range(3):
        high = value.astype(BF16)
        part = dot(high, order, 1, b)
        total = part if total is None else total + part
        value = value - high.astype(F32)
    return total


def pack(first, core, sq, sk, sv, so, cq, ck, cv, co, fg, fu, fd, self_out, cross_out, a_out, b_out, far_out):
    for out, parts in ((self_out, (sq, sk, sv, so)), (cross_out, (cq, co, ck, cv))):
        at = 0
        for part in parts:
            size = part.shape[1]
            out[:, at : at + size] = part[...]
            at += size
    odd = core[0] == 1
    half = fg.shape[1] // 2
    last = half - first
    for i, part in enumerate((fg, fu, fd)):
        low = part[:, :half].astype(F32)
        high = part[:, half:].astype(F32)
        mine = jnp.where(odd, high, low).astype(BF16)
        far = jnp.where(odd, low, high).astype(BF16)
        a_out[:, i * first : (i + 1) * first] = mine[:, :first]
        b_out[:, i * last : (i + 1) * last] = mine[:, first:]
        far_out[:, i * first : (i + 1) * first] = far[:, :first]
        far_out[:, 3 * first + i * last : 3 * first + (i + 1) * last] = far[:, first:]


def unpack(first, core, a, b, far, g_out, u_out, d_out):
    odd = core[0] == 1
    half = g_out.shape[1] // 2
    last = half - first
    for i, out in enumerate((g_out, u_out, d_out)):
        mine = jnp.concatenate(
            [a[:, i * first : (i + 1) * first], b[:, i * last : (i + 1) * last]], axis=1
        )
        other = jnp.concatenate(
            [
                far[:, i * first : (i + 1) * first],
                far[:, 3 * first + i * last : 3 * first + (i + 1) * last],
            ],
            axis=1,
        )
        out[:, :half] = jnp.where(odd, other, mine)
        out[:, half:] = jnp.where(odd, mine, other)


def turn(value):
    half = value.shape[1] // 2
    return jnp.concatenate([value[:, half:], value[:, :half]], axis=1)


def inner(value):
    b = value.shape[1] // 8
    return jnp.concatenate(
        [value[:, : 5 * b], value[:, 6 * b : 7 * b], value[:, 5 * b : 6 * b], value[:, 7 * b :]],
        axis=1,
    )


def both_cores(mine, other):
    return jnp.concatenate([inner(mine[...]), inner(turn(other[...]))], axis=0)


def pair_up(mine, other, out, out_t):
    value = both_cores(mine, other)
    out[...] = value
    out_t[...] = transposed(value)


def arrange(places, x_in, dy_in, feature, gains_in, x_out, dy_out, n_out, nt_out, gains_out, order_out):
    width = feature.shape[1]
    rows = lax.broadcasted_iota(jnp.int32, (width, width), 0)
    order = (rows == feature[...]).astype(F32).astype(BF16)
    order_out[...] = order
    gains = split_dot(gains_in[...], order, 0)
    gains_out[...] = gains
    x = dot(x_in[...], order)
    x_out[...] = x.astype(BF16)
    n = x * scale_of(x) * gains[0:1]
    n_out[...] = n.astype(BF16)
    nt_out[...] = n.T.astype(BF16)
    dy_out[...] = dot(dy_in[...], order).astype(BF16)


def arrange_memory(places, memory, order, out, out_t):
    part = memory.shape[1]
    for t in range(memory.shape[0]):
        block = dot(memory[places[t]], order[...])
        out[t * part : (t + 1) * part] = block.astype(BF16)
    out_t[...] = out[...].astype(F32).T.astype(BF16)


def self_forward(x, normed, bias, buckets, seg_col, seg_row, gains, w0, w1, w2, w3,
                 q_out, kt_out, vt_out, p_out, mixed_out, middle_out, n_out):
    weights = (w0, w1, w2, w3)
    width = x.shape[1]
    keys = w0.shape[1] - 2 * width
    kv = keys // 2
    length = x.shape[0]
    n = normed[...]
    q_out[...] = (project(n, [w[:, :width] for w in weights]).astype(BF16).astype(F32) * 0.125).astype(BF16)
    pair = project(n, [w[:, width : width + keys] for w in weights])
    pair_t = pair.T.astype(BF16)
    kt_out[...] = pair_t[:kv]
    vt_out[...] = pair_t[kv:]
    row = lax.broadcasted_iota(jnp.int32, (length, length), 0)
    column = lax.broadcasted_iota(jnp.int32, (length, length), 1)
    allowed = (column <= row) & (seg_col[...] == seg_row[...])
    lines = jnp.dot(bias[...], line_of(buckets[...], bias.shape[1]), precision=HIGHEST)
    for g in range(kv // DH):
        kk = spread(kt_out[g * DH : (g + 1) * DH])
        vv = spread(vt_out[g * DH : (g + 1) * DH])
        scores = dot(q_out[:, g * 2 * DH : (g + 1) * 2 * DH], kk)
        for h in range(2):
            part = scores[:, h * length : (h + 1) * length] + toeplitz(lines[2 * g + h : 2 * g + h + 1])
            p_out[g, :, h * length : (h + 1) * length] = softmax(jnp.where(allowed, part, NEGATIVE))
        mixed_out[:, g * 2 * DH : (g + 1) * 2 * DH] = dot(p_out[g], vv, 1, 1).astype(BF16)
    middle = x[...].astype(F32) + project_back(mixed_out[...], [w[:, width + keys :] for w in weights])
    middle_out[...] = middle
    n_out[...] = (middle * scale_of(middle) * gains[1:2]).astype(BF16)


def memory_forward(memory, w0, w1, w2, w3, pair_out):
    pair = project(memory[...], [w[...] for w in (w0, w1, w2, w3)])
    pair_out[...] = pair.T.astype(BF16)


def cross_forward(middle, normed, pair, seg_col, seg_row, gains, w0, w1, w2, w3,
                  q_out, p_out, mixed_out, second_out, n_out):
    weights = (w0, w1, w2, w3)
    width = middle.shape[1]
    kv = pair.shape[0] // 2
    span = pair.shape[1]
    q = project(normed[...], [w[:, :width] for w in weights])
    q_out[...] = (q.astype(BF16).astype(F32) * 0.125).astype(BF16)
    allowed = seg_col[...] == seg_row[...]
    for g in range(kv // DH):
        kk = spread(pair[g * DH : (g + 1) * DH])
        vv = spread(pair[kv + g * DH : kv + (g + 1) * DH])
        scores = dot(q_out[:, g * 2 * DH : (g + 1) * 2 * DH], kk)
        for h in range(2):
            part = scores[:, h * span : (h + 1) * span]
            p_out[g, :, h * span : (h + 1) * span] = softmax(jnp.where(allowed, part, NEGATIVE))
        mixed_out[:, g * 2 * DH : (g + 1) * 2 * DH] = dot(p_out[g], vv, 1, 1).astype(BF16)
    second = middle[...] + project_back(mixed_out[...], [w[:, width:] for w in weights])
    second_out[...] = second
    n_out[...] = (second * scale_of(second) * gains[2:3]).astype(BF16)


def ffn_work(n, nt, dy, dyt, w0, w1, g0, g1):
    weights = [w0[0], w1[0], w0[1], w1[1]]
    size = w0.shape[2] // 3
    pair = project(n[...], [w[:, : 2 * size] for w in weights])
    gate = pair[:, :size]
    lifted = pair[:, size:]
    hidden_grad = project(dy[...], [w[:, 2 * size :] for w in weights])
    root = 0.7978845608028654
    square = gate * gate
    tanh = jnp.tanh(root * gate * (1.0 + 0.044715 * square))
    half = 0.5 * (1.0 + tanh)
    gelu = gate * half
    slope = half + 0.5 * gate * (1.0 - tanh * tanh) * (root * (1.0 + 3.0 * 0.044715 * square))
    hidden = (gelu * lifted).astype(BF16)
    pair_grad = jnp.concatenate(
        [(hidden_grad * lifted * slope).astype(BF16), (hidden_grad * gelu).astype(BF16)], axis=1
    )
    rows = nt.shape[0] // 4
    for p in range(4):
        g = (g0, g1)[p % 2]
        mine = slice(p * rows, (p + 1) * rows)
        g[p // 2, :, : 2 * size] = dot(nt[mine], pair_grad).astype(BF16)
        g[p // 2, :, 2 * size :] = dot(dyt[mine], hidden).astype(BF16)
    res = project_back(hidden, [w[:, 2 * size :] for w in weights])
    dn = project_back(pair_grad, [w[:, : 2 * size] for w in weights])
    return res, dn


def ffn_first(mine, other, dy, dyt, w0, w1, n, nt, res, dn, g0, g1):
    value = both_cores(mine, other)
    n[...] = value
    nt[...] = transposed(value)
    res[...], dn[...] = ffn_work(n, nt, dy, dyt, w0, w1, g0, g1)


def ffn_second(n, nt, dy, dyt, res_in, dn_in, w0, w1, res_out, dn_out, far_out, g0, g1):
    res, dn = ffn_work(n, nt, dy, dyt, w0, w1, g0, g1)
    length = res_out.shape[0]
    width = res_out.shape[1]
    for i, (part, start, out) in enumerate(((res, res_in, res_out), (dn, dn_in, dn_out))):
        out[...] = inner(start[:length] + part[:length])
        far = turn(inner(start[length:] + part[length:]))
        far_out[:, i * width : (i + 1) * width] = far.astype(BF16)


def ffn_end(second, res, dn, far, dy, gains, w0, w1, w2, w3, result_out, grad_out, gain_out, branch_out, mixed_out):
    width = second.shape[1]
    result_out[...] = (second[...] + (res[...] + far[:, :width].astype(F32))).astype(BF16)
    back, gain_grad = norm_back(
        second[...], gains[2:3], dn[...] + far[:, width:].astype(F32)
    )
    grad = dy[...].astype(F32) + back
    grad_out[...] = grad
    gain_out[...] = gain_grad
    branch = grad.astype(BF16)
    branch_out[...] = branch
    mixed_out[...] = project(branch, [w[...] for w in (w0, w1, w2, w3)]).astype(BF16)


def attention_back(q, kt, vt, p, mixed_grad, span, g, head):
    lanes = slice(g * 2 * DH, (g + 1) * 2 * DH)
    kk = spread(kt)
    vv = spread(vt)
    queries = q[:, lanes]
    grad = mixed_grad[:, lanes]
    prob_grad = dot(grad, vv)
    probs = p[g]
    parts = []
    for h in range(2):
        one = probs[:, h * span : (h + 1) * span].astype(F32)
        change = prob_grad[:, h * span : (h + 1) * span]
        score = one * (change - jnp.sum(one * change, axis=1, keepdims=True))
        if head is not None:
            head(2 * g + h, score)
        parts.append(score.astype(BF16))
    score = jnp.concatenate(parts, axis=1)
    query_grad = (dot(score, kk, 1, 1) * 0.125).astype(BF16)
    key_grad = dot(queries, score, 0, 0)
    value_grad = dot(grad, probs, 0, 0)
    key_grad = key_grad[:DH, :span] + key_grad[DH:, span:]
    value_grad = value_grad[:DH, :span] + value_grad[DH:, span:]
    return query_grad, key_grad, value_grad


def cross_back(q, pair, p, mixed_grad, q_out, *pair_out):
    kv = pair.shape[0] // 2
    span = pair.shape[1]
    for g in range(kv // DH):
        mine = slice(g * DH, (g + 1) * DH)
        far = slice(kv + g * DH, kv + (g + 1) * DH)
        query_grad, key_grad, value_grad = attention_back(
            q, pair[mine], pair[far], p, mixed_grad, span, g, None
        )
        q_out[:, g * 2 * DH : (g + 1) * 2 * DH] = query_grad
        part = span // len(pair_out)
        for t, out in enumerate(pair_out):
            out[mine] = key_grad[:, t * part : (t + 1) * part].astype(BF16)
            out[far] = value_grad[:, t * part : (t + 1) * part].astype(BF16)


def cross_mid(q_grad, middle, grad, gains, w0, w1, w2, w3, s0, s1, s2, s3, grad_out, gain_out, branch_out, mixed_out):
    dn = project_back(q_grad[...], [w[...] for w in (w0, w1, w2, w3)])
    back, gain_grad = norm_back(middle[...], gains[1:2], dn)
    total = grad[...] + back
    grad_out[...] = total
    gain_out[...] = gain_grad
    low = total.astype(BF16)
    branch_out[...] = low
    mixed_out[...] = project(low, [s[...] for s in (s0, s1, s2, s3)]).astype(BF16)


def cross_grads(normed, q_grad, branch, mixed, low, self_mixed, g0, g1, g2, g3):
    width = mixed.shape[1]
    for p, g in enumerate((g0, g1, g2, g3)):
        g[:, :width] = dot(rows_of(normed, p), q_grad[...], 0, 0).astype(BF16)
        g[:, width : 2 * width] = dot(rows_of(branch, p), mixed[...], 0, 0).astype(BF16)
        g[:, 2 * width :] = dot(rows_of(low, p), self_mixed[...], 0, 0).astype(BF16)


def self_back(q, kt, vt, p, mixed_grad, buckets, out, table_out, lines):
    length = q.shape[0]
    width = q.shape[1]
    kv = kt.shape[0]

    def head(h, score):
        lines[h : h + 1] = diagonals(score)

    keys = []
    values = []
    for g in range(kv // DH):
        mine = slice(g * DH, (g + 1) * DH)
        query_grad, key_grad, value_grad = attention_back(
            q, kt[mine], vt[mine], p, mixed_grad, length, g, head
        )
        out[:, g * 2 * DH : (g + 1) * 2 * DH] = query_grad
        keys.append(key_grad)
        values.append(value_grad)
    out[:, width:] = jnp.concatenate(keys + values, axis=0).T.astype(BF16)
    table_out[...] = lax.dot_general(
        lines[...],
        line_of(buckets[...], table_out.shape[1]),
        (((1,), (1,)), ((), ())),
        precision=HIGHEST,
        preferred_element_type=F32,
    )


def restore(value, order):
    high = value.astype(BF16)
    low = (value - high.astype(F32)).astype(BF16)
    return dot(high, order, 1, 1) + dot(low, order, 1, 1)


def self_end(x, grad, grads, gains, order, cross_gain, ffn_gain, table, w0, w1, w2, w3, input_out, packed_out):
    dn = project_back(grads[...], [w[...] for w in (w0, w1, w2, w3)])
    back, gain_grad = norm_back(x[...].astype(F32), gains[0:1], dn)
    input_out[...] = restore(grad[...] + back, order[...])
    width = x.shape[1]
    found = jnp.concatenate([gain_grad, cross_gain[...], ffn_gain[...], jnp.zeros((5, width), F32)], axis=0)
    found = split_dot(found, order[...], 1)
    packed_out[...] = jnp.zeros_like(packed_out)
    lines = width // 128
    for i in range(3):
        for j in range(lines):
            packed_out[i * lines + j : i * lines + j + 1] = found[i : i + 1, j * 128 : (j + 1) * 128]
    packed_out[3 * lines :, : table.shape[1]] = table[...]


def self_grads(normed_t, grads, memory_t, *refs):
    size = normed_t.shape[0] // 4
    width = grads.shape[1]
    pair = jnp.concatenate([transposed(block[...]) for block in refs[:-4]], axis=0)
    for p, g in enumerate(refs[-4:]):
        mine = slice(p * size, (p + 1) * size)
        g[:, :width] = dot(normed_t[mine], grads[...]).astype(BF16)
        g[:, width:] = dot(memory_t[mine], pair).astype(BF16)


def memory_end(places, order, result, w0, w1, w2, w3, *refs):
    pair = jnp.concatenate([transposed(block[...]) for block in refs[:-2]], axis=0)
    out, result_out = refs[-2:]
    grad = restore(project_back(pair, [w[...] for w in (w0, w1, w2, w3)]), order[...])
    part = out.shape[1]
    for t in range(out.shape[0]):
        out[places[t]] = grad[t * part : (t + 1) * part]
    result_out[...] = dot(result[...], order[...], 1, 1).astype(BF16)


def idle(token, out):
    del token, out


def finish(held, came, token, out):
    out[...] = held[...] + came[...].astype(F32)


def shape(dims, kind):
    return jax.ShapeDtypeStruct(dims, kind)


def full(value):
    return pl.BlockSpec(value.shape, lambda i, rank=len(value.shape): (0,) * rank)


def columns(value, size, place):
    return pl.BlockSpec((value.shape[0], size), lambda i, place=place: (0, place))


SCALARS = pl.BlockSpec(memory_space=pltpu.SMEM)


def call(body, outs, args, specs=None, flops=0, scratch=(), room=12):
    specs = [full(a) if s is None else s for a, s in zip(args, specs or [None] * len(args))]
    moved = sum(int(np.prod(o.shape)) * o.dtype.itemsize for o in outs)
    moved += sum(int(np.prod(s.block_shape or a.shape)) * a.dtype.itemsize for a, s in zip(args, specs))
    return pl.pallas_call(
        body,
        grid=(1,),
        in_specs=specs,
        out_specs=[full(o) for o in outs],
        out_shape=outs,
        scratch_shapes=scratch,
        compiler_params=pltpu.CompilerParams(vmem_limit_bytes=min(2 * moved + room * MIB, 58 * MIB)),
        cost_estimate=pl.CostEstimate(flops=flops, bytes_accessed=moved, transcendentals=0),
    )(*args)


def shards(
    nm,
    nd,
    block_input,
    memory,
    out_grad,
    decoder_segments,
    encoder_segments,
    distance_buckets,
    self_gain,
    cross_gain,
    ffn_gain,
    position_bias,
    self_query,
    self_key,
    self_value,
    self_out,
    cross_query,
    cross_key,
    cross_value,
    cross_out,
    ffn_gate,
    ffn_up,
    ffn_down,
):
    n = nm * nd
    length, width = block_input.shape[2:]
    span = encoder_segments.shape[2]
    keys = self_key.shape[1]
    rows = self_query.shape[0]
    heads = position_bias.shape[1]
    buckets = position_bias.shape[0]
    hidden = ffn_gate.shape[1]
    place = lax.axis_index("mem")
    me = place * nd + lax.axis_index("dp")

    half = hidden // 2
    first = (half // LANES + 1) // 2 * LANES
    last = half - first
    core = (me & 1).reshape(1)
    both = shape((rows, 2 * width + 2 * keys), BF16)
    shard_s, shard_c, shard_a, shard_b, far = call(
        functools.partial(pack, first),
        [both, both, shape((rows, 3 * first), BF16), shape((rows, 3 * last), BF16), shape((rows, 3 * half), BF16)],
        (core, self_query, self_key, self_value, self_out, cross_query, cross_key, cross_value, cross_out, ffn_gate, ffn_up, ffn_down),
        [SCALARS] + [None] * 11,
        room=58,
    )
    run = Order(jnp.full((8, 128), me, F32))
    gs = Gather(shard_s, n, run)
    gc = Gather(shard_c, n, run)
    gs.go()
    far = run.wait(lax.ppermute(run.tie(far), AXES, sibling(n)))
    ga = Gather(jnp.stack([shard_a, far[:, : 3 * first]]), n, run, False)
    gb = Gather(jnp.stack([shard_b, far[:, 3 * first :]]), n, run, False)

    src = source(n, me)
    feature = (src[:, None] * rows + lax.iota(jnp.int32, rows)[None, :]).reshape(1, width)
    places = place ^ lax.iota(jnp.int32, nm)
    stream = (length, width)
    turned = (width, length)
    gains = jnp.concatenate([jnp.stack([self_gain, cross_gain, ffn_gain]), jnp.zeros((5, width), F32)])
    x, dy, self_normed, self_normed_t, gains, order = call(
        arrange,
        [
            shape(stream, BF16),
            shape(stream, BF16),
            shape(stream, BF16),
            shape(turned, BF16),
            shape((8, width), F32),
            shape((width, width), BF16),
        ],
        (places, block_input.reshape(stream), out_grad.reshape(stream), feature, gains),
        [SCALARS, None, None, None, None],
    )
    part = span // nm
    local, local_t = call(
        arrange_memory,
        [shape((span, width), BF16), shape((width, span), BF16)],
        (places, memory.reshape(nm, part, width), order),
        [SCALARS, None, None],
    )
    seg_col = decoder_segments.reshape(length, 1)
    seg_row = decoder_segments.reshape(1, length)
    key_seg = encoder_segments.reshape(nm, part)
    key_seg = jnp.concatenate(
        [lax.dynamic_index_in_dim(key_seg, place ^ t, 0, keepdims=True) for t in range(nm)], axis=1
    )
    bucket_line = jnp.roll(distance_buckets[::-1], 1).reshape(1, length)

    kv = keys
    groups = kv // DH
    two = (2 * length, width)
    work = 2 * 2 * length * width * 9
    narrow = part % LANES != 0
    v = types.SimpleNamespace()

    def prepare():
        v.normed = run.wait(self_normed)
        v.dy_far = lax.ppermute(dy, AXES, sibling(n))

    def prepare_grad():
        v.dy_far = run.wait(v.dy_far)
        v.dy_two, v.dyt_two = call(
            pair_up, [shape(two, BF16), shape((width, 2 * length), BF16)], (dy, v.dy_far)
        )
        v.dyt_two = run.wait(v.dyt_two)

    def prepare_memory():
        v.local = run.wait(local)

    def self_part():
        v.q, v.kt, v.vt, v.p, v.mixed, v.middle, normed = call(
            self_forward,
            [
                shape(stream, BF16),
                shape((kv, length), BF16),
                shape((kv, length), BF16),
                shape((groups, length, 2 * length), BF16),
                shape(stream, BF16),
                shape(stream, F32),
                shape(stream, BF16),
            ],
            (x, run.tie(v.normed), position_bias.T, bucket_line, seg_col, seg_row, gains, *gs.pieces),
            flops=2 * length * width * 3 * width,
        )
        v.cross_normed = run.wait(normed)

    def memory_part():
        v.pair_spec = [columns(w, 2 * kv, 2 * width // (2 * kv)) for w in gc.pieces]
        (pair_t,) = call(
            memory_forward,
            [shape((2 * kv, span), BF16)],
            (run.tie(v.local), *gc.pieces),
            [None] + v.pair_spec,
            flops=2 * span * width * 2 * kv,
        )
        pair_t = run.wait(pair_t)
        v.blocks = swap_rows([pair_t[:, t * part : (t + 1) * part] for t in range(nm)], nm, nd)

    def memory_there():
        v.pair_t = jnp.concatenate([run.wait(block) for block in v.blocks], axis=1)

    def cross_part():
        v.cross_q, v.cross_p, v.cross_mixed, v.second, normed = call(
            cross_forward,
            [
                shape(stream, BF16),
                shape((groups, length, 2 * span), BF16),
                shape(stream, BF16),
                shape(stream, F32),
                shape(stream, BF16),
            ],
            (v.middle, run.tie(v.cross_normed), v.pair_t, seg_col, key_seg, gains, *gc.pieces),
            [None] * 6 + [columns(w, 2 * width, 0) for w in gc.pieces],
            flops=2 * length * width * 2 * width,
        )
        v.ffn_normed = run.wait(normed)
        v.normed_far = lax.ppermute(v.ffn_normed, AXES, sibling(n))

    def ffn_part():
        outs = [shape(two, BF16), shape((width, 2 * length), BF16), shape(two, F32), shape(two, F32)]
        v.n_two, v.nt_two, res, v.dn, *pieces = call(
            ffn_first,
            outs + [shape(w.shape, BF16) for w in ga.pieces],
            (v.ffn_normed, run.wait(v.normed_far), v.dy_two, v.dyt_two, *ga.pieces),
            flops=work * first,
        )
        v.ra = Scatter(pieces, n, run)
        v.res = run.wait(res)

    def ffn_rest():
        outs = [shape(stream, F32), shape(stream, F32), shape((length, 2 * width), BF16)]
        v.res, v.dn, far, *pieces = call(
            ffn_second,
            outs + [shape(w.shape, BF16) for w in gb.pieces],
            (v.n_two, v.nt_two, v.dy_two, v.dyt_two, run.tie(v.res), v.dn, *gb.pieces),
            flops=work * last,
        )
        v.rb = Scatter(pieces, n, run)
        v.far = lax.ppermute(run.wait(far), AXES, sibling(n))

    def ffn_back():
        v.result, v.grad, v.ffn_gain_grad, v.branch, v.mixed_grad = call(
            ffn_end,
            [
                shape(stream, BF16),
                shape(stream, F32),
                shape((1, width), F32),
                shape(stream, BF16),
                shape(stream, BF16),
            ],
            (v.second, v.res, v.dn, run.wait(v.far), dy, gains, *gc.pieces),
            [None] * 6 + [columns(w, width, 1) for w in gc.pieces],
            flops=2 * length * width * width,
        )

    def cross_back_part():
        outs = [shape((2 * kv, part), BF16)] * nm
        if narrow:
            outs = [shape((2 * kv, span), BF16)]
        q_grad, *blocks = call(
            cross_back,
            [shape(stream, BF16)] + outs,
            (v.cross_q, v.pair_t, v.cross_p, run.tie(v.mixed_grad)),
            flops=2 * length * span * width * 8,
        )
        v.cross_q_grad = run.wait(q_grad)
        if narrow:
            blocks = [blocks[0][:, t * part : (t + 1) * part] for t in range(nm)]
        v.parts = blocks

    def memory_back():
        v.sent = swap_rows([v.parts[0]] + [run.tie(b) for b in v.parts[1:]], nm, nd)

    def memory_back_there():
        v.there = [run.wait(block) for block in v.sent]

    def cross_mid_part():
        v.grad, v.cross_gain_grad, v.low, v.mixed_grad = call(
            cross_mid,
            [shape(stream, F32), shape((1, width), F32), shape(stream, BF16), shape(stream, BF16)],
            (run.tie(v.cross_q_grad), v.middle, v.grad, gains, *gc.pieces, *gs.pieces),
            [None] * 4 + [columns(w, width, 0) for w in gc.pieces] + [columns(w, width, 2) for w in gs.pieces],
            flops=2 * length * width * width * 2,
        )
        v.mixed_grad = run.wait(v.mixed_grad)

    def cross_grads_part():
        pieces = call(
            cross_grads,
            [shape((width // 4, 3 * width), BF16)] * 4,
            (v.cross_normed, run.tie(v.cross_q_grad), v.branch, v.cross_mixed, v.low, v.mixed),
            flops=2 * length * width * width * 3,
        )
        run.wait(pieces[0])
        v.rc = Scatter(pieces, n, run)
        v.rc.go()

    def self_back_part():
        v.grads, table = call(
            self_back,
            [shape((length, width + 2 * kv), BF16), shape((heads, buckets), F32)],
            (v.q, v.kt, v.vt, v.p, run.tie(v.mixed_grad), bucket_line),
            flops=2 * length * length * width * 8,
            scratch=[pltpu.VMEM((heads, length), F32)],
        )
        v.table = run.wait(table)

    def self_grads_part():
        pieces = call(
            self_grads,
            [shape((width // 4, width + 4 * kv), BF16)] * 4,
            (self_normed_t, run.tie(v.grads), local_t, *v.there),
            flops=2 * (length + span // 2) * width * 2 * width,
        )
        run.wait(pieces[0])
        v.rs = Scatter(pieces, n, run)
        v.rs.go()

    def self_end_part():
        v.input_grad, packed = call(
            self_end,
            [shape(stream, F32), shape((3 * width // 128 + heads, 128), F32)],
            (x, v.grad, run.tie(v.grads), gains, order, v.cross_gain_grad, v.ffn_gain_grad, v.table, *gs.pieces),
            [None] * 8 + [columns(w, width + 2 * kv, 0) for w in gs.pieces],
            flops=2 * length * width * 4 * width,
        )
        v.total = Total(run.wait(packed), n, run)
        v.total.send()

    def memory_end_part():
        memory_grad, v.result = call(
            memory_end,
            [shape((nm, part, width), F32), shape(stream, BF16)],
            (places, run.tie(order), v.result, *gc.pieces, *v.there),
            [SCALARS] + [None] * 2 + v.pair_spec + [None] * nm,
            flops=2 * span * width * 3 * width,
        )
        v.memory_grad = run.wait(memory_grad)

    def columns_back():
        v.far = jnp.concatenate([v.ra.done()[1], v.rb.done()[1]], axis=1)
        v.far = lax.ppermute(v.far, AXES, sibling(n))

    actions = {
        "p": lambda: run.pace(20),
        "q": lambda: run.pace(7),
        "s": gs.go,
        "c": gc.go,
        "a": ga.go,
        "b": gb.go,
        "x1": prepare,
        "x2": prepare_grad,
        "x3": prepare_memory,
        "K1": self_part,
        "K2": memory_part,
        "w2": memory_there,
        "K3": cross_part,
        "K4": ffn_part,
        "K5": ffn_rest,
        "K6": ffn_back,
        "K7": cross_back_part,
        "m7": memory_back,
        "w7": memory_back_there,
        "K8": cross_mid_part,
        "K9": self_back_part,
        "K10": self_grads_part,
        "K11": cross_grads_part,
        "K12": self_end_part,
        "K13": memory_end_part,
        "A": lambda: v.ra.go(),
        "B": lambda: v.rb.go(),
        "C": lambda: v.rc.go(),
        "S": lambda: v.rs.go(),
        "t": lambda: v.total.go(),
        "u": columns_back,
    }
    for name in PLAN:
        actions[name]()

    memory_grad, result, input_grad = v.memory_grad, v.result, v.input_grad
    done_a, done_b, done_c = (group.done() for group in (v.ra, v.rb, v.rc))
    (done_s,) = call(
        finish,
        [shape(v.rs.held.shape, F32)],
        (v.rs.held, v.rs.came, run.token),
        [None, None, pl.BlockSpec(memory_space=pl.ANY)],
    )
    whole = shape((rows, hidden), F32)
    gate_done, up_done, down_done = call(
        functools.partial(unpack, first),
        [whole, whole, whole],
        (core, done_a[0], done_b[0], v.far),
        [SCALARS] + [None] * 3,
    )

    gain_lines = 3 * width // 128
    packed = v.total.value
    gain_grads = packed[:gain_lines].reshape(3, width)
    table = packed[gain_lines:, :buckets].T

    return (
        result.reshape(block_input.shape),
        input_grad.reshape(block_input.shape),
        memory_grad.reshape(memory.shape),
        gain_grads[0],
        gain_grads[1],
        gain_grads[2],
        table,
        done_s[:, :width],
        done_s[:, width : width + kv],
        done_s[:, width + kv : width + 2 * kv],
        done_c[:, 2 * width :],
        done_c[:, :width],
        done_s[:, width + 2 * kv : width + 3 * kv],
        done_s[:, width + 3 * kv :],
        done_c[:, width : 2 * width],
        gate_done,
        up_done,
        down_done,
    )


def solution(mesh):
    stream = P("dp", "mem", None, None)
    segments = P("dp", "mem", None)
    shard = P(AXES, None)
    in_specs = (stream, P("dp", None, "mem", None), stream, segments, segments) + (P(),) * 5 + (shard,) * 11
    out_specs = (stream, stream, P("dp", None, "mem", None)) + (P(),) * 4 + (shard,) * 11
    body = functools.partial(shards, mesh.shape["mem"], mesh.shape["dp"])
    return jax.shard_map(body, mesh=mesh, in_specs=in_specs, out_specs=out_specs, check_vma=False)
```

```python
import functools
import types

import jax
import jax.numpy as jnp
import numpy as np
from jax import lax
from jax.experimental import pallas as pl
from jax.experimental.pallas import tpu as pltpu
from jax.sharding import PartitionSpec as P

DH = 64
LANES = 128
EPSILON = 1e-06
NEGATIVE = -1e30
AXES = ("mem", "dp")
F32 = jnp.float32
BF16 = jnp.bfloat16
HIGHEST = lax.Precision.HIGHEST
MIB = 1024 * 1024


PLAN = " ".join((
    "s x1 s c",
    "x2 s x3 c",
    "c a a s",
    "p c s K1",
    "c a b b",
    "a c K2 b",
    "a w2 b K3",
    "K4 b A K5",
    "B K6 K7 A",
    "m7 K8 K9 B",
    "A w7 K10 K11",
    "S C K12 A",
    "B K13 t S",
    "t C A B",
    "S t C t",
    "S C B u",
    "t S C",
)).split()


def steps(n):
    high = list(range(n.bit_length() - 2, 2, -1))
    return (high + [2, 1], high + [1, 2])


def exchange(n, k):
    order = steps(n)
    return [(d, d ^ (1 << order[d & 1][k])) for d in range(n)]


def sibling(n):
    return [(d, d ^ 1) for d in range(n)]


def source(n, me):
    order = steps(n)
    half = n // 2
    table = np.zeros((2, half), np.int32)
    for core in range(2):
        for slot in range(half):
            for k in range(len(order[core])):
                if slot >> k & 1:
                    table[core, slot] ^= 1 << order[core][k]
    odd = (me & 1) == 1
    own = jnp.where(odd, table[1], table[0])
    other = jnp.where(odd, table[0], table[1])
    return jnp.concatenate([me ^ own, me ^ 1 ^ other])


class Order:
    def __init__(self, token):
        self.token = token

    def tie(self, value):
        value, self.token = lax.optimization_barrier((value, self.token))
        return value

    wait = tie

    def pace(self, micros):
        spec = pl.BlockSpec(memory_space=pl.ANY)
        self.token = pl.pallas_call(
            idle,
            in_specs=[spec],
            out_specs=spec,
            out_shape=shape(self.token.shape, self.token.dtype),
            input_output_aliases={0: 0},
            cost_estimate=pl.CostEstimate(
                flops=micros * 1000 * 1000 * 1000, bytes_accessed=0, transcendentals=0
            ),
        )(self.token)


class Gather:
    def __init__(self, shard, n, order, twin=True):
        self.n = n
        self.order = order
        self.held = shard
        self.last = n.bit_length() - 3
        self.k = 0
        self.flying = None
        self.twin = twin
        self.pieces = None

    def send(self):
        self.flying = lax.ppermute(self.held, AXES, exchange(self.n, self.k))

    def grow(self):
        came = self.order.wait(self.flying)
        self.held = jnp.concatenate([self.held, came], axis=self.held.ndim - 2)
        self.k += 1

    def go(self):
        if self.flying is None:
            self.held = self.order.tie(self.held)
            self.send()
        elif self.pieces is not None:
            self.pieces = self.pieces + [self.order.wait(p) for p in self.flying]
        elif self.k == self.last:
            self.pieces = [self.held, self.order.wait(self.flying)]
            if self.twin:
                self.flying = [lax.ppermute(p, AXES, sibling(self.n)) for p in self.pieces]
        else:
            if self.k == 0:
                for _ in range(self.n.bit_length() - 6):
                    self.grow()
                    self.send()
            self.grow()
            self.send()


class Scatter:
    def __init__(self, pieces, n, order):
        self.n = n
        self.order = order
        self.pieces = pieces
        self.k = n.bit_length() - 3
        self.flying = None
        self.both = len(pieces) == 4
        if not self.both:
            self.held = pieces[0]
            self.low = pieces[1]

    def send(self):
        self.flying = lax.ppermute(self.low, AXES, exchange(self.n, self.k))

    def shrink(self):
        came = self.order.wait(self.flying)
        self.k -= 1
        self.low, self.held = absorb(self.held, came)

    def go(self):
        if self.flying is None and self.both:
            self.flying = [lax.ppermute(p, AXES, sibling(self.n)) for p in self.pieces[2:]]
        elif self.both:
            there = [self.order.wait(p) for p in self.flying]
            self.low, self.held = absorb_twin(*self.pieces[:2], *there)
            self.both = False
            self.send()
        elif self.flying is None:
            self.send()
        elif self.k == 0:
            self.came = self.order.wait(self.flying)
        else:
            extra = self.n.bit_length() - 6
            if self.k == extra + 1:
                for _ in range(extra):
                    self.shrink()
                    self.send()
            self.shrink()
            self.send()

    def done(self):
        return self.held + self.came.astype(F32)


def absorb_step(held, came, low_out, held_out):
    half = low_out.shape[-2]
    low_out[...] = (held[..., half:, :].astype(F32) + came[..., half:, :].astype(F32)).astype(BF16)
    held_out[...] = held[..., :half, :].astype(F32) + came[..., :half, :].astype(F32)


def absorb_twin_step(held, low, held_came, low_came, low_out, held_out):
    low_out[...] = (low[...].astype(F32) + low_came[...].astype(F32)).astype(BF16)
    held_out[...] = held[...].astype(F32) + held_came[...].astype(F32)


def by_columns(body, args, dims):
    size = dims[-1]
    tiles = 3 if size % (3 * LANES) == 0 and dims[-2] >= 64 else 1

    def spec(whole):
        block = tuple(whole[:-1]) + (size // tiles,)
        return pl.BlockSpec(block, lambda j, rank=len(whole): (0,) * (rank - 1) + (j,))

    return pl.pallas_call(
        body,
        grid=(tiles,),
        in_specs=[spec(a.shape) for a in args],
        out_specs=[spec(dims), spec(dims)],
        out_shape=[shape(dims, BF16), shape(dims, F32)],
        compiler_params=pltpu.CompilerParams(vmem_limit_bytes=20 * MIB),
        cost_estimate=pl.CostEstimate(
            flops=2 * args[0].size, bytes_accessed=10 * args[0].size, transcendentals=0
        ),
    )(*args)


def absorb(held, came):
    dims = held.shape[:-2] + (held.shape[-2] // 2, held.shape[-1])
    return by_columns(absorb_step, (held, came), dims)


def absorb_twin(held, low, held_came, low_came):
    return by_columns(absorb_twin_step, (held, low, held_came, low_came), held.shape)


class Total:
    def __init__(self, value, n, order):
        self.value = value
        self.n = n
        self.order = order
        self.bit = 0

    def send(self):
        pairs = [(d, d ^ (1 << self.bit)) for d in range(self.n)]
        self.flying = lax.ppermute(self.value, AXES, pairs)

    def take(self):
        self.value = self.value + self.order.wait(self.flying)
        self.bit += 1

    def go(self):
        if self.bit == 4:
            for _ in range(self.n.bit_length() - 6):
                self.take()
                self.send()
        self.take()
        if self.bit < self.n.bit_length() - 1:
            self.send()


def swap_rows(blocks, nm, nd):
    n = nm * nd
    return [blocks[0]] + [
        lax.ppermute(blocks[t], AXES, [(d, d ^ (t * nd)) for d in range(n)]) for t in range(1, nm)
    ]


def dot(left, right, a=1, b=0):
    return lax.dot_general(left, right, (((a,), (b,)), ((), ())), preferred_element_type=F32)


def rows_of(left, p):
    size = left.shape[1] // 4
    return left[:, p * size : (p + 1) * size]


def project(left, weights):
    total = dot(rows_of(left, 0), weights[0])
    for p in range(1, 4):
        total = total + dot(rows_of(left, p), weights[p])
    return total


def project_back(left, weights):
    return jnp.concatenate([dot(left, w, 1, 1) for w in weights], axis=1)


def scale_of(stream):
    return lax.rsqrt(jnp.mean(stream * stream, axis=1, keepdims=True) + EPSILON)


def norm_back(stream, gain, grad):
    scale = scale_of(stream)
    weighted = grad * gain
    inner = jnp.mean(weighted * stream, axis=1, keepdims=True)
    out = scale * weighted - stream * (scale * scale * scale) * inner
    return out, jnp.sum(grad * stream * scale, axis=0, keepdims=True)


def transposed(value):
    return value.astype(F32).T.astype(BF16)


def spread(part):
    zero = jnp.zeros_like(part)
    top = jnp.concatenate([part, zero], axis=1)
    low = jnp.concatenate([zero, part], axis=1)
    return jnp.concatenate([top, low], axis=0)


def softmax(scores):
    expo = jnp.exp(scores - jnp.max(scores, axis=1, keepdims=True))
    return (expo / jnp.sum(expo, axis=1, keepdims=True)).astype(BF16)


def line_of(buckets, count):
    rows = lax.broadcasted_iota(jnp.int32, (count, buckets.shape[1]), 0)
    return (rows == buckets).astype(F32)


def pick(value, row):
    return lax.broadcasted_iota(jnp.int32, value.shape, 0) == row


def toeplitz(line):
    first = jnp.broadcast_to(line, (8, line.shape[1]))
    block = first
    for i in range(1, 8):
        block = jnp.where(pick(block, i), pltpu.roll(first, i, 1), block)
    size = 8
    while size < line.shape[1]:
        block = jnp.concatenate([block, pltpu.roll(block, size, 1)], axis=0)
        size *= 2
    return block


def diagonals(block):
    size = block.shape[0]
    while size > 8:
        size //= 2
        block = block[:size] + pltpu.roll(block[size:], block.shape[1] - size, 1)
    total = block
    for i in range(1, 8):
        total = jnp.where(pick(block, i), pltpu.roll(block, block.shape[1] - i, 1), total)
    return jnp.sum(total, axis=0, keepdims=True)


def split_dot(value, order, b):
    total = None
    for _ in range(3):
        high = value.astype(BF16)
        part = dot(high, order, 1, b)
        total = part if total is None else total + part
        value = value - high.astype(F32)
    return total


def pack(first, core, sq, sk, sv, so, cq, ck, cv, co, fg, fu, fd, self_out, cross_out, a_out, b_out, far_out):
    for out, parts in ((self_out, (sq, sk, sv, so)), (cross_out, (cq, co, ck, cv))):
        at = 0
        for part in parts:
            size = part.shape[1]
            out[:, at : at + size] = part[...]
            at += size
    odd = core[0] == 1
    half = fg.shape[1] // 2
    last = half - first
    for i, part in enumerate((fg, fu, fd)):
        low = part[:, :half].astype(F32)
        high = part[:, half:].astype(F32)
        mine = jnp.where(odd, high, low).astype(BF16)
        far = jnp.where(odd, low, high).astype(BF16)
        a_out[:, i * first : (i + 1) * first] = mine[:, :first]
        b_out[:, i * last : (i + 1) * last] = mine[:, first:]
        far_out[:, i * first : (i + 1) * first] = far[:, :first]
        far_out[:, 3 * first + i * last : 3 * first + (i + 1) * last] = far[:, first:]


def unpack(first, core, a, b, far, g_out, u_out, d_out):
    odd = core[0] == 1
    half = g_out.shape[1] // 2
    last = half - first
    for i, out in enumerate((g_out, u_out, d_out)):
        mine = jnp.concatenate(
            [a[:, i * first : (i + 1) * first], b[:, i * last : (i + 1) * last]], axis=1
        )
        other = jnp.concatenate(
            [
                far[:, i * first : (i + 1) * first],
                far[:, 3 * first + i * last : 3 * first + (i + 1) * last],
            ],
            axis=1,
        )
        out[:, :half] = jnp.where(odd, other, mine)
        out[:, half:] = jnp.where(odd, mine, other)


def turn(value):
    half = value.shape[1] // 2
    return jnp.concatenate([value[:, half:], value[:, :half]], axis=1)


def inner(value):
    b = value.shape[1] // 8
    return jnp.concatenate(
        [value[:, : 5 * b], value[:, 6 * b : 7 * b], value[:, 5 * b : 6 * b], value[:, 7 * b :]],
        axis=1,
    )


def both_cores(mine, other):
    return jnp.concatenate([inner(mine[...]), inner(turn(other[...]))], axis=0)


def pair_up(mine, other, out, out_t):
    value = both_cores(mine, other)
    out[...] = value
    out_t[...] = transposed(value)


def arrange(places, x_in, dy_in, feature, gains_in, x_out, dy_out, n_out, nt_out, gains_out, order_out):
    width = feature.shape[1]
    rows = lax.broadcasted_iota(jnp.int32, (width, width), 0)
    order = (rows == feature[...]).astype(F32).astype(BF16)
    order_out[...] = order
    gains = split_dot(gains_in[...], order, 0)
    gains_out[...] = gains
    x = dot(x_in[...], order)
    x_out[...] = x.astype(BF16)
    n = x * scale_of(x) * gains[0:1]
    n_out[...] = n.astype(BF16)
    nt_out[...] = n.T.astype(BF16)
    dy_out[...] = dot(dy_in[...], order).astype(BF16)


def arrange_memory(places, memory, order, out, out_t):
    part = memory.shape[1]
    for t in range(memory.shape[0]):
        block = dot(memory[places[t]], order[...])
        out[t * part : (t + 1) * part] = block.astype(BF16)
    out_t[...] = out[...].astype(F32).T.astype(BF16)


def self_forward(x, normed, bias, buckets, seg_col, seg_row, gains, w0, w1, w2, w3,
                 q_out, kt_out, vt_out, p_out, mixed_out, middle_out, n_out):
    weights = (w0, w1, w2, w3)
    width = x.shape[1]
    keys = w0.shape[1] - 2 * width
    kv = keys // 2
    length = x.shape[0]
    n = normed[...]
    q_out[...] = (project(n, [w[:, :width] for w in weights]).astype(BF16).astype(F32) * 0.125).astype(BF16)
    pair = project(n, [w[:, width : width + keys] for w in weights])
    pair_t = pair.T.astype(BF16)
    kt_out[...] = pair_t[:kv]
    vt_out[...] = pair_t[kv:]
    row = lax.broadcasted_iota(jnp.int32, (length, length), 0)
    column = lax.broadcasted_iota(jnp.int32, (length, length), 1)
    allowed = (column <= row) & (seg_col[...] == seg_row[...])
    lines = jnp.dot(bias[...], line_of(buckets[...], bias.shape[1]), precision=HIGHEST)
    for g in range(kv // DH):
        kk = spread(kt_out[g * DH : (g + 1) * DH])
        vv = spread(vt_out[g * DH : (g + 1) * DH])
        scores = dot(q_out[:, g * 2 * DH : (g + 1) * 2 * DH], kk)
        for h in range(2):
            part = scores[:, h * length : (h + 1) * length] + toeplitz(lines[2 * g + h : 2 * g + h + 1])
            p_out[g, :, h * length : (h + 1) * length] = softmax(jnp.where(allowed, part, NEGATIVE))
        mixed_out[:, g * 2 * DH : (g + 1) * 2 * DH] = dot(p_out[g], vv, 1, 1).astype(BF16)
    middle = x[...].astype(F32) + project_back(mixed_out[...], [w[:, width + keys :] for w in weights])
    middle_out[...] = middle
    n_out[...] = (middle * scale_of(middle) * gains[1:2]).astype(BF16)


def memory_forward(memory, w0, w1, w2, w3, pair_out):
    pair = project(memory[...], [w[...] for w in (w0, w1, w2, w3)])
    pair_out[...] = pair.T.astype(BF16)


def cross_forward(middle, normed, pair, seg_col, seg_row, gains, w0, w1, w2, w3,
                  q_out, p_out, mixed_out, second_out, n_out):
    weights = (w0, w1, w2, w3)
    width = middle.shape[1]
    kv = pair.shape[0] // 2
    span = pair.shape[1]
    q = project(normed[...], [w[:, :width] for w in weights])
    q_out[...] = (q.astype(BF16).astype(F32) * 0.125).astype(BF16)
    allowed = seg_col[...] == seg_row[...]
    for g in range(kv // DH):
        kk = spread(pair[g * DH : (g + 1) * DH])
        vv = spread(pair[kv + g * DH : kv + (g + 1) * DH])
        scores = dot(q_out[:, g * 2 * DH : (g + 1) * 2 * DH], kk)
        for h in range(2):
            part = scores[:, h * span : (h + 1) * span]
            p_out[g, :, h * span : (h + 1) * span] = softmax(jnp.where(allowed, part, NEGATIVE))
        mixed_out[:, g * 2 * DH : (g + 1) * 2 * DH] = dot(p_out[g], vv, 1, 1).astype(BF16)
    second = middle[...] + project_back(mixed_out[...], [w[:, width:] for w in weights])
    second_out[...] = second
    n_out[...] = (second * scale_of(second) * gains[2:3]).astype(BF16)


def ffn_work(n, nt, dy, dyt, w0, w1, g0, g1):
    weights = [w0[0], w1[0], w0[1], w1[1]]
    size = w0.shape[2] // 3
    pair = project(n[...], [w[:, : 2 * size] for w in weights])
    gate = pair[:, :size]
    lifted = pair[:, size:]
    hidden_grad = project(dy[...], [w[:, 2 * size :] for w in weights])
    root = 0.7978845608028654
    square = gate * gate
    tanh = jnp.tanh(root * gate * (1.0 + 0.044715 * square))
    half = 0.5 * (1.0 + tanh)
    gelu = gate * half
    slope = half + 0.5 * gate * (1.0 - tanh * tanh) * (root * (1.0 + 3.0 * 0.044715 * square))
    hidden = (gelu * lifted).astype(BF16)
    pair_grad = jnp.concatenate(
        [(hidden_grad * lifted * slope).astype(BF16), (hidden_grad * gelu).astype(BF16)], axis=1
    )
    rows = nt.shape[0] // 4
    for p in range(4):
        g = (g0, g1)[p % 2]
        mine = slice(p * rows, (p + 1) * rows)
        g[p // 2, :, : 2 * size] = dot(nt[mine], pair_grad).astype(BF16)
        g[p // 2, :, 2 * size :] = dot(dyt[mine], hidden).astype(BF16)
    res = project_back(hidden, [w[:, 2 * size :] for w in weights])
    dn = project_back(pair_grad, [w[:, : 2 * size] for w in weights])
    return res, dn


def ffn_first(mine, other, dy, dyt, w0, w1, n, nt, res, dn, g0, g1):
    value = both_cores(mine, other)
    n[...] = value
    nt[...] = transposed(value)
    res[...], dn[...] = ffn_work(n, nt, dy, dyt, w0, w1, g0, g1)


def ffn_second(n, nt, dy, dyt, res_in, dn_in, w0, w1, res_out, dn_out, far_out, g0, g1):
    res, dn = ffn_work(n, nt, dy, dyt, w0, w1, g0, g1)
    length = res_out.shape[0]
    width = res_out.shape[1]
    for i, (part, start, out) in enumerate(((res, res_in, res_out), (dn, dn_in, dn_out))):
        out[...] = inner(start[:length] + part[:length])
        far = turn(inner(start[length:] + part[length:]))
        far_out[:, i * width : (i + 1) * width] = far.astype(BF16)


def ffn_end(second, res, dn, far, dy, gains, w0, w1, w2, w3, result_out, grad_out, gain_out, branch_out, mixed_out):
    width = second.shape[1]
    result_out[...] = (second[...] + (res[...] + far[:, :width].astype(F32))).astype(BF16)
    back, gain_grad = norm_back(
        second[...], gains[2:3], dn[...] + far[:, width:].astype(F32)
    )
    grad = dy[...].astype(F32) + back
    grad_out[...] = grad
    gain_out[...] = gain_grad
    branch = grad.astype(BF16)
    branch_out[...] = branch
    mixed_out[...] = project(branch, [w[...] for w in (w0, w1, w2, w3)]).astype(BF16)


def attention_back(q, kt, vt, p, mixed_grad, span, g, head):
    lanes = slice(g * 2 * DH, (g + 1) * 2 * DH)
    kk = spread(kt)
    vv = spread(vt)
    queries = q[:, lanes]
    grad = mixed_grad[:, lanes]
    prob_grad = dot(grad, vv)
    probs = p[g]
    parts = []
    for h in range(2):
        one = probs[:, h * span : (h + 1) * span].astype(F32)
        change = prob_grad[:, h * span : (h + 1) * span]
        score = one * (change - jnp.sum(one * change, axis=1, keepdims=True))
        if head is not None:
            head(2 * g + h, score)
        parts.append(score.astype(BF16))
    score = jnp.concatenate(parts, axis=1)
    query_grad = (dot(score, kk, 1, 1) * 0.125).astype(BF16)
    key_grad = dot(queries, score, 0, 0)
    value_grad = dot(grad, probs, 0, 0)
    key_grad = key_grad[:DH, :span] + key_grad[DH:, span:]
    value_grad = value_grad[:DH, :span] + value_grad[DH:, span:]
    return query_grad, key_grad, value_grad


def cross_back(q, pair, p, mixed_grad, q_out, *pair_out):
    kv = pair.shape[0] // 2
    span = pair.shape[1]
    for g in range(kv // DH):
        mine = slice(g * DH, (g + 1) * DH)
        far = slice(kv + g * DH, kv + (g + 1) * DH)
        query_grad, key_grad, value_grad = attention_back(
            q, pair[mine], pair[far], p, mixed_grad, span, g, None
        )
        q_out[:, g * 2 * DH : (g + 1) * 2 * DH] = query_grad
        part = span // len(pair_out)
        for t, out in enumerate(pair_out):
            out[mine] = key_grad[:, t * part : (t + 1) * part].astype(BF16)
            out[far] = value_grad[:, t * part : (t + 1) * part].astype(BF16)


def cross_mid(q_grad, middle, grad, gains, w0, w1, w2, w3, s0, s1, s2, s3, grad_out, gain_out, branch_out, mixed_out):
    dn = project_back(q_grad[...], [w[...] for w in (w0, w1, w2, w3)])
    back, gain_grad = norm_back(middle[...], gains[1:2], dn)
    total = grad[...] + back
    grad_out[...] = total
    gain_out[...] = gain_grad
    low = total.astype(BF16)
    branch_out[...] = low
    mixed_out[...] = project(low, [s[...] for s in (s0, s1, s2, s3)]).astype(BF16)


def cross_grads(normed, q_grad, branch, mixed, low, self_mixed, g0, g1, g2, g3):
    width = mixed.shape[1]
    for p, g in enumerate((g0, g1, g2, g3)):
        g[:, :width] = dot(rows_of(normed, p), q_grad[...], 0, 0).astype(BF16)
        g[:, width : 2 * width] = dot(rows_of(branch, p), mixed[...], 0, 0).astype(BF16)
        g[:, 2 * width :] = dot(rows_of(low, p), self_mixed[...], 0, 0).astype(BF16)


def self_back(q, kt, vt, p, mixed_grad, buckets, out, table_out, lines):
    length = q.shape[0]
    width = q.shape[1]
    kv = kt.shape[0]

    def head(h, score):
        lines[h : h + 1] = diagonals(score)

    keys = []
    values = []
    for g in range(kv // DH):
        mine = slice(g * DH, (g + 1) * DH)
        query_grad, key_grad, value_grad = attention_back(
            q, kt[mine], vt[mine], p, mixed_grad, length, g, head
        )
        out[:, g * 2 * DH : (g + 1) * 2 * DH] = query_grad
        keys.append(key_grad)
        values.append(value_grad)
    out[:, width:] = jnp.concatenate(keys + values, axis=0).T.astype(BF16)
    table_out[...] = lax.dot_general(
        lines[...],
        line_of(buckets[...], table_out.shape[1]),
        (((1,), (1,)), ((), ())),
        precision=HIGHEST,
        preferred_element_type=F32,
    )


def restore(value, order):
    high = value.astype(BF16)
    low = (value - high.astype(F32)).astype(BF16)
    return dot(high, order, 1, 1) + dot(low, order, 1, 1)


def self_end(x, grad, grads, gains, order, cross_gain, ffn_gain, table, w0, w1, w2, w3, input_out, packed_out):
    dn = project_back(grads[...], [w[...] for w in (w0, w1, w2, w3)])
    back, gain_grad = norm_back(x[...].astype(F32), gains[0:1], dn)
    input_out[...] = restore(grad[...] + back, order[...])
    width = x.shape[1]
    found = jnp.concatenate([gain_grad, cross_gain[...], ffn_gain[...], jnp.zeros((5, width), F32)], axis=0)
    found = split_dot(found, order[...], 1)
    packed_out[...] = jnp.zeros_like(packed_out)
    lines = width // 128
    for i in range(3):
        for j in range(lines):
            packed_out[i * lines + j : i * lines + j + 1] = found[i : i + 1, j * 128 : (j + 1) * 128]
    packed_out[3 * lines :, : table.shape[1]] = table[...]


def self_grads(normed_t, grads, memory_t, *refs):
    size = normed_t.shape[0] // 4
    width = grads.shape[1]
    pair = jnp.concatenate([transposed(block[...]) for block in refs[:-4]], axis=0)
    for p, g in enumerate(refs[-4:]):
        mine = slice(p * size, (p + 1) * size)
        g[:, :width] = dot(normed_t[mine], grads[...]).astype(BF16)
        g[:, width:] = dot(memory_t[mine], pair).astype(BF16)


def memory_end(places, order, result, w0, w1, w2, w3, *refs):
    pair = jnp.concatenate([transposed(block[...]) for block in refs[:-2]], axis=0)
    out, result_out = refs[-2:]
    grad = restore(project_back(pair, [w[...] for w in (w0, w1, w2, w3)]), order[...])
    part = out.shape[1]
    for t in range(out.shape[0]):
        out[places[t]] = grad[t * part : (t + 1) * part]
    result_out[...] = dot(result[...], order[...], 1, 1).astype(BF16)


def idle(token, out):
    del token, out


def finish(held, came, token, out):
    out[...] = held[...] + came[...].astype(F32)


def shape(dims, kind):
    return jax.ShapeDtypeStruct(dims, kind)


def full(value):
    return pl.BlockSpec(value.shape, lambda i, rank=len(value.shape): (0,) * rank)


def columns(value, size, place):
    return pl.BlockSpec((value.shape[0], size), lambda i, place=place: (0, place))


SCALARS = pl.BlockSpec(memory_space=pltpu.SMEM)


def call(body, outs, args, specs=None, flops=0, scratch=(), room=12):
    specs = [full(a) if s is None else s for a, s in zip(args, specs or [None] * len(args))]
    moved = sum(int(np.prod(o.shape)) * o.dtype.itemsize for o in outs)
    moved += sum(int(np.prod(s.block_shape or a.shape)) * a.dtype.itemsize for a, s in zip(args, specs))
    return pl.pallas_call(
        body,
        grid=(1,),
        in_specs=specs,
        out_specs=[full(o) for o in outs],
        out_shape=outs,
        scratch_shapes=scratch,
        compiler_params=pltpu.CompilerParams(vmem_limit_bytes=min(2 * moved + room * MIB, 58 * MIB)),
        cost_estimate=pl.CostEstimate(flops=flops, bytes_accessed=moved, transcendentals=0),
    )(*args)


def shards(
    nm,
    nd,
    block_input,
    memory,
    out_grad,
    decoder_segments,
    encoder_segments,
    distance_buckets,
    self_gain,
    cross_gain,
    ffn_gain,
    position_bias,
    self_query,
    self_key,
    self_value,
    self_out,
    cross_query,
    cross_key,
    cross_value,
    cross_out,
    ffn_gate,
    ffn_up,
    ffn_down,
):
    n = nm * nd
    length, width = block_input.shape[2:]
    span = encoder_segments.shape[2]
    keys = self_key.shape[1]
    rows = self_query.shape[0]
    heads = position_bias.shape[1]
    buckets = position_bias.shape[0]
    hidden = ffn_gate.shape[1]
    place = lax.axis_index("mem")
    me = place * nd + lax.axis_index("dp")

    half = hidden // 2
    first = (half // LANES + 1) // 2 * LANES
    last = half - first
    core = (me & 1).reshape(1)
    both = shape((rows, 2 * width + 2 * keys), BF16)
    shard_s, shard_c, shard_a, shard_b, far = call(
        functools.partial(pack, first),
        [both, both, shape((rows, 3 * first), BF16), shape((rows, 3 * last), BF16), shape((rows, 3 * half), BF16)],
        (core, self_query, self_key, self_value, self_out, cross_query, cross_key, cross_value, cross_out, ffn_gate, ffn_up, ffn_down),
        [SCALARS] + [None] * 11,
        room=58,
    )
    run = Order(jnp.full((8, 128), me, F32))
    gs = Gather(shard_s, n, run)
    gc = Gather(shard_c, n, run)
    gs.go()
    far = run.wait(lax.ppermute(run.tie(far), AXES, sibling(n)))
    ga = Gather(jnp.stack([shard_a, far[:, : 3 * first]]), n, run, False)
    gb = Gather(jnp.stack([shard_b, far[:, 3 * first :]]), n, run, False)

    src = source(n, me)
    feature = (src[:, None] * rows + lax.iota(jnp.int32, rows)[None, :]).reshape(1, width)
    places = place ^ lax.iota(jnp.int32, nm)
    stream = (length, width)
    turned = (width, length)
    gains = jnp.concatenate([jnp.stack([self_gain, cross_gain, ffn_gain]), jnp.zeros((5, width), F32)])
    x, dy, self_normed, self_normed_t, gains, order = call(
        arrange,
        [
            shape(stream, BF16),
            shape(stream, BF16),
            shape(stream, BF16),
            shape(turned, BF16),
            shape((8, width), F32),
            shape((width, width), BF16),
        ],
        (places, block_input.reshape(stream), out_grad.reshape(stream), feature, gains),
        [SCALARS, None, None, None, None],
    )
    part = span // nm
    local, local_t = call(
        arrange_memory,
        [shape((span, width), BF16), shape((width, span), BF16)],
        (places, memory.reshape(nm, part, width), order),
        [SCALARS, None, None],
    )
    seg_col = decoder_segments.reshape(length, 1)
    seg_row = decoder_segments.reshape(1, length)
    key_seg = encoder_segments.reshape(nm, part)
    key_seg = jnp.concatenate(
        [lax.dynamic_index_in_dim(key_seg, place ^ t, 0, keepdims=True) for t in range(nm)], axis=1
    )
    bucket_line = jnp.roll(distance_buckets[::-1], 1).reshape(1, length)

    kv = keys
    groups = kv // DH
    two = (2 * length, width)
    work = 2 * 2 * length * width * 9
    narrow = part % LANES != 0
    v = types.SimpleNamespace()

    def prepare():
        v.normed = run.wait(self_normed)
        v.dy_far = lax.ppermute(dy, AXES, sibling(n))

    def prepare_grad():
        v.dy_far = run.wait(v.dy_far)
        v.dy_two, v.dyt_two = call(
            pair_up, [shape(two, BF16), shape((width, 2 * length), BF16)], (dy, v.dy_far)
        )
        v.dyt_two = run.wait(v.dyt_two)

    def prepare_memory():
        v.local = run.wait(local)

    def self_part():
        v.q, v.kt, v.vt, v.p, v.mixed, v.middle, normed = call(
            self_forward,
            [
                shape(stream, BF16),
                shape((kv, length), BF16),
                shape((kv, length), BF16),
                shape((groups, length, 2 * length), BF16),
                shape(stream, BF16),
                shape(stream, F32),
                shape(stream, BF16),
            ],
            (x, run.tie(v.normed), position_bias.T, bucket_line, seg_col, seg_row, gains, *gs.pieces),
            flops=2 * length * width * 3 * width,
        )
        v.cross_normed = run.wait(normed)

    def memory_part():
        v.pair_spec = [columns(w, 2 * kv, 2 * width // (2 * kv)) for w in gc.pieces]
        (pair_t,) = call(
            memory_forward,
            [shape((2 * kv, span), BF16)],
            (run.tie(v.local), *gc.pieces),
            [None] + v.pair_spec,
            flops=2 * span * width * 2 * kv,
        )
        pair_t = run.wait(pair_t)
        v.blocks = swap_rows([pair_t[:, t * part : (t + 1) * part] for t in range(nm)], nm, nd)

    def memory_there():
        v.pair_t = jnp.concatenate([run.wait(block) for block in v.blocks], axis=1)

    def cross_part():
        v.cross_q, v.cross_p, v.cross_mixed, v.second, normed = call(
            cross_forward,
            [
                shape(stream, BF16),
                shape((groups, length, 2 * span), BF16),
                shape(stream, BF16),
                shape(stream, F32),
                shape(stream, BF16),
            ],
            (v.middle, run.tie(v.cross_normed), v.pair_t, seg_col, key_seg, gains, *gc.pieces),
            [None] * 6 + [columns(w, 2 * width, 0) for w in gc.pieces],
            flops=2 * length * width * 2 * width,
        )
        v.ffn_normed = run.wait(normed)
        v.normed_far = lax.ppermute(v.ffn_normed, AXES, sibling(n))

    def ffn_part():
        outs = [shape(two, BF16), shape((width, 2 * length), BF16), shape(two, F32), shape(two, F32)]
        v.n_two, v.nt_two, res, v.dn, *pieces = call(
            ffn_first,
            outs + [shape(w.shape, BF16) for w in ga.pieces],
            (v.ffn_normed, run.wait(v.normed_far), v.dy_two, v.dyt_two, *ga.pieces),
            flops=work * first,
        )
        v.ra = Scatter(pieces, n, run)
        v.res = run.wait(res)

    def ffn_rest():
        outs = [shape(stream, F32), shape(stream, F32), shape((length, 2 * width), BF16)]
        v.res, v.dn, far, *pieces = call(
            ffn_second,
            outs + [shape(w.shape, BF16) for w in gb.pieces],
            (v.n_two, v.nt_two, v.dy_two, v.dyt_two, run.tie(v.res), v.dn, *gb.pieces),
            flops=work * last,
        )
        v.rb = Scatter(pieces, n, run)
        v.far = lax.ppermute(run.wait(far), AXES, sibling(n))

    def ffn_back():
        v.result, v.grad, v.ffn_gain_grad, v.branch, v.mixed_grad = call(
            ffn_end,
            [
                shape(stream, BF16),
                shape(stream, F32),
                shape((1, width), F32),
                shape(stream, BF16),
                shape(stream, BF16),
            ],
            (v.second, v.res, v.dn, run.wait(v.far), dy, gains, *gc.pieces),
            [None] * 6 + [columns(w, width, 1) for w in gc.pieces],
            flops=2 * length * width * width,
        )

    def cross_back_part():
        outs = [shape((2 * kv, part), BF16)] * nm
        if narrow:
            outs = [shape((2 * kv, span), BF16)]
        q_grad, *blocks = call(
            cross_back,
            [shape(stream, BF16)] + outs,
            (v.cross_q, v.pair_t, v.cross_p, run.tie(v.mixed_grad)),
            flops=2 * length * span * width * 8,
        )
        v.cross_q_grad = run.wait(q_grad)
        if narrow:
            blocks = [blocks[0][:, t * part : (t + 1) * part] for t in range(nm)]
        v.parts = blocks

    def memory_back():
        v.sent = swap_rows([v.parts[0]] + [run.tie(b) for b in v.parts[1:]], nm, nd)

    def memory_back_there():
        v.there = [run.wait(block) for block in v.sent]

    def cross_mid_part():
        v.grad, v.cross_gain_grad, v.low, v.mixed_grad = call(
            cross_mid,
            [shape(stream, F32), shape((1, width), F32), shape(stream, BF16), shape(stream, BF16)],
            (run.tie(v.cross_q_grad), v.middle, v.grad, gains, *gc.pieces, *gs.pieces),
            [None] * 4 + [columns(w, width, 0) for w in gc.pieces] + [columns(w, width, 2) for w in gs.pieces],
            flops=2 * length * width * width * 2,
        )
        v.mixed_grad = run.wait(v.mixed_grad)

    def cross_grads_part():
        pieces = call(
            cross_grads,
            [shape((width // 4, 3 * width), BF16)] * 4,
            (v.cross_normed, run.tie(v.cross_q_grad), v.branch, v.cross_mixed, v.low, v.mixed),
            flops=2 * length * width * width * 3,
        )
        run.wait(pieces[0])
        v.rc = Scatter(pieces, n, run)
        v.rc.go()

    def self_back_part():
        v.grads, table = call(
            self_back,
            [shape((length, width + 2 * kv), BF16), shape((heads, buckets), F32)],
            (v.q, v.kt, v.vt, v.p, run.tie(v.mixed_grad), bucket_line),
            flops=2 * length * length * width * 8,
            scratch=[pltpu.VMEM((heads, length), F32)],
        )
        v.table = run.wait(table)

    def self_grads_part():
        pieces = call(
            self_grads,
            [shape((width // 4, width + 4 * kv), BF16)] * 4,
            (self_normed_t, run.tie(v.grads), local_t, *v.there),
            flops=2 * (length + span // 2) * width * 2 * width,
        )
        run.wait(pieces[0])
        v.rs = Scatter(pieces, n, run)
        v.rs.go()

    def self_end_part():
        v.input_grad, packed = call(
            self_end,
            [shape(stream, F32), shape((3 * width // 128 + heads, 128), F32)],
            (x, v.grad, run.tie(v.grads), gains, order, v.cross_gain_grad, v.ffn_gain_grad, v.table, *gs.pieces),
            [None] * 8 + [columns(w, width + 2 * kv, 0) for w in gs.pieces],
            flops=2 * length * width * 4 * width,
        )
        v.total = Total(run.wait(packed), n, run)
        v.total.send()

    def memory_end_part():
        memory_grad, v.result = call(
            memory_end,
            [shape((nm, part, width), F32), shape(stream, BF16)],
            (places, run.tie(order), v.result, *gc.pieces, *v.there),
            [SCALARS] + [None] * 2 + v.pair_spec + [None] * nm,
            flops=2 * span * width * 3 * width,
        )
        v.memory_grad = run.wait(memory_grad)

    def columns_back():
        v.far = jnp.concatenate([v.ra.done()[1], v.rb.done()[1]], axis=1)
        v.far = lax.ppermute(v.far, AXES, sibling(n))

    actions = {
        "p": lambda: run.pace(20),
        "q": lambda: run.pace(7),
        "s": gs.go,
        "c": gc.go,
        "a": ga.go,
        "b": gb.go,
        "x1": prepare,
        "x2": prepare_grad,
        "x3": prepare_memory,
        "K1": self_part,
        "K2": memory_part,
        "w2": memory_there,
        "K3": cross_part,
        "K4": ffn_part,
        "K5": ffn_rest,
        "K6": ffn_back,
        "K7": cross_back_part,
        "m7": memory_back,
        "w7": memory_back_there,
        "K8": cross_mid_part,
        "K9": self_back_part,
        "K10": self_grads_part,
        "K11": cross_grads_part,
        "K12": self_end_part,
        "K13": memory_end_part,
        "A": lambda: v.ra.go(),
        "B": lambda: v.rb.go(),
        "C": lambda: v.rc.go(),
        "S": lambda: v.rs.go(),
        "t": lambda: v.total.go(),
        "u": columns_back,
    }
    for name in PLAN:
        actions[name]()

    memory_grad, result, input_grad = v.memory_grad, v.result, v.input_grad
    done_a, done_b, done_c = (group.done() for group in (v.ra, v.rb, v.rc))
    (done_s,) = call(
        finish,
        [shape(v.rs.held.shape, F32)],
        (v.rs.held, v.rs.came, run.token),
        [None, None, pl.BlockSpec(memory_space=pl.ANY)],
    )
    whole = shape((rows, hidden), F32)
    gate_done, up_done, down_done = call(
        functools.partial(unpack, first),
        [whole, whole, whole],
        (core, done_a[0], done_b[0], v.far),
        [SCALARS] + [None] * 3,
    )

    gain_lines = 3 * width // 128
    packed = v.total.value
    gain_grads = packed[:gain_lines].reshape(3, width)
    table = packed[gain_lines:, :buckets].T

    return (
        result.reshape(block_input.shape),
        input_grad.reshape(block_input.shape),
        memory_grad.reshape(memory.shape),
        gain_grads[0],
        gain_grads[1],
        gain_grads[2],
        table,
        done_s[:, :width],
        done_s[:, width : width + kv],
        done_s[:, width + kv : width + 2 * kv],
        done_c[:, 2 * width :],
        done_c[:, :width],
        done_s[:, width + 2 * kv : width + 3 * kv],
        done_s[:, width + 3 * kv :],
        done_c[:, width : 2 * width],
        gate_done,
        up_done,
        down_done,
    )


def solution(mesh):
    stream = P("dp", "mem", None, None)
    segments = P("dp", "mem", None)
    shard = P(AXES, None)
    in_specs = (stream, P("dp", None, "mem", None), stream, segments, segments) + (P(),) * 5 + (shard,) * 11
    out_specs = (stream, stream, P("dp", None, "mem", None)) + (P(),) * 4 + (shard,) * 11
    body = functools.partial(shards, mesh.shape["mem"], mesh.shape["dp"])
    return jax.shard_map(body, mesh=mesh, in_specs=in_specs, out_specs=out_specs, check_vma=False)
```

```python
import functools
import types

import jax
import jax.numpy as jnp
import numpy as np
from jax import lax
from jax.experimental import pallas as pl
from jax.experimental.pallas import tpu as pltpu
from jax.sharding import PartitionSpec as P

DH = 64
LANES = 128
EPSILON = 1e-06
NEGATIVE = -1e30
AXES = ("mem", "dp")
F32 = jnp.float32
BF16 = jnp.bfloat16
HIGHEST = lax.Precision.HIGHEST
MIB = 1024 * 1024


PLAN = " ".join((
    "s x1 s c",
    "x2 s x3 c",
    "c a a s",
    "p c s K1",
    "c a b b",
    "a c K2 b",
    "a w2 b K3",
    "K4 b A K5",
    "B K6 K7 A",
    "m7 K8 K9 B",
    "A w7 K10 K11",
    "S C K12 A",
    "B K13 t S",
    "t C B A",
    "S t C t",
    "S C B u",
    "t S C",
)).split()


def steps(n):
    high = list(range(n.bit_length() - 2, 2, -1))
    return (high + [2, 1], high + [1, 2])


def exchange(n, k):
    order = steps(n)
    return [(d, d ^ (1 << order[d & 1][k])) for d in range(n)]


def sibling(n):
    return [(d, d ^ 1) for d in range(n)]


def source(n, me):
    order = steps(n)
    half = n // 2
    table = np.zeros((2, half), np.int32)
    for core in range(2):
        for slot in range(half):
            for k in range(len(order[core])):
                if slot >> k & 1:
                    table[core, slot] ^= 1 << order[core][k]
    odd = (me & 1) == 1
    own = jnp.where(odd, table[1], table[0])
    other = jnp.where(odd, table[0], table[1])
    return jnp.concatenate([me ^ own, me ^ 1 ^ other])


class Order:
    def __init__(self, token):
        self.token = token

    def tie(self, value):
        value, self.token = lax.optimization_barrier((value, self.token))
        return value

    wait = tie

    def pace(self, micros):
        spec = pl.BlockSpec(memory_space=pl.ANY)
        self.token = pl.pallas_call(
            idle,
            in_specs=[spec],
            out_specs=spec,
            out_shape=shape(self.token.shape, self.token.dtype),
            input_output_aliases={0: 0},
            cost_estimate=pl.CostEstimate(
                flops=micros * 1000 * 1000 * 1000, bytes_accessed=0, transcendentals=0
            ),
        )(self.token)


class Gather:
    def __init__(self, shard, n, order, twin=True):
        self.n = n
        self.order = order
        self.held = shard
        self.last = n.bit_length() - 3
        self.k = 0
        self.flying = None
        self.twin = twin
        self.pieces = None

    def send(self):
        self.flying = lax.ppermute(self.held, AXES, exchange(self.n, self.k))

    def grow(self):
        came = self.order.wait(self.flying)
        self.held = jnp.concatenate([self.held, came], axis=self.held.ndim - 2)
        self.k += 1

    def go(self):
        if self.flying is None:
            self.held = self.order.tie(self.held)
            self.send()
        elif self.pieces is not None:
            self.pieces = self.pieces + [self.order.wait(p) for p in self.flying]
        elif self.k == self.last:
            self.pieces = [self.held, self.order.wait(self.flying)]
            if self.twin:
                self.flying = [lax.ppermute(p, AXES, sibling(self.n)) for p in self.pieces]
        else:
            if self.k == 0:
                for _ in range(self.n.bit_length() - 6):
                    self.grow()
                    self.send()
            self.grow()
            self.send()


class Scatter:
    def __init__(self, pieces, n, order):
        self.n = n
        self.order = order
        self.pieces = pieces
        self.k = n.bit_length() - 3
        self.flying = None
        self.both = len(pieces) == 3
        if not self.both:
            self.held = pieces[0]
            self.low = pieces[1]

    def send(self):
        self.flying = lax.ppermute(self.low, AXES, exchange(self.n, self.k))

    def shrink(self):
        came = self.order.wait(self.flying)
        self.k -= 1
        self.low, self.held = absorb(self.held, came)

    def go(self):
        if self.flying is None and self.both:
            self.flying = lax.ppermute(self.pieces[2], AXES, sibling(self.n))
        elif self.both:
            came = self.order.wait(self.flying)
            self.low, self.held = absorb_twin(*self.pieces[:2], came)
            self.both = False
            self.send()
        elif self.flying is None:
            self.send()
        elif self.k == 0:
            self.came = self.order.wait(self.flying)
        else:
            extra = self.n.bit_length() - 6
            if self.k == extra + 1:
                for _ in range(extra):
                    self.shrink()
                    self.send()
            self.shrink()
            self.send()

    def done(self):
        return self.held + self.came.astype(F32)


def absorb_step(held, came, low_out, held_out):
    half = low_out.shape[-2]
    low_out[...] = (held[..., half:, :].astype(F32) + came[..., half:, :].astype(F32)).astype(BF16)
    held_out[...] = held[..., :half, :].astype(F32) + came[..., :half, :].astype(F32)


def absorb_twin_step(held, low, came, low_out, held_out):
    low_out[...] = (low[...].astype(F32) + came[1].astype(F32)).astype(BF16)
    held_out[...] = held[...].astype(F32) + came[0].astype(F32)


def by_columns(body, args, dims):
    size = dims[-1]
    tiles = 3 if size % (3 * LANES) == 0 and dims[-2] >= 64 else 1

    def spec(whole):
        block = tuple(whole[:-1]) + (size // tiles,)
        return pl.BlockSpec(block, lambda j, rank=len(whole): (0,) * (rank - 1) + (j,))

    return pl.pallas_call(
        body,
        grid=(tiles,),
        in_specs=[spec(a.shape) for a in args],
        out_specs=[spec(dims), spec(dims)],
        out_shape=[shape(dims, BF16), shape(dims, F32)],
        compiler_params=pltpu.CompilerParams(vmem_limit_bytes=20 * MIB),
        cost_estimate=pl.CostEstimate(
            flops=2 * args[0].size, bytes_accessed=10 * args[0].size, transcendentals=0
        ),
    )(*args)


def absorb(held, came):
    dims = held.shape[:-2] + (held.shape[-2] // 2, held.shape[-1])
    return by_columns(absorb_step, (held, came), dims)


def absorb_twin(held, low, came):
    return by_columns(absorb_twin_step, (held, low, came), held.shape)


class Total:
    def __init__(self, value, n, order):
        self.value = value
        self.n = n
        self.order = order
        self.bit = 0

    def send(self):
        pairs = [(d, d ^ (1 << self.bit)) for d in range(self.n)]
        self.flying = lax.ppermute(self.value, AXES, pairs)

    def take(self):
        self.value = self.value + self.order.wait(self.flying)
        self.bit += 1

    def go(self):
        if self.bit == 4:
            for _ in range(self.n.bit_length() - 6):
                self.take()
                self.send()
        self.take()
        if self.bit < self.n.bit_length() - 1:
            self.send()


def swap_rows(blocks, nm, nd):
    n = nm * nd
    return [blocks[0]] + [
        lax.ppermute(blocks[t], AXES, [(d, d ^ (t * nd)) for d in range(n)]) for t in range(1, nm)
    ]


def dot(left, right, a=1, b=0):
    return lax.dot_general(left, right, (((a,), (b,)), ((), ())), preferred_element_type=F32)


def rows_of(left, p):
    size = left.shape[1] // 4
    return left[:, p * size : (p + 1) * size]


def project(left, weights):
    total = dot(rows_of(left, 0), weights[0])
    for p in range(1, 4):
        total = total + dot(rows_of(left, p), weights[p])
    return total


def project_back(left, weights):
    return jnp.concatenate([dot(left, w, 1, 1) for w in weights], axis=1)


def scale_of(stream):
    return lax.rsqrt(jnp.mean(stream * stream, axis=1, keepdims=True) + EPSILON)


def norm_back(stream, gain, grad):
    scale = scale_of(stream)
    weighted = grad * gain
    inner = jnp.mean(weighted * stream, axis=1, keepdims=True)
    out = scale * weighted - stream * (scale * scale * scale) * inner
    return out, jnp.sum(grad * stream * scale, axis=0, keepdims=True)


def transposed(value):
    return value.astype(F32).T.astype(BF16)


def spread(part):
    zero = jnp.zeros_like(part)
    top = jnp.concatenate([part, zero], axis=1)
    low = jnp.concatenate([zero, part], axis=1)
    return jnp.concatenate([top, low], axis=0)


def softmax(scores):
    expo = jnp.exp(scores - jnp.max(scores, axis=1, keepdims=True))
    return (expo / jnp.sum(expo, axis=1, keepdims=True)).astype(BF16)


def line_of(buckets, count):
    rows = lax.broadcasted_iota(jnp.int32, (count, buckets.shape[1]), 0)
    return (rows == buckets).astype(F32)


def pick(value, row):
    return lax.broadcasted_iota(jnp.int32, value.shape, 0) == row


def toeplitz(line):
    first = jnp.broadcast_to(line, (8, line.shape[1]))
    block = first
    for i in range(1, 8):
        block = jnp.where(pick(block, i), pltpu.roll(first, i, 1), block)
    size = 8
    while size < line.shape[1]:
        block = jnp.concatenate([block, pltpu.roll(block, size, 1)], axis=0)
        size *= 2
    return block


def diagonals(block):
    size = block.shape[0]
    while size > 8:
        size //= 2
        block = block[:size] + pltpu.roll(block[size:], block.shape[1] - size, 1)
    total = block
    for i in range(1, 8):
        total = jnp.where(pick(block, i), pltpu.roll(block, block.shape[1] - i, 1), total)
    return jnp.sum(total, axis=0, keepdims=True)


def split_dot(value, order, b):
    total = None
    for _ in range(3):
        high = value.astype(BF16)
        part = dot(high, order, 1, b)
        total = part if total is None else total + part
        value = value - high.astype(F32)
    return total


def pack(first, core, sq, sk, sv, so, cq, ck, cv, co, fg, fu, fd, self_out, cross_out, a_out, b_out, far_out):
    for out, parts in ((self_out, (sq, sk, sv, so)), (cross_out, (cq, co, ck, cv))):
        at = 0
        for part in parts:
            size = part.shape[1]
            out[:, at : at + size] = part[...]
            at += size
    odd = core[0] == 1
    half = fg.shape[1] // 2
    last = half - first
    for i, part in enumerate((fg, fu, fd)):
        low = part[:, :half].astype(F32)
        high = part[:, half:].astype(F32)
        mine = jnp.where(odd, high, low).astype(BF16)
        far = jnp.where(odd, low, high).astype(BF16)
        a_out[:, i * first : (i + 1) * first] = mine[:, :first]
        b_out[:, i * last : (i + 1) * last] = mine[:, first:]
        far_out[:, i * first : (i + 1) * first] = far[:, :first]
        far_out[:, 3 * first + i * last : 3 * first + (i + 1) * last] = far[:, first:]


def unpack(first, core, a, b, far, g_out, u_out, d_out):
    odd = core[0] == 1
    half = g_out.shape[1] // 2
    last = half - first
    for i, out in enumerate((g_out, u_out, d_out)):
        mine = jnp.concatenate(
            [a[:, i * first : (i + 1) * first], b[:, i * last : (i + 1) * last]], axis=1
        )
        other = jnp.concatenate(
            [
                far[:, i * first : (i + 1) * first],
                far[:, 3 * first + i * last : 3 * first + (i + 1) * last],
            ],
            axis=1,
        )
        out[:, :half] = jnp.where(odd, other, mine)
        out[:, half:] = jnp.where(odd, mine, other)


def turn(value):
    half = value.shape[1] // 2
    return jnp.concatenate([value[:, half:], value[:, :half]], axis=1)


def inner(value):
    b = value.shape[1] // 8
    return jnp.concatenate(
        [value[:, : 5 * b], value[:, 6 * b : 7 * b], value[:, 5 * b : 6 * b], value[:, 7 * b :]],
        axis=1,
    )


def both_cores(mine, other):
    return jnp.concatenate([inner(mine[...]), inner(turn(other[...]))], axis=0)


def pair_up(mine, other, out, out_t):
    value = both_cores(mine, other)
    out[...] = value
    out_t[...] = transposed(value)


def arrange(places, x_in, dy_in, feature, gains_in, x_out, dy_out, n_out, nt_out, gains_out, order_out):
    width = feature.shape[1]
    rows = lax.broadcasted_iota(jnp.int32, (width, width), 0)
    order = (rows == feature[...]).astype(F32).astype(BF16)
    order_out[...] = order
    gains = split_dot(gains_in[...], order, 0)
    gains_out[...] = gains
    x = dot(x_in[...], order)
    x_out[...] = x.astype(BF16)
    n = x * scale_of(x) * gains[0:1]
    n_out[...] = n.astype(BF16)
    nt_out[...] = n.T.astype(BF16)
    dy_out[...] = dot(dy_in[...], order).astype(BF16)


def arrange_memory(places, memory, order, out, out_t):
    part = memory.shape[1]
    for t in range(memory.shape[0]):
        block = dot(memory[places[t]], order[...])
        out[t * part : (t + 1) * part] = block.astype(BF16)
    out_t[...] = out[...].astype(F32).T.astype(BF16)


def self_forward(x, normed, bias, buckets, seg_col, seg_row, gains, w0, w1, w2, w3,
                 q_out, kt_out, vt_out, p_out, mixed_out, middle_out, n_out):
    weights = (w0, w1, w2, w3)
    width = x.shape[1]
    keys = w0.shape[1] - 2 * width
    kv = keys // 2
    length = x.shape[0]
    n = normed[...]
    q_out[...] = (project(n, [w[:, :width] for w in weights]).astype(BF16).astype(F32) * 0.125).astype(BF16)
    pair = project(n, [w[:, width : width + keys] for w in weights])
    pair_t = pair.T.astype(BF16)
    kt_out[...] = pair_t[:kv]
    vt_out[...] = pair_t[kv:]
    row = lax.broadcasted_iota(jnp.int32, (length, length), 0)
    column = lax.broadcasted_iota(jnp.int32, (length, length), 1)
    allowed = (column <= row) & (seg_col[...] == seg_row[...])
    lines = jnp.dot(bias[...], line_of(buckets[...], bias.shape[1]), precision=HIGHEST)
    for g in range(kv // DH):
        kk = spread(kt_out[g * DH : (g + 1) * DH])
        vv = spread(vt_out[g * DH : (g + 1) * DH])
        scores = dot(q_out[:, g * 2 * DH : (g + 1) * 2 * DH], kk)
        for h in range(2):
            part = scores[:, h * length : (h + 1) * length] + toeplitz(lines[2 * g + h : 2 * g + h + 1])
            p_out[g, :, h * length : (h + 1) * length] = softmax(jnp.where(allowed, part, NEGATIVE))
        mixed_out[:, g * 2 * DH : (g + 1) * 2 * DH] = dot(p_out[g], vv, 1, 1).astype(BF16)
    middle = x[...].astype(F32) + project_back(mixed_out[...], [w[:, width + keys :] for w in weights])
    middle_out[...] = middle
    n_out[...] = (middle * scale_of(middle) * gains[1:2]).astype(BF16)


def memory_forward(memory, w0, w1, w2, w3, pair_out):
    pair = project(memory[...], [w[...] for w in (w0, w1, w2, w3)])
    pair_out[...] = pair.T.astype(BF16)


def cross_forward(middle, normed, pair, seg_col, seg_row, gains, w0, w1, w2, w3,
                  q_out, p_out, mixed_out, second_out, n_out):
    weights = (w0, w1, w2, w3)
    width = middle.shape[1]
    kv = pair.shape[0] // 2
    span = pair.shape[1]
    q = project(normed[...], [w[:, :width] for w in weights])
    q_out[...] = (q.astype(BF16).astype(F32) * 0.125).astype(BF16)
    allowed = seg_col[...] == seg_row[...]
    for g in range(kv // DH):
        kk = spread(pair[g * DH : (g + 1) * DH])
        vv = spread(pair[kv + g * DH : kv + (g + 1) * DH])
        scores = dot(q_out[:, g * 2 * DH : (g + 1) * 2 * DH], kk)
        for h in range(2):
            part = scores[:, h * span : (h + 1) * span]
            p_out[g, :, h * span : (h + 1) * span] = softmax(jnp.where(allowed, part, NEGATIVE))
        mixed_out[:, g * 2 * DH : (g + 1) * 2 * DH] = dot(p_out[g], vv, 1, 1).astype(BF16)
    second = middle[...] + project_back(mixed_out[...], [w[:, width:] for w in weights])
    second_out[...] = second
    n_out[...] = (second * scale_of(second) * gains[2:3]).astype(BF16)


def ffn_work(n, nt, dy, dyt, w0, w1, g0, g1):
    weights = [w0[0], w1[0], w0[1], w1[1]]
    size = w0.shape[2] // 3
    pair = project(n[...], [w[:, : 2 * size] for w in weights])
    gate = pair[:, :size]
    lifted = pair[:, size:]
    hidden_grad = project(dy[...], [w[:, 2 * size :] for w in weights])
    root = 0.7978845608028654
    square = gate * gate
    tanh = jnp.tanh(root * gate * (1.0 + 0.044715 * square))
    half = 0.5 * (1.0 + tanh)
    gelu = gate * half
    slope = half + 0.5 * gate * (1.0 - tanh * tanh) * (root * (1.0 + 3.0 * 0.044715 * square))
    hidden = (gelu * lifted).astype(BF16)
    pair_grad = jnp.concatenate(
        [(hidden_grad * lifted * slope).astype(BF16), (hidden_grad * gelu).astype(BF16)], axis=1
    )
    rows = nt.shape[0] // 4
    for p in range(4):
        g = (g0, g1)[p % 2]
        mine = slice(p * rows, (p + 1) * rows)
        g[p // 2, :, : 2 * size] = dot(nt[mine], pair_grad).astype(BF16)
        g[p // 2, :, 2 * size :] = dot(dyt[mine], hidden).astype(BF16)
    res = project_back(hidden, [w[:, 2 * size :] for w in weights])
    dn = project_back(pair_grad, [w[:, : 2 * size] for w in weights])
    return res, dn


def ffn_first(mine, other, dy, dyt, w0, w1, n, nt, res, dn, g0, g1):
    value = both_cores(mine, other)
    n[...] = value
    nt[...] = transposed(value)
    res[...], dn[...] = ffn_work(n, nt, dy, dyt, w0, w1, g0, g1)


def ffn_second(n, nt, dy, dyt, res_in, dn_in, w0, w1, res_out, dn_out, far_out, g0, g1):
    res, dn = ffn_work(n, nt, dy, dyt, w0, w1, g0, g1)
    length = res_out.shape[0]
    width = res_out.shape[1]
    for i, (part, start, out) in enumerate(((res, res_in, res_out), (dn, dn_in, dn_out))):
        out[...] = inner(start[:length] + part[:length])
        far = turn(inner(start[length:] + part[length:]))
        far_out[:, i * width : (i + 1) * width] = far.astype(BF16)


def ffn_end(second, res, dn, far, dy, gains, w0, w1, w2, w3, result_out, grad_out, gain_out, branch_out, mixed_out):
    width = second.shape[1]
    result_out[...] = (second[...] + (res[...] + far[:, :width].astype(F32))).astype(BF16)
    back, gain_grad = norm_back(
        second[...], gains[2:3], dn[...] + far[:, width:].astype(F32)
    )
    grad = dy[...].astype(F32) + back
    grad_out[...] = grad
    gain_out[...] = gain_grad
    branch = grad.astype(BF16)
    branch_out[...] = branch
    mixed_out[...] = project(branch, [w[...] for w in (w0, w1, w2, w3)]).astype(BF16)


def attention_back(q, kt, vt, p, mixed_grad, span, g, head):
    lanes = slice(g * 2 * DH, (g + 1) * 2 * DH)
    kk = spread(kt)
    vv = spread(vt)
    queries = q[:, lanes]
    grad = mixed_grad[:, lanes]
    prob_grad = dot(grad, vv)
    probs = p[g]
    parts = []
    for h in range(2):
        one = probs[:, h * span : (h + 1) * span].astype(F32)
        change = prob_grad[:, h * span : (h + 1) * span]
        score = one * (change - jnp.sum(one * change, axis=1, keepdims=True))
        if head is not None:
            head(2 * g + h, score)
        parts.append(score.astype(BF16))
    score = jnp.concatenate(parts, axis=1)
    query_grad = (dot(score, kk, 1, 1) * 0.125).astype(BF16)
    key_grad = dot(queries, score, 0, 0)
    value_grad = dot(grad, probs, 0, 0)
    key_grad = key_grad[:DH, :span] + key_grad[DH:, span:]
    value_grad = value_grad[:DH, :span] + value_grad[DH:, span:]
    return query_grad, key_grad, value_grad


def cross_back(q, pair, p, mixed_grad, q_out, *pair_out):
    kv = pair.shape[0] // 2
    span = pair.shape[1]
    for g in range(kv // DH):
        mine = slice(g * DH, (g + 1) * DH)
        far = slice(kv + g * DH, kv + (g + 1) * DH)
        query_grad, key_grad, value_grad = attention_back(
            q, pair[mine], pair[far], p, mixed_grad, span, g, None
        )
        q_out[:, g * 2 * DH : (g + 1) * 2 * DH] = query_grad
        part = span // len(pair_out)
        for t, out in enumerate(pair_out):
            out[mine] = key_grad[:, t * part : (t + 1) * part].astype(BF16)
            out[far] = value_grad[:, t * part : (t + 1) * part].astype(BF16)


def cross_mid(q_grad, middle, grad, gains, w0, w1, w2, w3, s0, s1, s2, s3, grad_out, gain_out, branch_out, mixed_out):
    dn = project_back(q_grad[...], [w[...] for w in (w0, w1, w2, w3)])
    back, gain_grad = norm_back(middle[...], gains[1:2], dn)
    total = grad[...] + back
    grad_out[...] = total
    gain_out[...] = gain_grad
    low = total.astype(BF16)
    branch_out[...] = low
    mixed_out[...] = project(low, [s[...] for s in (s0, s1, s2, s3)]).astype(BF16)


def cross_grads(normed, q_grad, branch, mixed, low, self_mixed, g0, g1, far):
    width = mixed.shape[1]
    for p, g in enumerate((g0, g1, far.at[0], far.at[1])):
        g[:, :width] = dot(rows_of(normed, p), q_grad[...], 0, 0).astype(BF16)
        g[:, width : 2 * width] = dot(rows_of(branch, p), mixed[...], 0, 0).astype(BF16)
        g[:, 2 * width :] = dot(rows_of(low, p), self_mixed[...], 0, 0).astype(BF16)


def self_back(q, kt, vt, p, mixed_grad, buckets, out, table_out, lines):
    length = q.shape[0]
    width = q.shape[1]
    kv = kt.shape[0]

    def head(h, score):
        lines[h : h + 1] = diagonals(score)

    keys = []
    values = []
    for g in range(kv // DH):
        mine = slice(g * DH, (g + 1) * DH)
        query_grad, key_grad, value_grad = attention_back(
            q, kt[mine], vt[mine], p, mixed_grad, length, g, head
        )
        out[:, g * 2 * DH : (g + 1) * 2 * DH] = query_grad
        keys.append(key_grad)
        values.append(value_grad)
    out[:, width:] = jnp.concatenate(keys + values, axis=0).T.astype(BF16)
    table_out[...] = lax.dot_general(
        lines[...],
        line_of(buckets[...], table_out.shape[1]),
        (((1,), (1,)), ((), ())),
        precision=HIGHEST,
        preferred_element_type=F32,
    )


def restore(value, order):
    high = value.astype(BF16)
    low = (value - high.astype(F32)).astype(BF16)
    return dot(high, order, 1, 1) + dot(low, order, 1, 1)


def self_end(x, grad, grads, gains, order, cross_gain, ffn_gain, table, w0, w1, w2, w3, input_out, packed_out):
    dn = project_back(grads[...], [w[...] for w in (w0, w1, w2, w3)])
    back, gain_grad = norm_back(x[...].astype(F32), gains[0:1], dn)
    input_out[...] = restore(grad[...] + back, order[...])
    width = x.shape[1]
    found = jnp.concatenate([gain_grad, cross_gain[...], ffn_gain[...], jnp.zeros((5, width), F32)], axis=0)
    found = split_dot(found, order[...], 1)
    packed_out[...] = jnp.zeros_like(packed_out)
    lines = width // 128
    for i in range(3):
        for j in range(lines):
            packed_out[i * lines + j : i * lines + j + 1] = found[i : i + 1, j * 128 : (j + 1) * 128]
    packed_out[3 * lines :, : table.shape[1]] = table[...]


def self_grads(normed_t, grads, memory_t, *refs):
    size = normed_t.shape[0] // 4
    width = grads.shape[1]
    pair = jnp.concatenate([transposed(block[...]) for block in refs[:-3]], axis=0)
    g0, g1, far = refs[-3:]
    for p, g in enumerate((g0, g1, far.at[0], far.at[1])):
        mine = slice(p * size, (p + 1) * size)
        g[:, :width] = dot(normed_t[mine], grads[...]).astype(BF16)
        g[:, width:] = dot(memory_t[mine], pair).astype(BF16)


def memory_end(places, order, result, w0, w1, w2, w3, *refs):
    pair = jnp.concatenate([transposed(block[...]) for block in refs[:-2]], axis=0)
    out, result_out = refs[-2:]
    grad = restore(project_back(pair, [w[...] for w in (w0, w1, w2, w3)]), order[...])
    part = out.shape[1]
    for t in range(out.shape[0]):
        out[places[t]] = grad[t * part : (t + 1) * part]
    result_out[...] = dot(result[...], order[...], 1, 1).astype(BF16)


def idle(token, out):
    del token, out


def finish(held, came, token, out):
    out[...] = held[...] + came[...].astype(F32)


def shape(dims, kind):
    return jax.ShapeDtypeStruct(dims, kind)


def full(value):
    return pl.BlockSpec(value.shape, lambda i, rank=len(value.shape): (0,) * rank)


def columns(value, size, place):
    return pl.BlockSpec((value.shape[0], size), lambda i, place=place: (0, place))


SCALARS = pl.BlockSpec(memory_space=pltpu.SMEM)


def call(body, outs, args, specs=None, flops=0, scratch=(), room=12):
    specs = [full(a) if s is None else s for a, s in zip(args, specs or [None] * len(args))]
    moved = sum(int(np.prod(o.shape)) * o.dtype.itemsize for o in outs)
    moved += sum(int(np.prod(s.block_shape or a.shape)) * a.dtype.itemsize for a, s in zip(args, specs))
    return pl.pallas_call(
        body,
        grid=(1,),
        in_specs=specs,
        out_specs=[full(o) for o in outs],
        out_shape=outs,
        scratch_shapes=scratch,
        compiler_params=pltpu.CompilerParams(vmem_limit_bytes=min(2 * moved + room * MIB, 58 * MIB)),
        cost_estimate=pl.CostEstimate(flops=flops, bytes_accessed=moved, transcendentals=0),
    )(*args)


def shards(
    nm,
    nd,
    block_input,
    memory,
    out_grad,
    decoder_segments,
    encoder_segments,
    distance_buckets,
    self_gain,
    cross_gain,
    ffn_gain,
    position_bias,
    self_query,
    self_key,
    self_value,
    self_out,
    cross_query,
    cross_key,
    cross_value,
    cross_out,
    ffn_gate,
    ffn_up,
    ffn_down,
):
    n = nm * nd
    length, width = block_input.shape[2:]
    span = encoder_segments.shape[2]
    keys = self_key.shape[1]
    rows = self_query.shape[0]
    heads = position_bias.shape[1]
    buckets = position_bias.shape[0]
    hidden = ffn_gate.shape[1]
    place = lax.axis_index("mem")
    me = place * nd + lax.axis_index("dp")

    half = hidden // 2
    first = (half // LANES + 1) // 2 * LANES
    last = half - first
    core = (me & 1).reshape(1)
    both = shape((rows, 2 * width + 2 * keys), BF16)
    shard_s, shard_c, shard_a, shard_b, far = call(
        functools.partial(pack, first),
        [both, both, shape((rows, 3 * first), BF16), shape((rows, 3 * last), BF16), shape((rows, 3 * half), BF16)],
        (core, self_query, self_key, self_value, self_out, cross_query, cross_key, cross_value, cross_out, ffn_gate, ffn_up, ffn_down),
        [SCALARS] + [None] * 11,
        room=58,
    )
    run = Order(jnp.full((8, 128), me, F32))
    gs = Gather(shard_s, n, run)
    gc = Gather(shard_c, n, run)
    gs.go()
    far = run.wait(lax.ppermute(run.tie(far), AXES, sibling(n)))
    ga = Gather(jnp.stack([shard_a, far[:, : 3 * first]]), n, run, False)
    gb = Gather(jnp.stack([shard_b, far[:, 3 * first :]]), n, run, False)

    src = source(n, me)
    feature = (src[:, None] * rows + lax.iota(jnp.int32, rows)[None, :]).reshape(1, width)
    places = place ^ lax.iota(jnp.int32, nm)
    stream = (length, width)
    turned = (width, length)
    gains = jnp.concatenate([jnp.stack([self_gain, cross_gain, ffn_gain]), jnp.zeros((5, width), F32)])
    x, dy, self_normed, self_normed_t, gains, order = call(
        arrange,
        [
            shape(stream, BF16),
            shape(stream, BF16),
            shape(stream, BF16),
            shape(turned, BF16),
            shape((8, width), F32),
            shape((width, width), BF16),
        ],
        (places, block_input.reshape(stream), out_grad.reshape(stream), feature, gains),
        [SCALARS, None, None, None, None],
    )
    part = span // nm
    local, local_t = call(
        arrange_memory,
        [shape((span, width), BF16), shape((width, span), BF16)],
        (places, memory.reshape(nm, part, width), order),
        [SCALARS, None, None],
    )
    seg_col = decoder_segments.reshape(length, 1)
    seg_row = decoder_segments.reshape(1, length)
    key_seg = encoder_segments.reshape(nm, part)
    key_seg = jnp.concatenate(
        [lax.dynamic_index_in_dim(key_seg, place ^ t, 0, keepdims=True) for t in range(nm)], axis=1
    )
    bucket_line = jnp.roll(distance_buckets[::-1], 1).reshape(1, length)

    kv = keys
    groups = kv // DH
    two = (2 * length, width)
    work = 2 * 2 * length * width * 9
    narrow = part % LANES != 0
    v = types.SimpleNamespace()

    def prepare():
        v.normed = run.wait(self_normed)
        v.dy_far = lax.ppermute(dy, AXES, sibling(n))

    def prepare_grad():
        v.dy_far = run.wait(v.dy_far)
        v.dy_two, v.dyt_two = call(
            pair_up, [shape(two, BF16), shape((width, 2 * length), BF16)], (dy, v.dy_far)
        )
        v.dyt_two = run.wait(v.dyt_two)

    def prepare_memory():
        v.local = run.wait(local)

    def self_part():
        v.q, v.kt, v.vt, v.p, v.mixed, v.middle, normed = call(
            self_forward,
            [
                shape(stream, BF16),
                shape((kv, length), BF16),
                shape((kv, length), BF16),
                shape((groups, length, 2 * length), BF16),
                shape(stream, BF16),
                shape(stream, F32),
                shape(stream, BF16),
            ],
            (x, run.tie(v.normed), position_bias.T, bucket_line, seg_col, seg_row, gains, *gs.pieces),
            flops=2 * length * width * 3 * width,
        )
        v.cross_normed = run.wait(normed)

    def memory_part():
        v.pair_spec = [columns(w, 2 * kv, 2 * width // (2 * kv)) for w in gc.pieces]
        (pair_t,) = call(
            memory_forward,
            [shape((2 * kv, span), BF16)],
            (run.tie(v.local), *gc.pieces),
            [None] + v.pair_spec,
            flops=2 * span * width * 2 * kv,
        )
        pair_t = run.wait(pair_t)
        v.blocks = swap_rows([pair_t[:, t * part : (t + 1) * part] for t in range(nm)], nm, nd)

    def memory_there():
        v.pair_t = jnp.concatenate([run.wait(block) for block in v.blocks], axis=1)

    def cross_part():
        v.cross_q, v.cross_p, v.cross_mixed, v.second, normed = call(
            cross_forward,
            [
                shape(stream, BF16),
                shape((groups, length, 2 * span), BF16),
                shape(stream, BF16),
                shape(stream, F32),
                shape(stream, BF16),
            ],
            (v.middle, run.tie(v.cross_normed), v.pair_t, seg_col, key_seg, gains, *gc.pieces),
            [None] * 6 + [columns(w, 2 * width, 0) for w in gc.pieces],
            flops=2 * length * width * 2 * width,
        )
        v.ffn_normed = run.wait(normed)
        v.normed_far = lax.ppermute(v.ffn_normed, AXES, sibling(n))

    def ffn_part():
        outs = [shape(two, BF16), shape((width, 2 * length), BF16), shape(two, F32), shape(two, F32)]
        v.n_two, v.nt_two, res, v.dn, *pieces = call(
            ffn_first,
            outs + [shape(w.shape, BF16) for w in ga.pieces],
            (v.ffn_normed, run.wait(v.normed_far), v.dy_two, v.dyt_two, *ga.pieces),
            flops=work * first,
        )
        v.ra = Scatter(pieces, n, run)
        v.res = run.wait(res)

    def ffn_rest():
        outs = [shape(stream, F32), shape(stream, F32), shape((length, 2 * width), BF16)]
        v.res, v.dn, far, *pieces = call(
            ffn_second,
            outs + [shape(w.shape, BF16) for w in gb.pieces],
            (v.n_two, v.nt_two, v.dy_two, v.dyt_two, run.tie(v.res), v.dn, *gb.pieces),
            flops=work * last,
        )
        v.rb = Scatter(pieces, n, run)
        v.far = lax.ppermute(run.wait(far), AXES, sibling(n))

    def ffn_back():
        v.result, v.grad, v.ffn_gain_grad, v.branch, v.mixed_grad = call(
            ffn_end,
            [
                shape(stream, BF16),
                shape(stream, F32),
                shape((1, width), F32),
                shape(stream, BF16),
                shape(stream, BF16),
            ],
            (v.second, v.res, v.dn, run.wait(v.far), dy, gains, *gc.pieces),
            [None] * 6 + [columns(w, width, 1) for w in gc.pieces],
            flops=2 * length * width * width,
        )

    def cross_back_part():
        outs = [shape((2 * kv, part), BF16)] * nm
        if narrow:
            outs = [shape((2 * kv, span), BF16)]
        q_grad, *blocks = call(
            cross_back,
            [shape(stream, BF16)] + outs,
            (v.cross_q, v.pair_t, v.cross_p, run.tie(v.mixed_grad)),
            flops=2 * length * span * width * 8,
        )
        v.cross_q_grad = run.wait(q_grad)
        if narrow:
            blocks = [blocks[0][:, t * part : (t + 1) * part] for t in range(nm)]
        v.parts = blocks

    def memory_back():
        v.sent = swap_rows([v.parts[0]] + [run.tie(b) for b in v.parts[1:]], nm, nd)

    def memory_back_there():
        v.there = [run.wait(block) for block in v.sent]

    def cross_mid_part():
        v.grad, v.cross_gain_grad, v.low, v.mixed_grad = call(
            cross_mid,
            [shape(stream, F32), shape((1, width), F32), shape(stream, BF16), shape(stream, BF16)],
            (run.tie(v.cross_q_grad), v.middle, v.grad, gains, *gc.pieces, *gs.pieces),
            [None] * 4 + [columns(w, width, 0) for w in gc.pieces] + [columns(w, width, 2) for w in gs.pieces],
            flops=2 * length * width * width * 2,
        )
        v.mixed_grad = run.wait(v.mixed_grad)

    def cross_grads_part():
        pieces = call(
            cross_grads,
            [shape((width // 4, 3 * width), BF16)] * 2 + [shape((2, width // 4, 3 * width), BF16)],
            (v.cross_normed, run.tie(v.cross_q_grad), v.branch, v.cross_mixed, v.low, v.mixed),
            flops=2 * length * width * width * 3,
        )
        run.wait(pieces[0])
        v.rc = Scatter(pieces, n, run)
        v.rc.go()

    def self_back_part():
        v.grads, table = call(
            self_back,
            [shape((length, width + 2 * kv), BF16), shape((heads, buckets), F32)],
            (v.q, v.kt, v.vt, v.p, run.tie(v.mixed_grad), bucket_line),
            flops=2 * length * length * width * 8,
            scratch=[pltpu.VMEM((heads, length), F32)],
        )
        v.table = run.wait(table)

    def self_grads_part():
        pieces = call(
            self_grads,
            [shape((width // 4, width + 4 * kv), BF16)] * 2 + [shape((2, width // 4, width + 4 * kv), BF16)],
            (self_normed_t, run.tie(v.grads), local_t, *v.there),
            flops=2 * (length + span // 2) * width * 2 * width,
        )
        run.wait(pieces[0])
        v.rs = Scatter(pieces, n, run)
        v.rs.go()

    def self_end_part():
        v.input_grad, packed = call(
            self_end,
            [shape(stream, F32), shape((3 * width // 128 + heads, 128), F32)],
            (x, v.grad, run.tie(v.grads), gains, order, v.cross_gain_grad, v.ffn_gain_grad, v.table, *gs.pieces),
            [None] * 8 + [columns(w, width + 2 * kv, 0) for w in gs.pieces],
            flops=2 * length * width * 4 * width,
        )
        v.total = Total(run.wait(packed), n, run)
        v.total.send()

    def memory_end_part():
        memory_grad, v.result = call(
            memory_end,
            [shape((nm, part, width), F32), shape(stream, BF16)],
            (places, run.tie(order), v.result, *gc.pieces, *v.there),
            [SCALARS] + [None] * 2 + v.pair_spec + [None] * nm,
            flops=2 * span * width * 3 * width,
        )
        v.memory_grad = run.wait(memory_grad)

    def columns_back():
        v.far = jnp.concatenate([v.ra.done()[1], v.rb.done()[1]], axis=1)
        v.far = lax.ppermute(v.far, AXES, sibling(n))

    actions = {
        "p": lambda: run.pace(20),
        "q": lambda: run.pace(7),
        "s": gs.go,
        "c": gc.go,
        "a": ga.go,
        "b": gb.go,
        "x1": prepare,
        "x2": prepare_grad,
        "x3": prepare_memory,
        "K1": self_part,
        "K2": memory_part,
        "w2": memory_there,
        "K3": cross_part,
        "K4": ffn_part,
        "K5": ffn_rest,
        "K6": ffn_back,
        "K7": cross_back_part,
        "m7": memory_back,
        "w7": memory_back_there,
        "K8": cross_mid_part,
        "K9": self_back_part,
        "K10": self_grads_part,
        "K11": cross_grads_part,
        "K12": self_end_part,
        "K13": memory_end_part,
        "A": lambda: v.ra.go(),
        "B": lambda: v.rb.go(),
        "C": lambda: v.rc.go(),
        "S": lambda: v.rs.go(),
        "t": lambda: v.total.go(),
        "u": columns_back,
    }
    for name in PLAN:
        actions[name]()

    memory_grad, result, input_grad = v.memory_grad, v.result, v.input_grad
    done_a, done_b, done_c = (group.done() for group in (v.ra, v.rb, v.rc))
    (done_s,) = call(
        finish,
        [shape(v.rs.held.shape, F32)],
        (v.rs.held, v.rs.came, run.token),
        [None, None, pl.BlockSpec(memory_space=pl.ANY)],
    )
    whole = shape((rows, hidden), F32)
    gate_done, up_done, down_done = call(
        functools.partial(unpack, first),
        [whole, whole, whole],
        (core, done_a[0], done_b[0], v.far),
        [SCALARS] + [None] * 3,
    )

    gain_lines = 3 * width // 128
    packed = v.total.value
    gain_grads = packed[:gain_lines].reshape(3, width)
    table = packed[gain_lines:, :buckets].T

    return (
        result.reshape(block_input.shape),
        input_grad.reshape(block_input.shape),
        memory_grad.reshape(memory.shape),
        gain_grads[0],
        gain_grads[1],
        gain_grads[2],
        table,
        done_s[:, :width],
        done_s[:, width : width + kv],
        done_s[:, width + kv : width + 2 * kv],
        done_c[:, 2 * width :],
        done_c[:, :width],
        done_s[:, width + 2 * kv : width + 3 * kv],
        done_s[:, width + 3 * kv :],
        done_c[:, width : 2 * width],
        gate_done,
        up_done,
        down_done,
    )


def solution(mesh):
    stream = P("dp", "mem", None, None)
    segments = P("dp", "mem", None)
    shard = P(AXES, None)
    in_specs = (stream, P("dp", None, "mem", None), stream, segments, segments) + (P(),) * 5 + (shard,) * 11
    out_specs = (stream, stream, P("dp", None, "mem", None)) + (P(),) * 4 + (shard,) * 11
    body = functools.partial(shards, mesh.shape["mem"], mesh.shape["dp"])
    return jax.shard_map(body, mesh=mesh, in_specs=in_specs, out_specs=out_specs, check_vma=False)
```
